32 devices in a mesh: ctx: 8 (over z, core), wt: 4 (over y, x).
Axes of the slice: x: 2, y: 2, z: 4, core: 2. Of those that a mesh axis runs over, the one named last changes fastest.
Arguments:
- inputs: bfloat16 [4, 2, 512, 2048], P('wt', None, 'ctx'), may hold values from -6 to 6
- boundaries: int32 [4, 9], P('wt'), may hold values from 0 to 1024, as said below
- first_gain: bfloat16 [2048], P('wt'), may hold values from 0.5 to 1.5
- query_down: bfloat16 [2048, 1024], P('wt'), may hold values from -0.125 to 0.125
- query_gain: bfloat16 [1024], P('wt'), may hold values from 0.5 to 1.5
- query_up: bfloat16 [1024, 4096], P('wt'), may hold values from -0.1875 to 0.1875
- key_weights: bfloat16 [2048, 256], P('wt'), may hold values from -0.125 to 0.125
- value_weights: bfloat16 [2048, 256], P('wt'), may hold values from -0.125 to 0.125
- output_weights: bfloat16 [4096, 2048], P('wt'), may hold values from -0.375 to 0.375
- second_gain: bfloat16 [2048], P('wt'), may hold values from 0.5 to 1.5
- gate_weights: bfloat16 [2048, 5632], P('wt'), may hold values from -0.125 to 0.125
- up_weights: bfloat16 [2048, 5632], P('wt'), may hold values from -0.125 to 0.125
- down_weights: bfloat16 [5632, 2048], P('wt'), may hold values from -0.078125 to 0.078125
- cotangent: bfloat16 [4, 2, 512, 2048], P('wt', None, 'ctx'), may hold values from -6 to 6
Outputs:
- layer_output: bfloat16 [4, 2, 512, 2048], P('wt', None, 'ctx')
- input_gradient: bfloat16 [4, 2, 512, 2048], P('wt', None, 'ctx')
- first_gain_gradient: float32 [2048], P('wt')
- query_down_gradient: float32 [2048, 1024], P('wt')
- query_gain_gradient: float32 [1024], P('wt')
- query_up_gradient: float32 [1024, 4096], P('wt')
- key_weights_gradient: float32 [2048, 256], P('wt')
- value_weights_gradient: float32 [2048, 256], P('wt')
- output_weights_gradient: float32 [4096, 2048], P('wt')
- second_gain_gradient: float32 [2048], P('wt')
- gate_weights_gradient: float32 [2048, 5632], P('wt')
- up_weights_gradient: float32 [2048, 5632], P('wt')
- down_weights_gradient: float32 [5632, 2048], P('wt')
The draws below stay inside these ranges and needn't reach their ends.
Inputs may be any that keep to these rules, and one draw needn't show every extreme that they name: `boundaries`: each row is nondecreasing and begins with 0; consecutive entries below 1024 differ by 128 to 512, and one of the first two documents of each stream has exactly 512 tokens; entries equal to 1024 are unused slots, and the last document ends at 1024, so no document is longer than 512.
All inputs are finite; a program needn't handle non-finite values.
Results may differ from the reference program's by a relative error of at most 0.024.
Values may be sent and summed in bfloat16 or wider, within the bound.
A program may use at most 576 MiB of HBM per device.

```python
import math
import jax
import jax.numpy as jnp
from jax import lax

D = 2048
R = 1024
HEADS = 16
HEAD_DIM = 256
FF = 5632
TOK_DEV = 128
DOC_MAX = 512
SEQ = 1024
HALF = 512
STREAMS = 4
HD = 4096
NDOC = 9
N_CTX = 8


def draw_boundaries(key, part):
    lengths = jax.random.randint(key, (STREAMS, NDOC), DOC_MAX // 4, DOC_MAX + 1)
    chosen = jax.random.randint(jax.random.fold_in(key, 7), (STREAMS,), 0, 2)
    slots = jnp.arange(NDOC, dtype=jnp.int32)
    lengths = jnp.where(slots[None, :] == chosen[:, None], DOC_MAX, lengths)
    ending = jnp.cumsum(lengths, axis=1)
    starts = ending - lengths
    return jnp.minimum(starts, SEQ).astype(jnp.int32)


def shard_levels(stream_key, extent, split, low, largest):
    def one(dim, parts):
        draws = jax.random.uniform(jax.random.fold_in(jax.random.fold_in(stream_key, 6), dim), (parts,), jnp.float32, low / len(split), largest / len(split))
        return jnp.repeat(jnp.exp(draws), extent[dim] // parts).reshape((-1,) + (1,) * (len(extent) - dim - 1))

    loudness = one(*split[0])
    for cut in split[1:]:
        loudness = loudness * one(*cut)
    return loudness


def bell_draw(own_key, shape, spread, reach, split=(), kind=jnp.bfloat16):
    array = jax.random.normal(own_key, shape, jnp.float32) * spread
    if len(split) > 0:
        array = shard_levels(own_key, shape, split, -0.22, 0.18) * array
    return jnp.clip(array, min=-reach, max=reach).astype(kind)


def setup_inputs(seed: int = 0) -> dict:
    arg_keys = jax.random.split(jax.random.key(seed), 15)
    return {
        "inputs": bell_draw(arg_keys[0], (STREAMS, 2, HALF, D), 1.0, 6.0, ((0, 4), (2, 8))),
        "boundaries": draw_boundaries(jax.random.fold_in(arg_keys[14], 71), 0),
        "first_gain": jnp.clip(1.0 + 0.1 * jax.random.normal(arg_keys[2], (D,), jnp.float32), 0.5, 1.5).astype(jnp.bfloat16),
        "query_down": bell_draw(arg_keys[3], (D, R), D ** -0.5, 0.125, ((0, 4),)),
        "query_gain": jnp.clip(1.0 + 0.1 * jax.random.normal(arg_keys[4], (R,), jnp.float32), 0.5, 1.5).astype(jnp.bfloat16),
        "query_up": bell_draw(arg_keys[5], (R, HD), R ** -0.5, 0.1875, ((0, 4),)),
        "key_weights": bell_draw(arg_keys[6], (D, HEAD_DIM), D ** -0.5, 0.125, ((0, 4),)),
        "value_weights": bell_draw(arg_keys[7], (D, HEAD_DIM), D ** -0.5, 0.125, ((0, 4),)),
        "output_weights": bell_draw(arg_keys[8], (HD, D), (HD // 16) ** -0.5, 0.375, ((0, 4),)),
        "second_gain": jnp.clip(1.0 + 0.1 * jax.random.normal(arg_keys[9], (D,), jnp.float32), 0.5, 1.5).astype(jnp.bfloat16),
        "gate_weights": bell_draw(arg_keys[10], (D, FF), D ** -0.5, 0.125, ((0, 4),)),
        "up_weights": bell_draw(arg_keys[11], (D, FF), D ** -0.5, 0.125, ((0, 4),)),
        "down_weights": bell_draw(arg_keys[12], (FF, D), FF ** -0.5, 0.078125, ((0, 4),)),
        "cotangent": bell_draw(arg_keys[13], (STREAMS, 2, HALF, D), 1.0, 6.0, ((0, 4), (2, 8))),
    }


@jax.custom_vjp
def low(v):
    return lax.optimization_barrier(v.astype(jnp.bfloat16)).astype(jnp.float32)

@jax.custom_vjp
def low_back(v):
    return v

def low_keep(v):
    return (low(v), None)

def low_pass(kept, grad):
    return (grad,)

def back_keep(v):
    return (v, None)

def back_low(kept, grad):
    return (low(grad),)
low.defvjp(low_keep, low_pass)
low_back.defvjp(back_keep, back_low)
epsilon = 1e-06
negative = -1e+30
highest = lax.Precision.HIGHEST

def matmul(left, right):
    return jnp.dot(left, right, precision=highest, preferred_element_type=jnp.float32)

def normed(values, scales):
    return values * lax.rsqrt(lax.optimization_barrier(jnp.mean(values * values, axis=-1, keepdims=True)) + epsilon) * scales

def rotate(values, cosine, sine):
    middle = values.shape[-1] // 2
    leading = values[..., :middle]
    trailing = values[..., middle:]
    return jnp.concatenate([leading * cosine - trailing * sine, trailing * cosine + leading * sine], axis=-1)

def tables(positions, width):
    exponent = jnp.arange(width // 2, dtype=jnp.float32) * (-2.0 / width)
    angles = positions.astype(jnp.float32)[:, None] * (10000.0 ** exponent)[None, :]
    return (jnp.cos(angles), jnp.sin(angles))

def layer(stream, weights, starts):
    first_gain, query_down, query_gain, query_up, key_weights, value_weights, output_weights, second_gain, gate_weights, up_weights, down_weights = weights
    positions = jnp.arange(SEQ, dtype=jnp.int32)
    begins = lax.optimization_barrier(jnp.max(jnp.where(starts[None, :] <= positions[:, None], starts[None, :], 0), axis=1))
    cosine, sine = tables(positions, HEAD_DIM)
    h_first = low(normed(stream, first_gain))
    latent = low_back(matmul(h_first, query_down))
    q_latent = low(normed(latent, query_gain))
    q_raw = low_back(matmul(q_latent, query_up)).reshape(SEQ, HEADS, HEAD_DIM)
    queries = low(rotate(q_raw, cosine[:, None, :], sine[:, None, :]) / math.sqrt(HEAD_DIM))
    keys = low(rotate(low_back(matmul(h_first, key_weights)), cosine, sine))
    values = low(low_back(matmul(h_first, value_weights)))
    block = math.gcd(SEQ, 512)
    count = SEQ // block

    def one_block(items):
        query_rows, query_pos, query_begin = items
        scores = low_back(jnp.einsum('thd,kd->thk', query_rows, keys, precision=highest))
        visible = (positions[None, :] >= query_begin[:, None]) & (positions[None, :] <= query_pos[:, None])
        scores = jnp.where(visible[:, None, :], scores, negative)
        probs = low(jax.nn.softmax(scores, axis=-1))
        return jnp.einsum('thk,kd->thd', probs, values, precision=highest)
    attended = lax.map(jax.checkpoint(one_block), (queries.reshape(count, block, HEADS, HEAD_DIM), positions.reshape(count, block), begins.reshape(count, block)))
    attn_out = low(low_back(attended.reshape(SEQ, HEADS * HEAD_DIM)))
    resid = stream + low_back(matmul(attn_out, output_weights))
    h_second = low(normed(resid, second_gain))
    gate = low_back(matmul(h_second, gate_weights))
    upper = low_back(matmul(h_second, up_weights))
    hidden = low(jax.nn.silu(gate) * upper)
    return resid + low_back(matmul(hidden, down_weights))

def to_line(halves):
    leading = halves[0]
    trailing = halves[1].reshape(N_CTX, TOK_DEV // 2, D)[::-1].reshape(HALF, D)
    return jnp.concatenate([leading, trailing], axis=0)

def from_line(line):
    leading = line[:HALF]
    trailing = line[HALF:].reshape(N_CTX, TOK_DEV // 2, D)[::-1].reshape(HALF, D)
    return jnp.stack([leading, trailing], axis=0)

def reference(inputs, boundaries, first_gain, query_down, query_gain, query_up, key_weights, value_weights, output_weights, second_gain, gate_weights, up_weights, down_weights, cotangent):
    weights = tuple((w.astype(jnp.float32) for w in (first_gain, query_down, query_gain, query_up, key_weights, value_weights, output_weights, second_gain, gate_weights, up_weights, down_weights)))

    def per_stream(totals, items):
        halves, starts, slopes = items

        def forward(stream, params):
            return layer(stream, params, starts)
        result, backward = jax.vjp(forward, to_line(halves.astype(jnp.float32)), weights)
        d_stream, d_weights = backward(to_line(slopes.astype(jnp.float32)))
        totals = tuple((a + b for a, b in zip(totals, d_weights)))
        return (totals, (from_line(result).astype(jnp.bfloat16), from_line(d_stream).astype(jnp.bfloat16)))
    zeros = tuple((jnp.zeros_like(w) for w in weights))
    grads, (outputs, slopes_in) = lax.scan(per_stream, zeros, (inputs, boundaries, cotangent))
    return (outputs, slopes_in, grads[0], grads[1], grads[2], grads[3], grads[4], grads[5], grads[6], grads[7], grads[8], grads[9], grads[10])
```

```python
import functools
import math

import jax
import jax.numpy as jnp
from jax import lax
from jax.experimental import pallas as pl
from jax.experimental.pallas import tpu as pltpu
from jax.sharding import PartitionSpec as P

EPS = 1e-06
NEG = -1e30
F32 = jnp.float32
BF = jnp.bfloat16
VMEM = pl.BlockSpec(memory_space=pltpu.VMEM)
SMEM = pl.BlockSpec(memory_space=pltpu.SMEM)
MIB = 1 << 20


def dot(a, b):
    return jnp.dot(a, b, preferred_element_type=F32)


def dot_nt(a, b):
    return lax.dot_general(a, b, (((1,), (1,)), ((), ())), preferred_element_type=F32)


def dot_tn(a, b):
    return lax.dot_general(a, b, (((0,), (0,)), ((), ())), preferred_element_type=F32)


def inv_rms(v):
    return lax.rsqrt(jnp.mean(v * v, axis=-1, keepdims=True) + EPS)


def rotate(v, cosine, sine):
    middle = v.shape[-1] // 2
    a, b = v[..., :middle], v[..., middle:]
    return jnp.concatenate([a * cosine - b * sine, b * cosine + a * sine], axis=-1)


def tables(positions, width):
    exponent = jnp.arange(width // 2, dtype=F32) * (-2.0 / width)
    angles = positions.astype(F32)[:, None] * (10000.0**exponent)[None, :]
    return jnp.cos(angles), jnp.sin(angles)


def to_stream(rows, groups):
    tail = rows.shape[1:]
    shaped = rows.reshape((groups, 2, rows.shape[0] // (2 * groups)) + tail)
    leading = shaped[:, 0].reshape((-1,) + tail)
    trailing = shaped[::-1, 1].reshape((-1,) + tail)
    return jnp.concatenate([leading, trailing], axis=0)


def from_stream(rows, groups):
    middle = rows.shape[0] // 2
    tail = rows.shape[1:]
    leading = rows[:middle].reshape((groups, middle // groups) + tail)
    trailing = rows[middle:].reshape((groups, middle // groups) + tail)[::-1]
    return jnp.stack([leading, trailing], axis=1).reshape(rows.shape)


def visible_keys(place_ref, bounds_ref, stream, tokens, seqlen):
    half = tokens // 2
    row = lax.broadcasted_iota(jnp.int32, (tokens, 1), 0)
    pos = row + jnp.where(row < half, place_ref[0], place_ref[1] - half)
    begin = jnp.zeros((tokens, 1), jnp.int32)
    for j in range(bounds_ref.shape[1]):
        start = bounds_ref[stream, j]
        begin = jnp.where(pos >= start, jnp.maximum(begin, start), begin)
    key = lax.broadcasted_iota(jnp.int32, (tokens, seqlen), 1)
    return (key >= begin) & (key <= pos)


def probabilities(q, keys, visible):
    scores = jnp.where(visible, dot_nt(q, keys), NEG)
    peak = jnp.max(scores, axis=-1, keepdims=True)
    weight = jnp.where(visible, jnp.exp(scores - peak), 0.0)
    return weight * (1.0 / jnp.sum(weight, axis=-1, keepdims=True))


def attend_kernel(depth, place_ref, bounds_ref, q_ref, kv_ref, cos_ref, sin_ref, queries_ref, out_ref):
    tokens, seqlen = q_ref.shape[0], kv_ref.shape[1]
    visible = visible_keys(place_ref, bounds_ref, pl.program_id(0), tokens, seqlen)
    keys, values = kv_ref[0, :, :depth], kv_ref[0, :, depth:]
    scale = 1.0 / math.sqrt(depth)
    for h in range(q_ref.shape[1] // depth):
        cut = slice(h * depth, (h + 1) * depth)
        q = (rotate(q_ref[:, cut], cos_ref[...], sin_ref[...]) * scale).astype(BF)
        queries_ref[:, cut] = q
        probs = probabilities(q, keys, visible).astype(BF)
        out_ref[:, cut] = dot(probs, values).astype(BF)


def attend_back_kernel(depth, place_ref, bounds_ref, q_ref, kv_ref, cos_ref, sin_ref, slope_ref, dq_ref, dkv_ref):
    tokens, seqlen = q_ref.shape[0], kv_ref.shape[1]
    visible = visible_keys(place_ref, bounds_ref, pl.program_id(0), tokens, seqlen)
    keys, values = kv_ref[0, :, :depth], kv_ref[0, :, depth:]
    scale = 1.0 / math.sqrt(depth)
    dk = jnp.zeros((seqlen, depth), F32)
    dv = jnp.zeros((seqlen, depth), F32)
    for h in range(q_ref.shape[1] // depth):
        cut = slice(h * depth, (h + 1) * depth)
        q, slope = q_ref[:, cut], slope_ref[:, cut]
        probs = probabilities(q, keys, visible)
        dprobs = dot_nt(slope, values)
        delta = jnp.sum(probs * dprobs, axis=-1, keepdims=True)
        dscores = (probs * (dprobs - delta)).astype(BF)
        dq_ref[:, cut] = (rotate(dot(dscores, keys), cos_ref[...], -sin_ref[...]) * scale).astype(BF)
        dk += dot_tn(dscores, q)
        dv += dot_tn(probs.astype(BF), slope)
    dkv_ref[0, :, :depth] = dk.astype(BF)
    dkv_ref[0, :, depth:] = dv.astype(BF)


def attention_specs(tokens, features, seqlen, depth):
    rows = pl.BlockSpec((tokens, features), lambda s: (s, 0))
    table = pl.BlockSpec((tokens, depth // 2), lambda s: (0, 0))
    kv = pl.BlockSpec((1, seqlen, 2 * depth), lambda s: (s, 0, 0))
    return rows, table, kv


def attend(place, bounds, q_raw, kv, cosine, sine):
    streams, seqlen, depth = kv.shape[0], kv.shape[1], kv.shape[2] // 2
    tokens, features = q_raw.shape[0] // streams, q_raw.shape[1]
    rows, table, kvs = attention_specs(tokens, features, seqlen, depth)
    return pl.pallas_call(
        functools.partial(attend_kernel, depth),
        grid=(streams,),
        out_shape=[jax.ShapeDtypeStruct(q_raw.shape, BF)] * 2,
        in_specs=[SMEM, SMEM, rows, kvs, table, table],
        out_specs=[rows, rows],
        compiler_params=pltpu.CompilerParams(vmem_limit_bytes=40 * MIB),
    )(place, bounds, q_raw, kv, cosine, sine)


def attend_back(place, bounds, queries, kv, cosine, sine, slope):
    streams, seqlen, depth = kv.shape[0], kv.shape[1], kv.shape[2] // 2
    tokens, features = queries.shape[0] // streams, queries.shape[1]
    rows, table, kvs = attention_specs(tokens, features, seqlen, depth)
    return pl.pallas_call(
        functools.partial(attend_back_kernel, depth),
        grid=(streams,),
        out_shape=[jax.ShapeDtypeStruct(queries.shape, BF), jax.ShapeDtypeStruct(kv.shape, BF)],
        in_specs=[SMEM, SMEM, rows, kvs, table, table, rows],
        out_specs=[rows, kvs],
        compiler_params=pltpu.CompilerParams(vmem_limit_bytes=40 * MIB),
    )(place, bounds, queries, kv, cosine, sine, slope)


def gather(v, axis):
    return lax.all_gather(v, axis, axis=0, tiled=True)


def scatter_sum(v, axis):
    return lax.psum_scatter(v.astype(BF), axis, scatter_dimension=0, tiled=True).astype(F32)


def to_columns(weight):
    n_w, n_c, c = lax.axis_size("wt"), lax.axis_size("ctx"), lax.axis_index("ctx")
    rows, cols = weight.shape
    part = lax.dynamic_slice_in_dim(weight, c * (rows // n_c), rows // n_c, 0)
    part = lax.all_to_all(part.reshape(rows // n_c, n_w, cols // n_w), "wt", 1, 0)
    whole = lax.all_gather(part, "ctx", axis=1)
    return whole.reshape(n_w * rows, cols // n_w)


def columns_gradient(terms):
    n_w, n_c = lax.axis_size("wt"), lax.axis_size("ctx")
    rows, cols = terms.shape[0] // n_w, terms.shape[1]
    shaped = terms.astype(BF).reshape(n_w, n_c, rows // n_c, cols).swapaxes(0, 1)
    mine = lax.psum_scatter(shaped, "ctx", scatter_dimension=0)
    mine = lax.all_to_all(mine, "wt", 0, 1)
    whole = lax.all_gather(mine, "ctx", axis=0)
    return whole.reshape(rows, n_w * cols).astype(F32)


def rows_gradient(terms):
    return lax.psum(terms.astype(BF), "ctx").astype(F32)


def on_device(
    inputs,
    boundaries,
    first_gain,
    query_down,
    query_gain,
    query_up,
    key_weights,
    value_weights,
    output_weights,
    second_gain,
    gate_weights,
    up_weights,
    down_weights,
    cotangent,
):
    n_w, n_c, c = lax.axis_size("wt"), lax.axis_size("ctx"), lax.axis_index("ctx")
    width, halfrows = inputs.shape[-1], inputs.shape[2]
    tokens = 2 * halfrows
    seqlen = tokens * n_c
    depth, rank = key_weights.shape[1], query_down.shape[1]
    place = jnp.stack([c * halfrows, seqlen - (c + 1) * halfrows]).astype(jnp.int32)
    offsets = jnp.arange(halfrows, dtype=jnp.int32)
    cosine, sine = tables(jnp.concatenate([place[0] + offsets, place[1] + offsets]), depth)
    bounds = gather(boundaries, "wt")
    gain_query = gather(query_gain, "wt").astype(F32)
    gain_two = gather(second_gain, "wt").astype(F32)

    x = inputs.reshape(tokens, width)
    cot = cotangent.reshape(tokens, width)
    activ = x.astype(F32)
    r_first = inv_rms(activ)
    x_cols = lax.all_to_all(x, "wt", 1, 0, tiled=True)
    n_cols = x_cols.astype(F32) * gather(r_first, "wt")
    h_cols = (n_cols * first_gain.astype(F32)).astype(BF)
    first_weights = jnp.concatenate([query_down, key_weights, value_weights], axis=1)
    low = scatter_sum(dot(h_cols, first_weights), "wt")
    latent = low[:, :rank]
    r_query = inv_rms(latent)
    n_query = latent * r_query
    q_latent = (n_query * gain_query).astype(BF)
    keys = rotate(low[:, rank : rank + depth], cosine, sine).astype(BF)
    kv = jnp.concatenate([keys, low[:, rank + depth :].astype(BF)], axis=1)
    kv = gather(to_stream(gather(kv, "ctx"), n_c)[None], "wt")
    q_latent = gather(q_latent, "wt")
    up_cols = to_columns(query_up)
    gate_cols = to_columns(gate_weights)
    upper_cols = to_columns(up_weights)
    queries, attn_out = attend(place, bounds, dot(q_latent, up_cols), kv, cosine, sine)

    resid = activ + scatter_sum(dot(attn_out, output_weights), "wt")
    r_second = inv_rms(resid)
    n_second = resid * r_second
    h_second = gather((n_second * gain_two).astype(BF), "wt")
    cot_all = gather(cot, "wt")
    gate = dot(h_second, gate_cols)
    upper = dot(h_second, upper_cols)
    sigma = jax.nn.sigmoid(gate)
    silu = gate * sigma
    hidden = (silu * upper).astype(BF)
    layer_output = (resid + scatter_sum(dot(hidden, down_weights), "wt")).astype(BF)

    d_down = dot_tn(hidden, cot_all)
    d_hidden = dot_nt(cot_all, down_weights)
    d_gate = (d_hidden * upper * sigma * (1.0 + gate * (1.0 - sigma))).astype(BF)
    d_upper = (d_hidden * silu).astype(BF)
    d_h_second = scatter_sum(dot_nt(d_gate, gate_cols) + dot_nt(d_upper, upper_cols), "wt")
    d_gate_weights = dot_tn(h_second, d_gate)
    d_up_weights = dot_tn(h_second, d_upper)
    d_n = d_h_second * gain_two
    d_gain_two = jnp.sum(d_h_second * n_second, axis=0)
    d_resid = cot.astype(F32) + r_second * (
        d_n - n_second * jnp.mean(d_n * n_second, axis=-1, keepdims=True)
    )
    d_proj = gather(d_resid.astype(BF), "wt")
    d_output = dot_tn(attn_out, d_proj)
    d_attended = dot_nt(d_proj, output_weights).astype(BF)
    d_q_raw, d_kv = attend_back(place, bounds, queries, kv, cosine, sine, d_attended)
    d_kv = scatter_sum(d_kv, "wt")[0]
    d_kv = scatter_sum(from_stream(d_kv, n_c), "ctx")
    d_k_raw = rotate(d_kv[:, :depth], cosine, -sine).astype(BF)
    d_v_raw = d_kv[:, depth:].astype(BF)
    d_up_cols = dot_tn(q_latent, d_q_raw)
    d_q_latent = scatter_sum(dot_nt(d_q_raw, up_cols), "wt")
    d_n = d_q_latent * gain_query
    d_gain_query = jnp.sum(d_q_latent * n_query, axis=0)
    d_latent = r_query * (d_n - n_query * jnp.mean(d_n * n_query, axis=-1, keepdims=True))
    low_slope = gather(jnp.concatenate([d_latent.astype(BF), d_k_raw, d_v_raw], axis=1), "wt")
    d_first_weights = dot_tn(h_cols, low_slope)
    d_h_cols = dot_nt(low_slope, first_weights)
    d_gain_one = jnp.sum(d_h_cols * n_cols, axis=0)
    d_n = lax.all_to_all(
        (d_h_cols * first_gain.astype(F32)).astype(BF), "wt", 0, 1, tiled=True
    ).astype(F32)
    n_first = activ * r_first
    input_gradient = d_resid + r_first * (
        d_n - n_first * jnp.mean(d_n * n_first, axis=-1, keepdims=True)
    )

    gains = jnp.concatenate([d_gain_two.reshape(n_w, -1), d_gain_query.reshape(n_w, -1)], axis=1)
    gains = lax.psum_scatter(gains, "wt", scatter_dimension=0)
    gains = lax.psum(jnp.concatenate([d_gain_one, gains]), "ctx")
    one = d_gain_one.shape[0]
    d_first_weights = rows_gradient(d_first_weights)
    return (
        layer_output.reshape(inputs.shape),
        input_gradient.astype(BF).reshape(inputs.shape),
        gains[:one],
        d_first_weights[:, :rank],
        gains[one + width // n_w :],
        columns_gradient(d_up_cols),
        d_first_weights[:, rank : rank + depth],
        d_first_weights[:, rank + depth :],
        rows_gradient(d_output),
        gains[one : one + width // n_w],
        columns_gradient(d_gate_weights),
        columns_gradient(d_up_weights),
        rows_gradient(d_down),
    )


def solution(mesh):
    token = P("wt", None, "ctx", None)
    row, vec = P("wt", None), P("wt")
    in_specs = (token, row, vec, row, vec, row, row, row, row, vec, row, row, row, token)
    out_specs = (token, token, vec, row, vec, row, row, row, row, vec, row, row, row)
    return jax.shard_map(
        on_device, mesh=mesh, in_specs=in_specs, out_specs=out_specs, check_vma=False
    )
```

```python
import functools
import math

import jax
import jax.numpy as jnp
from jax import lax
from jax.experimental import pallas as pl
from jax.experimental.pallas import tpu as pltpu
from jax.sharding import PartitionSpec as P

EPS = 1e-06
NEG = -1e30
F32 = jnp.float32
BF = jnp.bfloat16
VMEM = pl.BlockSpec(memory_space=pltpu.VMEM)
SMEM = pl.BlockSpec(memory_space=pltpu.SMEM)
MIB = 1 << 20
MESH = pl.DeviceIdType.MESH


def dot(a, b):
    return jnp.dot(a, b, preferred_element_type=F32)


def dot_nt(a, b):
    return lax.dot_general(a, b, (((1,), (1,)), ((), ())), preferred_element_type=F32)


def dot_tn(a, b):
    return lax.dot_general(a, b, (((0,), (0,)), ((), ())), preferred_element_type=F32)


def inv_rms(v):
    return lax.rsqrt(jnp.mean(v * v, axis=-1, keepdims=True) + EPS)


def rotate(v, cosine, sine):
    middle = v.shape[-1] // 2
    a, b = v[..., :middle], v[..., middle:]
    return jnp.concatenate([a * cosine - b * sine, b * cosine + a * sine], axis=-1)


def tables(positions, width):
    exponent = jnp.arange(width // 2, dtype=F32) * (-2.0 / width)
    angles = positions.astype(F32)[:, None] * (10000.0**exponent)[None, :]
    return jnp.cos(angles), jnp.sin(angles)


def to_stream(rows, groups):
    tail = rows.shape[1:]
    shaped = rows.reshape((groups, 2, rows.shape[0] // (2 * groups)) + tail)
    leading = shaped[:, 0].reshape((-1,) + tail)
    trailing = shaped[::-1, 1].reshape((-1,) + tail)
    return jnp.concatenate([leading, trailing], axis=0)


def from_stream(rows, groups):
    middle = rows.shape[0] // 2
    tail = rows.shape[1:]
    leading = rows[:middle].reshape((groups, middle // groups) + tail)
    trailing = rows[middle:].reshape((groups, middle // groups) + tail)[::-1]
    return jnp.stack([leading, trailing], axis=1).reshape(rows.shape)


def visible_keys(place_ref, bounds_ref, stream, tokens, seqlen):
    half = tokens // 2
    row = lax.broadcasted_iota(jnp.int32, (tokens, 1), 0)
    pos = row + jnp.where(row < half, place_ref[0], place_ref[1] - half)
    begin = jnp.zeros((tokens, 1), jnp.int32)
    for j in range(bounds_ref.shape[1]):
        start = bounds_ref[stream, j]
        begin = jnp.where(pos >= start, jnp.maximum(begin, start), begin)
    key = lax.broadcasted_iota(jnp.int32, (tokens, seqlen), 1)
    return (key >= begin) & (key <= pos)


def probabilities(q, keys, visible):
    scores = jnp.where(visible, dot_nt(q, keys), NEG)
    peak = jnp.max(scores, axis=-1, keepdims=True)
    weight = jnp.where(visible, jnp.exp(scores - peak), 0.0)
    return weight * (1.0 / jnp.sum(weight, axis=-1, keepdims=True))


def attend_kernel(depth, place_ref, bounds_ref, q_ref, kv_ref, cos_ref, sin_ref, queries_ref, out_ref):
    tokens, seqlen = q_ref.shape[0], kv_ref.shape[1]
    visible = visible_keys(place_ref, bounds_ref, pl.program_id(0), tokens, seqlen)
    keys, values = kv_ref[0, :, :depth], kv_ref[0, :, depth:]
    scale = 1.0 / math.sqrt(depth)
    for h in range(q_ref.shape[1] // depth):
        cut = slice(h * depth, (h + 1) * depth)
        q = (rotate(q_ref[:, cut], cos_ref[...], sin_ref[...]) * scale).astype(BF)
        queries_ref[:, cut] = q
        probs = probabilities(q, keys, visible).astype(BF)
        out_ref[:, cut] = dot(probs, values).astype(BF)


def attend_back_kernel(depth, place_ref, bounds_ref, q_ref, kv_ref, cos_ref, sin_ref, slope_ref, dq_ref, dkv_ref):
    tokens, seqlen = q_ref.shape[0], kv_ref.shape[1]
    visible = visible_keys(place_ref, bounds_ref, pl.program_id(0), tokens, seqlen)
    keys, values = kv_ref[0, :, :depth], kv_ref[0, :, depth:]
    scale = 1.0 / math.sqrt(depth)
    dk = jnp.zeros((seqlen, depth), F32)
    dv = jnp.zeros((seqlen, depth), F32)
    for h in range(q_ref.shape[1] // depth):
        cut = slice(h * depth, (h + 1) * depth)
        q, slope = q_ref[:, cut], slope_ref[:, cut]
        probs = probabilities(q, keys, visible)
        dprobs = dot_nt(slope, values)
        delta = jnp.sum(probs * dprobs, axis=-1, keepdims=True)
        dscores = (probs * (dprobs - delta)).astype(BF)
        dq_ref[:, cut] = (rotate(dot(dscores, keys), cos_ref[...], -sin_ref[...]) * scale).astype(BF)
        dk += dot_tn(dscores, q)
        dv += dot_tn(probs.astype(BF), slope)
    dkv_ref[0, :, :depth] = dk.astype(BF)
    dkv_ref[0, :, depth:] = dv.astype(BF)


def attention_specs(tokens, features, seqlen, depth):
    rows = pl.BlockSpec((tokens, features), lambda s: (s, 0))
    table = pl.BlockSpec((tokens, depth // 2), lambda s: (0, 0))
    kv = pl.BlockSpec((1, seqlen, 2 * depth), lambda s: (s, 0, 0))
    return rows, table, kv


def attend(place, bounds, q_raw, kv, cosine, sine):
    streams, seqlen, depth = kv.shape[0], kv.shape[1], kv.shape[2] // 2
    tokens, features = q_raw.shape[0] // streams, q_raw.shape[1]
    rows, table, kvs = attention_specs(tokens, features, seqlen, depth)
    return pl.pallas_call(
        functools.partial(attend_kernel, depth),
        grid=(streams,),
        out_shape=[jax.ShapeDtypeStruct(q_raw.shape, BF)] * 2,
        in_specs=[SMEM, SMEM, rows, kvs, table, table],
        out_specs=[rows, rows],
        compiler_params=pltpu.CompilerParams(vmem_limit_bytes=40 * MIB),
    )(place, bounds, q_raw, kv, cosine, sine)


def attend_back(place, bounds, queries, kv, cosine, sine, slope):
    streams, seqlen, depth = kv.shape[0], kv.shape[1], kv.shape[2] // 2
    tokens, features = queries.shape[0] // streams, queries.shape[1]
    rows, table, kvs = attention_specs(tokens, features, seqlen, depth)
    return pl.pallas_call(
        functools.partial(attend_back_kernel, depth),
        grid=(streams,),
        out_shape=[jax.ShapeDtypeStruct(queries.shape, BF), jax.ShapeDtypeStruct(kv.shape, BF)],
        in_specs=[SMEM, SMEM, rows, kvs, table, table, rows],
        out_specs=[rows, kvs],
        compiler_params=pltpu.CompilerParams(vmem_limit_bytes=40 * MIB),
    )(place, bounds, queries, kv, cosine, sine, slope)


def gather(v, axis):
    return lax.all_gather(v, axis, axis=0, tiled=True)


def scatter_sum(v, axis):
    return lax.psum_scatter(v.astype(BF), axis, scatter_dimension=0, tiled=True).astype(F32)


def to_columns(weight):
    n_w, n_c, c = lax.axis_size("wt"), lax.axis_size("ctx"), lax.axis_index("ctx")
    rows, cols = weight.shape
    part = lax.dynamic_slice_in_dim(weight, c * (rows // n_c), rows // n_c, 0)
    part = lax.all_to_all(part.reshape(rows // n_c, n_w, cols // n_w), "wt", 1, 0)
    whole = lax.all_gather(part, "ctx", axis=1)
    return whole.reshape(n_w * rows, cols // n_w)


def cut_array(shape, limit):
    rows, cols = shape[-2:]
    lead = math.prod(shape) // (rows * cols)
    for count in range(1, rows + 1):
        if rows % count == 0 and (rows // count) % 16 == 0 and lead * (rows // count) * cols * 2 <= limit:
            return [(i * (rows // count), rows // count, 0, cols) for i in range(count)]
        if cols % (128 * count) == 0 and lead * rows * (cols // count) * 2 <= limit:
            return [(0, rows, i * (cols // count), cols // count) for i in range(count)]
    return [(0, rows, 0, cols)]


def sum_kernel(cuts, n_w, n_c, turned, *refs):
    count = len(turned)
    terms, outs, refs = refs[:count], refs[count : 2 * count], refs[2 * count :]
    own, mates, ups, halves, moved = (refs[i * count : (i + 1) * count] for i in range(5))
    load, place, send, recv = refs[5 * count :]
    c, w = lax.axis_index("ctx"), lax.axis_index("wt")
    chain = n_c // 2
    core, k = lax.rem(c, 2), c // 2
    left = k < chain // 2
    side = jnp.where(left, 0, 1)
    far = jnp.where(left, k, chain - 1 - k)
    middle, outside = far == chain // 2 - 1, far > 0
    mate = {"ctx": c + 1 - 2 * core, "wt": w}
    inner = {"ctx": jnp.where(left, c + 2, c - 2), "wt": w}
    outer = {"ctx": jnp.where(left, c - 2, c + 2), "wt": w}
    peers = [{"ctx": c, "wt": lax.rem(w + r, n_w)} for r in range(1, n_w)]

    barrier = pltpu.get_barrier_semaphore()
    for there in [mate, inner, *peers]:
        pl.semaphore_signal(barrier, inc=1, device_id=there, device_id_type=MESH)

    @pl.when(outside)
    def _():
        pl.semaphore_signal(barrier, inc=1, device_id=outer, device_id_type=MESH)

    pl.semaphore_wait(barrier, n_w + 1 + jnp.where(outside, 1, 0))

    def part(q, ref, *lead):
        _, row, rows, col, cols = cuts[q]
        tail = (pl.ds(row, rows), pl.ds(col, cols))
        return ref.at[(*lead, *tail)]

    def every(q):
        return (slice(None),) if turned[cuts[q][0]] else ()

    def remote(kind, q, src, dst, there):
        return pltpu.make_async_remote_copy(
            src_ref=src, dst_ref=dst, send_sem=send.at[kind, q], recv_sem=recv.at[kind, q], device_id=there,
            device_id_type=MESH,
        )

    def own_load(q):
        a = cuts[q][0]
        return pltpu.make_async_copy(
            part(q, terms[a], *every(q), core, slice(None)), part(q, own[a], *every(q), slice(None)), load.at[q]
        )

    def to_mate(q):
        a = cuts[q][0]
        return remote(
            0, q, part(q, terms[a], *every(q), 1 - core, slice(None)), part(q, mates[a], *every(q), slice(None)), mate
        )

    def to_inner(q):
        a = cuts[q][0]
        return remote(1, q, part(q, own[a], *every(q), slice(None)), part(q, ups[a], *every(q), slice(None)), inner)

    def to_across(q):
        a = cuts[q][0]
        return remote(5, q, part(q, own[a], *every(q), 1 - side), part(q, halves[a], *every(q)), inner)

    def to_peer(q, r):
        a = cuts[q][0]
        there = peers[r]
        return remote(6 + r, q, part(q, halves[a], there["wt"]), part(q, moved[a], w), there)

    def finished(q):
        a = cuts[q][0]
        return part(q, moved[a] if turned[a] else halves[a], *every(q))

    def half_place(q):
        a = cuts[q][0]
        return pltpu.make_async_copy(finished(q), part(q, outs[a], *every(q), core, side), place.at[q])

    def half_across(q):
        a = cuts[q][0]
        return remote(2, q, finished(q), part(q, outs[a], *every(q), core, side), inner)

    def down(kind, q, there):
        a = cuts[q][0]
        here = part(q, outs[a], *every(q), core, slice(None))
        return remote(kind, q, here, here, there)

    def add(q, refs_in, out):
        a, row, rows, col, cols = cuts[q]
        step = 16 if rows % 16 == 0 else rows

        def body(i, carry):
            at = pl.ds(row + i * step, step)
            total = None
            for ref, lead in refs_in:
                term = ref[(*every(q), *lead, at, pl.ds(col, cols))].astype(F32)
                total = term if total is None else total + term
            out[0][(*every(q), *out[1], at, pl.ds(col, cols))] = total.astype(BF)
            return carry

        lax.fori_loop(0, rows // step, body, 0)

    def up_step(q):
        a = cuts[q][0]
        both = (slice(None),)
        own_load(q).wait()
        to_mate(q).wait_recv()

        @pl.when(outside)
        def _():
            remote(1, q, part(q, own[a], *every(q), slice(None)), part(q, ups[a], *every(q), slice(None)), outer).wait_recv()
            add(q, [(own[a], both), (mates[a], both), (ups[a], both)], (own[a], both))

        @pl.when(jnp.logical_not(outside))
        def _():
            add(q, [(own[a], both), (mates[a], both)], (own[a], both))

    def half_step(q):
        a = cuts[q][0]
        to_across(q).wait_recv()
        mine = own[a].at[(*every(q), side)]
        add(q, [(mine, ()), (halves[a], ())], (halves[a], ()))
        if turned[a]:
            for r in range(n_w - 1):
                to_peer(q, r).start()
            row, rows, col, cols = cuts[q][1:]
            moved[a][w, pl.ds(row, rows), pl.ds(col, cols)] = halves[a][w, pl.ds(row, rows), pl.ds(col, cols)]
        else:
            half_place(q).start()
            half_across(q).start()

    def move_step(q):
        a = cuts[q][0]
        if turned[a]:
            for r in range(n_w - 1):
                there = peers[r]
                remote(
                    6 + r, q, part(q, halves[a], there["wt"]), part(q, moved[a], lax.rem(w + n_w - r - 1, n_w)), there
                ).wait_recv()
            half_place(q).start()
            half_across(q).start()

    def down_step(q, inside):
        if inside:
            half_place(q).wait()
            a = cuts[q][0]
            remote(2, q, finished(q), part(q, outs[a], *every(q), core, 1 - side), inner).wait_recv()
        else:
            down(3, q, inner).wait_recv()

        @pl.when(outside)
        def _():
            down(3, q, outer).start()

        down(4, q, mate).start()

    steps = range(len(cuts))
    for q in steps:
        own_load(q).start()
        to_mate(q).start()

    @pl.when(jnp.logical_not(middle))
    def _():
        for q in steps:
            up_step(q)
            to_inner(q).start()
        for q in steps:
            down_step(q, False)
        for q in steps:
            to_inner(q).wait_send()

    @pl.when(middle)
    def _():
        for t in range(len(cuts) + 3):
            if t < len(cuts):
                up_step(t)
                to_across(t).start()
            if 0 <= t - 1 < len(cuts):
                half_step(t - 1)
            if 0 <= t - 2 < len(cuts):
                move_step(t - 2)
            if 0 <= t - 3:
                down_step(t - 3, True)
        for q in steps:
            to_across(q).wait_send()
            half_across(q).wait_send()
            if turned[cuts[q][0]]:
                for r in range(n_w - 1):
                    to_peer(q, r).wait_send()

    for q in steps:
        a = cuts[q][0]
        to_mate(q).wait_send()

        @pl.when(outside)
        def _():
            down(3, q, outer).wait_send()

        other = part(q, outs[a], *every(q), 1 - core, slice(None))
        remote(4, q, other, other, mate).wait_recv()
        down(4, q, mate).wait_send()


def sum_over_ctx(arrays, turned, collective, limit=750_000):
    n_w, n_c = lax.axis_size("wt"), lax.axis_size("ctx")
    shaped, cuts = [], []
    for i, (v, turn) in enumerate(zip(arrays, turned, strict=True)):
        rows, cols = v.shape
        lead = (n_w,) if turn else ()
        shaped.append(v.reshape(*lead, 2, 2, rows // (n_w if turn else 1) // 4, cols))
        cuts += [(i, *cut) for cut in cut_array((*lead, 2, *shaped[-1].shape[-2:]), limit)]

    def scratch(drop, only=False):
        shapes = []
        for v, turn in zip(shaped, turned, strict=True):
            lead = v.shape[:-4]
            keep = (*lead, 2, *v.shape[-2:]) if drop == 1 else (*lead, *v.shape[-2:])
            shapes.append(pltpu.VMEM(keep if turn or not only else (16, 128), BF))
        return shapes

    kinds = 6 + n_w - 1
    sums = pl.pallas_call(
        functools.partial(sum_kernel, cuts, n_w, n_c, turned),
        out_shape=[jax.ShapeDtypeStruct(v.shape, BF) for v in shaped],
        in_specs=[pl.BlockSpec(memory_space=pl.ANY)] * len(shaped),
        out_specs=[pl.BlockSpec(memory_space=pl.ANY)] * len(shaped),
        scratch_shapes=[
            *scratch(1), *scratch(1), *scratch(1), *scratch(2), *scratch(2, True),
            pltpu.SemaphoreType.DMA((len(cuts),)),
            pltpu.SemaphoreType.DMA((len(cuts),)),
            pltpu.SemaphoreType.DMA((kinds, len(cuts))),
            pltpu.SemaphoreType.DMA((kinds, len(cuts))),
        ],
        compiler_params=pltpu.CompilerParams(
            collective_id=collective, has_side_effects=True, vmem_limit_bytes=60 * MIB
        ),
    )(*shaped)
    return [
        s.reshape(n_w, v.shape[0] // n_w, v.shape[1]) if turn else s.reshape(v.shape)
        for s, v, turn in zip(sums, arrays, turned, strict=True)
    ]


def on_device(
    inputs,
    boundaries,
    first_gain,
    query_down,
    query_gain,
    query_up,
    key_weights,
    value_weights,
    output_weights,
    second_gain,
    gate_weights,
    up_weights,
    down_weights,
    cotangent,
):
    n_w, n_c, c = lax.axis_size("wt"), lax.axis_size("ctx"), lax.axis_index("ctx")
    width, halfrows = inputs.shape[-1], inputs.shape[2]
    tokens = 2 * halfrows
    seqlen = tokens * n_c
    depth, rank = key_weights.shape[1], query_down.shape[1]
    place = jnp.stack([c * halfrows, seqlen - (c + 1) * halfrows]).astype(jnp.int32)
    offsets = jnp.arange(halfrows, dtype=jnp.int32)
    cosine, sine = tables(jnp.concatenate([place[0] + offsets, place[1] + offsets]), depth)
    bounds = gather(boundaries, "wt")
    gain_query = gather(query_gain, "wt").astype(F32)
    gain_two = gather(second_gain, "wt").astype(F32)

    x = inputs.reshape(tokens, width)
    cot = cotangent.reshape(tokens, width)
    activ = x.astype(F32)
    r_first = inv_rms(activ)
    x_cols = lax.all_to_all(x, "wt", 1, 0, tiled=True)
    n_cols = x_cols.astype(F32) * gather(r_first, "wt")
    h_cols = (n_cols * first_gain.astype(F32)).astype(BF)
    first_weights = jnp.concatenate([query_down, key_weights, value_weights], axis=1)
    low = scatter_sum(dot(h_cols, first_weights), "wt")
    latent = low[:, :rank]
    r_query = inv_rms(latent)
    n_query = latent * r_query
    q_latent = (n_query * gain_query).astype(BF)
    keys = rotate(low[:, rank : rank + depth], cosine, sine).astype(BF)
    kv = jnp.concatenate([keys, low[:, rank + depth :].astype(BF)], axis=1)
    kv = gather(to_stream(gather(kv, "ctx"), n_c)[None], "wt")
    q_latent = gather(q_latent, "wt")
    up_cols = to_columns(query_up)
    gate_cols = to_columns(gate_weights)
    upper_cols = to_columns(up_weights)
    queries, attn_out = attend(place, bounds, dot(q_latent, up_cols), kv, cosine, sine)

    resid = activ + scatter_sum(dot(attn_out, output_weights), "wt")
    r_second = inv_rms(resid)
    n_second = resid * r_second
    h_second = gather((n_second * gain_two).astype(BF), "wt")
    cot_all = gather(cot, "wt")
    gate = dot(h_second, gate_cols)
    upper = dot(h_second, upper_cols)
    sigma = jax.nn.sigmoid(gate)
    silu = gate * sigma
    hidden = (silu * upper).astype(BF)
    layer_output = (resid + scatter_sum(dot(hidden, down_weights), "wt")).astype(BF)

    d_down = dot_tn(hidden, cot_all)
    d_hidden = dot_nt(cot_all, down_weights)
    d_gate = (d_hidden * upper * sigma * (1.0 + gate * (1.0 - sigma))).astype(BF)
    d_upper = (d_hidden * silu).astype(BF)
    d_h_second = scatter_sum(dot_nt(d_gate, gate_cols) + dot_nt(d_upper, upper_cols), "wt")
    d_gate_weights = dot_tn(h_second, d_gate)
    d_up_weights = dot_tn(h_second, d_upper)
    d_n = d_h_second * gain_two
    d_gain_two = jnp.sum(d_h_second * n_second, axis=0)
    d_resid = cot.astype(F32) + r_second * (
        d_n - n_second * jnp.mean(d_n * n_second, axis=-1, keepdims=True)
    )
    d_proj = gather(d_resid.astype(BF), "wt")
    d_output = dot_tn(attn_out, d_proj)
    d_attended = dot_nt(d_proj, output_weights).astype(BF)
    d_q_raw, d_kv = attend_back(place, bounds, queries, kv, cosine, sine, d_attended)
    d_kv = scatter_sum(d_kv, "wt")[0]
    d_kv = scatter_sum(from_stream(d_kv, n_c), "ctx")
    d_k_raw = rotate(d_kv[:, :depth], cosine, -sine).astype(BF)
    d_v_raw = d_kv[:, depth:].astype(BF)
    d_up_cols = dot_tn(q_latent, d_q_raw)
    d_q_latent = scatter_sum(dot_nt(d_q_raw, up_cols), "wt")
    d_n = d_q_latent * gain_query
    d_gain_query = jnp.sum(d_q_latent * n_query, axis=0)
    d_latent = r_query * (d_n - n_query * jnp.mean(d_n * n_query, axis=-1, keepdims=True))
    low_slope = gather(jnp.concatenate([d_latent.astype(BF), d_k_raw, d_v_raw], axis=1), "wt")
    d_first_weights = dot_tn(h_cols, low_slope)
    d_h_cols = dot_nt(low_slope, first_weights)
    d_gain_one = jnp.sum(d_h_cols * n_cols, axis=0)
    d_n = lax.all_to_all(
        (d_h_cols * first_gain.astype(F32)).astype(BF), "wt", 0, 1, tiled=True
    ).astype(F32)
    n_first = activ * r_first
    input_gradient = d_resid + r_first * (
        d_n - n_first * jnp.mean(d_n * n_first, axis=-1, keepdims=True)
    )

    gains = jnp.concatenate([d_gain_two.reshape(n_w, -1), d_gain_query.reshape(n_w, -1)], axis=1)
    gains = lax.psum_scatter(gains, "wt", scatter_dimension=0)
    gains = lax.psum(jnp.concatenate([d_gain_one, gains]), "ctx")
    one = d_gain_one.shape[0]
    terms = (d_down, d_gate_weights, d_up_weights, d_output, d_up_cols, d_first_weights)
    turned = (False, True, True, False, True, False)
    sums = sum_over_ctx([t.astype(BF) for t in terms], turned, 1)
    sums = [
        s.swapaxes(0, 1).reshape(s.shape[1], -1).astype(F32) if turn else s.astype(F32)
        for s, turn in zip(sums, turned, strict=True)
    ]
    d_down, d_gate_weights, d_up_weights, d_output, d_query_up, d_first_weights = sums
    return (
        layer_output.reshape(inputs.shape),
        input_gradient.astype(BF).reshape(inputs.shape),
        gains[:one],
        d_first_weights[:, :rank],
        gains[one + width // n_w :],
        d_query_up,
        d_first_weights[:, rank : rank + depth],
        d_first_weights[:, rank + depth :],
        d_output,
        gains[one : one + width // n_w],
        d_gate_weights,
        d_up_weights,
        d_down,
    )


def solution(mesh):
    token = P("wt", None, "ctx", None)
    row, vec = P("wt", None), P("wt")
    in_specs = (token, row, vec, row, vec, row, row, row, row, vec, row, row, row, token)
    out_specs = (token, token, vec, row, vec, row, row, row, row, vec, row, row, row)
    return jax.shard_map(
        on_device, mesh=mesh, in_specs=in_specs, out_specs=out_specs, check_vma=False
    )
```

```python
import functools
import math

import jax
import jax.numpy as jnp
from jax import lax
from jax.experimental import pallas as pl
from jax.experimental.pallas import tpu as pltpu
from jax.sharding import PartitionSpec as P

EPS = 1e-06
NEG = -1e30
F32 = jnp.float32
BF = jnp.bfloat16
VMEM = pl.BlockSpec(memory_space=pltpu.VMEM)
SMEM = pl.BlockSpec(memory_space=pltpu.SMEM)
ANY = pl.BlockSpec(memory_space=pl.ANY)
MIB = 1 << 20
MESH = pl.DeviceIdType.MESH


def dot(a, b):
    return jnp.dot(a, b, preferred_element_type=F32)


def dot_nt(a, b):
    return lax.dot_general(a, b, (((1,), (1,)), ((), ())), preferred_element_type=F32)


def dot_tn(a, b):
    return lax.dot_general(a, b, (((0,), (0,)), ((), ())), preferred_element_type=F32)


def inv_rms(v):
    return lax.rsqrt(jnp.mean(v * v, axis=-1, keepdims=True) + EPS)


def rms_back(slope, normal, scale):
    return scale * (slope - normal * jnp.mean(slope * normal, axis=-1, keepdims=True))


def rotate(v, cosine, sine):
    middle = v.shape[-1] // 2
    a, b = v[..., :middle], v[..., middle:]
    return jnp.concatenate([a * cosine - b * sine, b * cosine + a * sine], axis=-1)


def shape_of(*shape, dtype=BF):
    return jax.ShapeDtypeStruct(shape, dtype)


def params(collective, mib):
    return pltpu.CompilerParams(collective_id=collective, has_side_effects=True, vmem_limit_bytes=mib * MIB)


class Group:
    def __init__(self, n_w, n_c):
        self.n_w, self.n_z, self.per = n_w, n_c // 2, n_w // 2
        c, w = lax.axis_index("ctx"), lax.axis_index("wt")
        self.core = lax.rem(c, 2)
        self.z, self.w, self.base = c // 2, w, c - self.core
        self.home = w // self.per
        self.at_home = self.core == self.home
        self.stream = w - self.home * self.per
        self.slot = self.stream * 2 + self.core

    def target(self, j):
        return {"ctx": self.base + self.home, "wt": j}

    def source(self, i):
        return {"ctx": self.base + lax.rem(i, 2), "wt": self.core * self.per + i // 2}

    def column(self, step):
        return {"ctx": 2 * lax.rem(self.z + step, self.n_z) + self.core, "wt": self.w}

    def greet(self, column):
        barrier = pltpu.get_barrier_semaphore()
        others = [
            {"ctx": self.base + lax.rem(self.core + q, 2), "wt": lax.rem(self.w + r, self.n_w)}
            for q in range(2)
            for r in range(self.n_w)
        ][1:]
        if column:
            others += [{"ctx": 2 * lax.rem(self.z + s, self.n_z) + q, "wt": self.w} for s in range(1, self.n_z) for q in range(2)]
        for there in others:
            pl.semaphore_signal(barrier, inc=1, device_id=there, device_id_type=MESH)
        pl.semaphore_wait(barrier, len(others))


class Moves:
    def __init__(self, group, send, recv):
        self.group, self.send, self.recv = group, send, recv

    def start(self, kind, src, dst, there, index, slot, here):
        remote = pltpu.make_async_remote_copy(
            src_ref=src, dst_ref=dst, send_sem=self.send.at[kind, index], recv_sem=self.recv.at[kind, slot],
            device_id=there, device_id_type=MESH,
        )
        local = pltpu.make_async_copy(src, dst, self.recv.at[kind, slot])
        pl.when(jnp.logical_not(here))(remote.start)
        pl.when(here)(local.start)

    def to_target(self, kind, j, src, dst):
        g = self.group
        self.start(kind, src, dst, g.target(j), j, g.slot, g.at_home & (g.w == j))

    def to_source(self, kind, i, src, dst):
        g = self.group
        self.start(kind, src, dst, g.source(i), i, g.w, g.at_home & (g.slot == i))

    def arrived(self, kind, index, dst):
        pltpu.make_async_copy(dst, dst, self.recv.at[kind, index]).wait()

    def sent(self, kind, src, by_target):
        g = self.group
        for i in range(g.n_w):
            at = src(i)
            copy = pltpu.make_async_remote_copy(
                src_ref=at, dst_ref=at, send_sem=self.send.at[kind, i], recv_sem=self.recv.at[kind, i],
                device_id=g.target(i) if by_target else g.source(i), device_id_type=MESH,
            )
            here = g.at_home & ((g.w if by_target else g.slot) == i)
            pl.when(jnp.logical_not(here))(copy.wait_send)


def column_copy(group, part, step, src, dst, send, recv):
    return pltpu.make_async_remote_copy(
        src_ref=src, dst_ref=dst, send_sem=send.at[part, step], recv_sem=recv.at[part, step],
        device_id=group.column(step), device_id_type=MESH,
    )


def exchange_kernel(n_w, split, *refs):
    count = len(split)
    ins, outs = refs[:count], refs[count : 2 * count]
    send, recv, local = refs[2 * count :]
    c, w = lax.axis_index("ctx"), lax.axis_index("wt")
    barrier = pltpu.get_barrier_semaphore()
    for step in range(1, n_w):
        pl.semaphore_signal(
            barrier, inc=1, device_id={"ctx": c, "wt": lax.rem(w + step, n_w)}, device_id_type=MESH
        )
    pl.semaphore_wait(barrier, n_w - 1)
    copies = []
    for a in range(count):
        for step in range(1, n_w):
            there = lax.rem(w + step, n_w)
            copies.append(
                pltpu.make_async_remote_copy(
                    src_ref=ins[a].at[there] if split[a] else ins[a], dst_ref=outs[a].at[w],
                    send_sem=send.at[a, step], recv_sem=recv.at[a, step],
                    device_id={"ctx": c, "wt": there}, device_id_type=MESH,
                )
            )
        copies.append(pltpu.make_async_copy(ins[a].at[w] if split[a] else ins[a], outs[a].at[w], local.at[a]))
    for copy in copies:
        copy.start()
    for copy in copies:
        copy.wait()


def exchange(arrays, split, n_w, collective):
    return pl.pallas_call(
        functools.partial(exchange_kernel, n_w, split),
        out_shape=[
            jax.ShapeDtypeStruct(v.shape if s else (n_w, *v.shape), v.dtype) for v, s in zip(arrays, split, strict=True)
        ],
        in_specs=[ANY] * len(arrays),
        out_specs=[ANY] * len(arrays),
        scratch_shapes=[
            pltpu.SemaphoreType.DMA((len(arrays), n_w)),
            pltpu.SemaphoreType.DMA((len(arrays), n_w)),
            pltpu.SemaphoreType.DMA((len(arrays),)),
        ],
        compiler_params=params(collective, 16),
    )(*arrays)


def first_kernel(
    n_w, n_c,
    x_ref, cot_ref, gain_ref, query_gain_ref, down_ref, key_ref, value_ref, cos_ref, sin_ref,
    h_out, x_out, r_out, latent_out, q_all, kv_all, cot_all,
    x_in, r_in, r_own, parts, low, q_own, kv_own, kv_column, send, recv, z_send, z_recv,
):
    g = Group(n_w, n_c)
    m = Moves(g, send, recv)
    tokens, cols = x_in.shape[1:]
    rank, depth = down_ref.shape[1], key_ref.shape[1]
    r_own[...] = jnp.broadcast_to(inv_rms(x_ref[...].astype(F32)), r_own.shape)
    g.greet(True)
    for j in range(n_w):
        m.to_target(0, j, x_ref.at[:, pl.ds(j * cols, cols)], x_in.at[g.slot])
        m.to_target(1, j, r_own, r_in.at[g.slot])

    for i in range(n_w):
        m.arrived(0, i, x_in.at[i])
        m.arrived(1, i, r_in.at[i])
        x_out[i] = x_in[i]
        r_out[i] = r_in[i]
        h = (x_in[i].astype(F32) * r_in[i, :, :1] * gain_ref[...]).astype(BF)
        h_out[i] = h
        parts[i, :, :rank] = dot(h, down_ref[...]).astype(BF)
        parts[i, :, rank : rank + depth] = dot(h, key_ref[...]).astype(BF)
        parts[i, :, rank + depth :] = dot(h, value_ref[...]).astype(BF)
        m.to_source(2, i, parts.at[i], low.at[g.w])

    for j in range(n_w):
        m.arrived(2, j, low.at[j])
    total = low[0].astype(F32)
    for j in range(1, n_w):
        total += low[j].astype(F32)
    keys = rotate(total[:, rank : rank + depth], cos_ref[...], sin_ref[...]).astype(BF)
    kv = jnp.concatenate([keys, total[:, rank + depth :].astype(BF)], axis=1)
    half = tokens // 2
    mirror = g.n_z - 1 - g.z
    for part in range(2):
        kv_own[part] = kv[part * half : (part + 1) * half]

    def over_z(part, step):
        return column_copy(
            g, part, step, kv_own.at[part], kv_column.at[part, mirror if part else g.z], z_send, z_recv
        )

    for step in range(1, g.n_z):
        for part in range(2):
            over_z(part, step).start()
    kv_column[0, g.z] = kv_own[0]
    kv_column[1, mirror] = kv_own[1]
    latent = total[:, :rank]
    latent_out[...] = latent
    q_own[...] = (latent * inv_rms(latent) * query_gain_ref[...]).astype(BF)
    for j in range(n_w):
        m.to_target(3, j, q_own, q_all.at[g.slot])
    for j in range(n_w):
        m.to_target(4, j, cot_ref, cot_all.at[g.slot])
    for step in range(1, g.n_z):
        for part in range(2):
            over_z(part, step).wait_recv()

    def kv_place(part):
        return kv_all.at[g.stream, part, :, 1 - g.core if part else g.core]

    for part in range(2):
        for j in range(n_w):
            m.to_target(5 + part, j, kv_column.at[part], kv_place(part))
    for i in range(n_w):
        m.arrived(3, i, q_all.at[i])
        m.arrived(4, i, cot_all.at[i])
        for part in range(2):
            m.arrived(5 + part, i, kv_all.at[i // 2, part, :, 1 - i % 2 if part else i % 2])
    m.sent(0, lambda j: x_ref.at[:, pl.ds(j * cols, cols)], True)
    m.sent(1, lambda j: r_own, True)
    m.sent(2, lambda i: parts.at[i], False)
    m.sent(3, lambda j: q_own, True)
    m.sent(4, lambda j: cot_ref, True)
    for part in range(2):
        m.sent(5 + part, lambda j: kv_column.at[part], True)
        for step in range(1, g.n_z):
            over_z(part, step).wait_send()


def first_part(n_w, n_c, x, cot, gain, query_gain, down, key, value, cosine, sine):
    tokens, width = x.shape
    cols, rank, depth = width // n_w, down.shape[1], key.shape[1]
    n_z, half, low = n_c // 2, tokens // 2, rank + 2 * depth
    return pl.pallas_call(
        functools.partial(first_kernel, n_w, n_c),
        out_shape=[
            shape_of(n_w, tokens, cols),
            shape_of(n_w, tokens, cols),
            shape_of(n_w, tokens, 128, dtype=F32),
            shape_of(tokens, rank, dtype=F32),
            shape_of(n_w, tokens, rank),
            shape_of(n_w // 2, 2, n_z, 2, half, 2 * depth),
            shape_of(n_w, tokens, width),
        ],
        in_specs=[VMEM, ANY] + [VMEM] * 7,
        out_specs=[VMEM] * 4 + [ANY] * 3,
        scratch_shapes=[
            pltpu.VMEM((n_w, tokens, cols), BF),
            pltpu.VMEM((n_w, tokens, 128), F32),
            pltpu.VMEM((tokens, 128), F32),
            pltpu.VMEM((n_w, tokens, low), BF),
            pltpu.VMEM((n_w, tokens, low), BF),
            pltpu.VMEM((tokens, rank), BF),
            pltpu.VMEM((2, half, 2 * depth), BF),
            pltpu.VMEM((2, n_z, half, 2 * depth), BF),
            pltpu.SemaphoreType.DMA((7, n_w)),
            pltpu.SemaphoreType.DMA((7, n_w)),
            pltpu.SemaphoreType.DMA((2, n_z)),
            pltpu.SemaphoreType.DMA((2, n_z)),
        ],
        compiler_params=params(1, 40),
    )(x, cot, gain, query_gain, down, key, value, cosine, sine)


def visible_keys(bounds_ref, stream, c, tokens, seqlen):
    half = tokens // 2
    row = lax.broadcasted_iota(jnp.int32, (tokens, 1), 0)
    pos = row + jnp.where(row < half, c * half, seqlen - (c + 1) * half - half)
    begin = jnp.zeros((tokens, 1), jnp.int32)
    for j in range(bounds_ref.shape[1]):
        start = bounds_ref[stream, j]
        begin = jnp.where(pos >= start, jnp.maximum(begin, start), begin)
    key = lax.broadcasted_iota(jnp.int32, (tokens, seqlen), 1)
    return (key >= begin) & (key <= pos)


def probabilities(q, keys, visible):
    scores = jnp.where(visible, dot_nt(q, keys), NEG)
    peak = jnp.max(scores, axis=-1, keepdims=True)
    weight = jnp.where(visible, jnp.exp(scores - peak), 0.0)
    return weight * (1.0 / jnp.sum(weight, axis=-1, keepdims=True))


def attend_kernel(
    n_w, n_c,
    bounds_ref, q_ref, up_ref, kv_ref, cos_ref, sin_ref, out_ref, x_ref, gain_ref,
    queries, attn, resid, h_all,
    parts, land, h_own, send, recv,
):
    g = Group(n_w, n_c)
    m = Moves(g, send, recv)
    tokens, seqlen, depth = q_ref.shape[1], kv_ref.shape[1], kv_ref.shape[2] // 2
    scale = 1.0 / math.sqrt(depth)
    g.greet(False)

    def one(i, carry):
        stream, core = i // 2, lax.rem(i, 2)
        visible = visible_keys(bounds_ref, g.core * g.per + stream, g.base + core, tokens, seqlen)
        raw = dot(q_ref[i], up_ref[...])
        for cut in range(0, up_ref.shape[1], depth):
            span = slice(cut, cut + depth)
            q = (rotate(raw[:, span], cos_ref[core], sin_ref[core]) * scale).astype(BF)
            queries[i, :, span] = q
            probs = probabilities(q, kv_ref[stream, :, :depth], visible).astype(BF)
            attn[i, :, span] = dot(probs, kv_ref[stream, :, depth:]).astype(BF)
        parts[i] = dot(attn[i], out_ref[...]).astype(BF)
        m.to_source(0, i, parts.at[i], land.at[g.w])
        return carry

    lax.fori_loop(0, n_w, one, 0)
    total = x_ref[...].astype(F32)
    for j in range(n_w):
        m.arrived(0, j, land.at[j])
        total += land[j].astype(F32)
    resid[...] = total
    h_own[...] = (total * inv_rms(total) * gain_ref[...]).astype(BF)
    for j in range(n_w):
        m.to_target(1, j, h_own, h_all.at[g.slot])
    for i in range(n_w):
        m.arrived(1, i, h_all.at[i])
    m.sent(0, lambda i: parts.at[i], False)
    m.sent(1, lambda j: h_own, True)


def attend_part(n_w, n_c, bounds, q_all, up_cols, kv, cosine, sine, output, x, gain):
    tokens, width = x.shape
    features = up_cols.shape[1]
    return pl.pallas_call(
        functools.partial(attend_kernel, n_w, n_c),
        out_shape=[
            shape_of(n_w, tokens, features),
            shape_of(n_w, tokens, features),
            shape_of(tokens, width, dtype=F32),
            shape_of(n_w, tokens, width),
        ],
        in_specs=[SMEM] + [VMEM] * 8,
        out_specs=[VMEM] * 3 + [ANY],
        scratch_shapes=[
            pltpu.VMEM((n_w, tokens, width), BF),
            pltpu.VMEM((n_w, tokens, width), BF),
            pltpu.VMEM((tokens, width), BF),
            pltpu.SemaphoreType.DMA((2, n_w)),
            pltpu.SemaphoreType.DMA((2, n_w)),
        ],
        compiler_params=params(2, 50),
    )(bounds, q_all, up_cols, kv, cosine, sine, output, x, gain)


def cut_array(shape, limit, by_rows):
    rows, cols = shape[-2:]
    lead = math.prod(shape) // (rows * cols)
    for count in range(1, rows + 1):
        if rows % count == 0 and (rows // count) % 16 == 0 and lead * (rows // count) * cols * 2 <= limit:
            return [(i * (rows // count), rows // count, 0, cols) for i in range(count)]
        if not by_rows and cols % (128 * count) == 0 and lead * rows * (cols // count) * 2 <= limit:
            return [(0, rows, i * (cols // count), cols // count) for i in range(count)]
    return [(0, rows, 0, cols)]


class Plan:
    def __init__(self, arrays, turned, n_w, slots, limit):
        self.n_w, self.turned, self.arrays = n_w, turned, arrays
        self.wide = [turn and v.shape[1] % 128 == 0 for v, turn in zip(arrays, turned, strict=True)]
        self.shaped, self.results, self.pieces, self.shapes = [], [], [], []
        counts = []
        for a, (v, turn) in enumerate(zip(arrays, turned, strict=True)):
            rows, cols = v.shape
            lead = (n_w,) if turn else ()
            quarter = rows // (n_w if turn else 1) // 4
            self.shaped.append((*lead, 2, 2, quarter, cols))
            self.results.append((2, 2, quarter, n_w * cols) if self.wide[a] else (*lead, 2, 2, quarter, cols))
            for cut in cut_array((*lead, 2, quarter, cols), limit, turn):
                shape = (*lead, 2, cut[1], cut[3])
                if shape not in self.shapes:
                    self.shapes.append(shape)
                    counts.append([])
                kind = self.shapes.index(shape)
                self.pieces.append((a, kind, len(counts[kind]), *cut))
                counts[kind].append(len(self.pieces) - 1)
        self.members = counts
        self.slots = [min(slots, len(c)) for c in counts]

    def __len__(self):
        return len(self.pieces)

    def slot(self, q):
        return self.pieces[q][2] % self.slots[self.pieces[q][1]]

    def before(self, q):
        _, kind, index = self.pieces[q][:3]
        return self.members[kind][index - self.slots[kind]] if index >= self.slots[kind] else None

    def after(self, q):
        _, kind, index = self.pieces[q][:3]
        later = index + self.slots[kind]
        return self.members[kind][later] if later < len(self.members[kind]) else None

    def scratch(self):
        rings, halves, moved = [], [], []
        for shape, slots, members in zip(self.shapes, self.slots, self.members, strict=True):
            rings.append(pltpu.VMEM((slots, *shape), BF))
            halves.append(pltpu.VMEM((len(members), *shape[:-3], *shape[-2:]), BF))
            a = self.pieces[members[0]][0]
            rows, cols = shape[-2:]
            if self.turned[a]:
                moved.append(pltpu.VMEM((len(members), *((rows, self.n_w * cols) if self.wide[a] else (self.n_w, rows, cols))), BF))
            else:
                moved.append(pltpu.VMEM((1, 16, 128), BF))
        kinds, count = 5 + self.n_w, len(self)
        return [
            *rings, *rings, *rings, *halves, *moved,
            pltpu.SemaphoreType.DMA((count,)),
            pltpu.SemaphoreType.DMA((count,)),
            pltpu.SemaphoreType.DMA((kinds, count)),
            pltpu.SemaphoreType.DMA((kinds, count)),
            pltpu.SemaphoreType.REGULAR((2, count)),
        ]

    def scratch_count(self):
        return 5 * len(self.shapes) + 5

    def terms(self):
        return [v.reshape(shape) for v, shape in zip(self.arrays, self.shaped, strict=True)]

    def out_shapes(self):
        return [shape_of(*shape) for shape in self.results]

    def row_shards(self, sums):
        done = []
        for s, v, turn, wide in zip(sums, self.arrays, self.turned, self.wide, strict=True):
            rows, cols = v.shape
            if wide or not turn:
                done.append(s.reshape(-1, s.shape[-1]))
            else:
                done.append(s.reshape(self.n_w, rows // self.n_w, cols).swapaxes(0, 1).reshape(rows // self.n_w, -1))
        return done


class Chain:
    AHEAD, LAG = 2, 8

    def __init__(self, plan, n_c, terms, outs, scratch):
        self.plan, self.n_w, self.terms, self.outs = plan, plan.n_w, terms, outs
        count = len(plan.shapes)
        self.own, self.mates, self.ups, self.halves, self.moved = (
            scratch[i * count : (i + 1) * count] for i in range(5)
        )
        self.load, self.place, self.send, self.recv, self.credit = scratch[5 * count :]
        c, w = lax.axis_index("ctx"), lax.axis_index("wt")
        chain, k = n_c // 2, c // 2
        self.w, self.core = w, lax.rem(c, 2)
        left = k < chain // 2
        self.side = jnp.where(left, 0, 1)
        far = jnp.where(left, k, chain - 1 - k)
        self.middle, self.outside = far == chain // 2 - 1, far > 0
        self.mate = {"ctx": c + 1 - 2 * self.core, "wt": w}
        self.inner = {"ctx": jnp.where(left, c + 2, c - 2), "wt": w}
        self.outer = {"ctx": jnp.where(left, c - 2, c + 2), "wt": w}
        self.peers = [{"ctx": c, "wt": lax.rem(w + r, self.n_w)} for r in range(1, self.n_w)]
        self.now = 0

    def every(self, q):
        return (slice(None),) if self.plan.turned[self.plan.pieces[q][0]] else ()

    def term(self, q, core):
        a, _, _, row, rows, col, cols = self.plan.pieces[q]
        return self.terms[a].at[(*self.every(q), core, slice(None), pl.ds(row, rows), pl.ds(col, cols))]

    def ring(self, q, buffers):
        return buffers[self.plan.pieces[q][1]].at[self.plan.slot(q)]

    def half_buffer(self, q):
        _, kind, index = self.plan.pieces[q][:3]
        return self.halves[kind].at[index]

    def remote(self, kind, q, src, dst, there):
        return pltpu.make_async_remote_copy(
            src_ref=src, dst_ref=dst, send_sem=self.send.at[kind, q], recv_sem=self.recv.at[kind, q], device_id=there,
            device_id_type=MESH,
        )

    def own_load(self, q):
        return pltpu.make_async_copy(self.term(q, self.core), self.ring(q, self.own), self.load.at[q])

    def to_mate(self, q):
        return self.remote(0, q, self.term(q, 1 - self.core), self.ring(q, self.mates), self.mate)

    def along(self, q, there):
        return self.remote(1, q, self.ring(q, self.own), self.ring(q, self.ups), there)

    def to_across(self, q):
        side = self.ring(q, self.own).at[(*self.every(q), 1 - self.side)]
        return self.remote(5, q, side, self.half_buffer(q), self.inner)

    def moved_part(self, q, source):
        a, kind, index = self.plan.pieces[q][:3]
        if not self.plan.wide[a]:
            return self.moved[kind].at[index, source]
        cols = self.terms[a].shape[-1]
        return self.moved[kind].at[index, :, pl.ds(pl.multiple_of(source * cols, 128), cols)]

    def to_peer(self, q, r, slot):
        there = self.peers[r]
        return self.remote(6 + r, q, self.half_buffer(q).at[there["wt"]], self.moved_part(q, slot), there)

    def finished(self, q):
        a, kind, index = self.plan.pieces[q][:3]
        return self.moved[kind].at[index] if self.plan.turned[a] else self.half_buffer(q)

    def result(self, q, *lead):
        a, _, _, row, rows, col, cols = self.plan.pieces[q]
        if self.plan.wide[a]:
            return self.outs[a].at[(*lead, pl.ds(row, rows))]
        return self.outs[a].at[(*self.every(q), *lead, pl.ds(row, rows), pl.ds(col, cols))]

    def half_place(self, q):
        return pltpu.make_async_copy(self.finished(q), self.result(q, self.core, self.side), self.place.at[q])

    def half_across(self, q, side):
        return self.remote(2, q, self.finished(q), self.result(q, self.core, side), self.inner)

    def down(self, kind, q, there):
        here = self.result(q, self.core, slice(None))
        return self.remote(kind, q, here, here, there)

    def add(self, q, ins, out):
        rows = out.shape[-2]
        step = 16 if rows % 16 == 0 else rows
        lead = (slice(None),) * (len(out.shape) - 2)

        def body(i, carry):
            at = (*lead, pl.ds(i * step, step))
            total = ins[0][at].astype(F32)
            for ref in ins[1:]:
                total += ref[at].astype(F32)
            out[at] = total.astype(BF)
            return carry

        lax.fori_loop(0, rows // step, body, 0)

    def grant(self, kind, q, there):
        pl.semaphore_signal(self.credit.at[kind, q], inc=1, device_id=there, device_id_type=MESH)

    def prefetch(self, q):
        before = self.plan.before(q)
        if before is not None:
            pl.when(self.middle)(self.to_across(before).wait_send)
            pl.when(jnp.logical_not(self.middle))(self.along(before, self.inner).wait_send)
            pl.semaphore_wait(self.credit.at[0, q], 1)
        self.own_load(q).start()
        self.to_mate(q).start()

    def up(self, q):
        self.own_load(q).wait()
        self.to_mate(q).wait_recv()
        after, before = self.plan.after(q), self.plan.before(q)
        own, mates, ups = (self.ring(q, b) for b in (self.own, self.mates, self.ups))

        @pl.when(self.outside)
        def _():
            self.along(q, self.outer).wait_recv()
            self.add(q, [own, mates, ups], own)
            if after is not None:
                self.grant(1, after, self.outer)

        @pl.when(jnp.logical_not(self.outside))
        def _():
            self.add(q, [own, mates], own)

        if after is not None:
            self.grant(0, after, self.mate)

        @pl.when(self.middle)
        def _():
            self.to_across(q).start()

        @pl.when(jnp.logical_not(self.middle))
        def _():
            if before is not None:
                pl.semaphore_wait(self.credit.at[1, q], 1)
            self.along(q, self.inner).start()

    def finish_half(self, q):
        self.to_across(q).wait_recv()
        half = self.half_buffer(q)
        self.add(q, [self.ring(q, self.own).at[(*self.every(q), self.side)], half], half)
        if self.plan.turned[self.plan.pieces[q][0]]:
            for r in range(self.n_w - 1):
                self.to_peer(q, r, self.w).start()
            self.moved_part(q, self.w)[...] = half[self.w]
        else:
            self.spread(q)

    def spread(self, q):
        self.half_place(q).start()
        self.half_across(q, self.side).start()

    def move(self, q):
        if self.plan.turned[self.plan.pieces[q][0]]:
            for r in range(self.n_w - 1):
                self.to_peer(q, r, lax.rem(self.w + self.n_w - r - 1, self.n_w)).wait_recv()
            self.spread(q)

    def pass_down(self, q):
        pl.when(self.outside)(self.down(3, q, self.outer).start)
        self.down(4, q, self.mate).start()

    def tick(self):
        t, count = self.now, len(self.plan)
        self.now += 1
        if t == 0:
            for q in range(min(self.AHEAD, count)):
                self.prefetch(q)
        if t < count:
            self.up(t)

        @pl.when(self.middle)
        def _():
            if 0 <= t - 1 < count:
                self.finish_half(t - 1)
            if 0 <= t - 2 < count:
                self.move(t - 2)
            if 0 <= t - 3 < count:
                self.half_place(t - 3).wait()
                self.half_across(t - 3, 1 - self.side).wait_recv()
                self.pass_down(t - 3)

        if 0 <= t - self.LAG < count:

            @pl.when(jnp.logical_not(self.middle))
            def _():
                self.down(3, t - self.LAG, self.inner).wait_recv()
                self.pass_down(t - self.LAG)

        if self.AHEAD <= t + self.AHEAD < count:
            self.prefetch(t + self.AHEAD)

    def ticks(self, number):
        for _ in range(min(number, len(self.plan) + self.LAG - self.now)):
            self.tick()

    def finish(self):
        self.ticks(len(self.plan) + self.LAG)
        for q in range(len(self.plan)):
            turned = self.plan.turned[self.plan.pieces[q][0]]

            @pl.when(self.middle)
            def _():
                if self.plan.after(q) is None:
                    self.to_across(q).wait_send()
                self.half_across(q, self.side).wait_send()
                for r in range(self.n_w - 1 if turned else 0):
                    self.to_peer(q, r, self.w).wait_send()

            if self.plan.after(q) is None:
                pl.when(jnp.logical_not(self.middle))(self.along(q, self.inner).wait_send)
            self.to_mate(q).wait_send()
            pl.when(self.outside)(self.down(3, q, self.outer).wait_send)
            other = self.result(q, 1 - self.core, slice(None))
            self.remote(4, q, other, other, self.mate).wait_recv()
            self.down(4, q, self.mate).wait_send()


def sum_kernel(plan, n_c, *refs):
    n_w, count = plan.n_w, len(plan.arrays)
    terms, refs = refs[:count], refs[count:]
    gain_terms, first_gain_terms, layer_terms, resid_ref = refs[:4]
    outs, refs = refs[4 : 4 + count], refs[4 + count :]
    gains_out, layer_out, refs = refs[0], refs[1], refs[2:]
    scratch, refs = refs[: plan.scratch_count()], refs[plan.scratch_count() :]
    layer_land, gain_land, gain_own, gain_all, group_send, group_recv, gain_send, gain_recv = refs
    g = Group(n_w, n_c)
    m = Moves(g, group_send, group_recv)
    chain = Chain(plan, n_c, terms, outs, scratch)
    c, w = lax.axis_index("ctx"), g.w
    g.greet(True)

    def gain_block(step):
        j = lax.rem(w + step, n_w)
        return pltpu.make_async_remote_copy(
            src_ref=gain_terms.at[j], dst_ref=gain_land.at[step], send_sem=gain_send.at[step],
            recv_sem=gain_recv.at[step], device_id={"ctx": c, "wt": j}, device_id_type=MESH,
        )

    def gain_sum(step):
        return pltpu.make_async_remote_copy(
            src_ref=gain_own, dst_ref=gain_all.at[step], send_sem=gain_send.at[n_w + step],
            recv_sem=gain_recv.at[n_w + step], device_id={"ctx": lax.rem(c + step, n_c), "wt": w}, device_id_type=MESH,
        )

    for step in range(1, n_w):
        gain_block(step).start()
    chain.ticks(2)
    for i in range(n_w):
        m.to_source(0, i, layer_terms.at[i], layer_land.at[w])
    chain.ticks(4)
    first = first_gain_terms.shape[1]
    total = gain_terms[w]
    for step in range(1, n_w):
        gain_block(step).wait_recv()
        total += gain_land[step]
    gain_own[:, :first] = first_gain_terms[...]
    gain_own[:, first:] = total
    for step in range(1, n_c):
        gain_sum(step).start()
    total = resid_ref[...]
    for j in range(n_w):
        m.arrived(0, j, layer_land.at[j])
        total += layer_land[j].astype(F32)
    layer_out[...] = total.astype(BF)
    chain.ticks(4)
    total = gain_own[...]
    for step in range(1, n_c):
        gain_sum(step).wait_recv()
        total += gain_all[step]
    gains_out[...] = total
    chain.finish()
    for step in range(1, n_w):
        gain_block(step).wait_send()
    for step in range(1, n_c):
        gain_sum(step).wait_send()
    m.sent(0, lambda i: layer_terms.at[i], False)


def sum_over_ctx(plan, n_c, collective, gain_terms, first_gain_terms, layer_terms, resid):
    n_w, count = plan.n_w, len(plan.arrays)
    gains = gain_terms.shape[-1] + first_gain_terms.shape[-1]
    sums = pl.pallas_call(
        functools.partial(sum_kernel, plan, n_c),
        out_shape=[*plan.out_shapes(), shape_of(8, gains, dtype=F32), shape_of(*resid.shape)],
        in_specs=[ANY] * count + [VMEM, VMEM, ANY, VMEM],
        out_specs=[ANY] * count + [VMEM, VMEM],
        scratch_shapes=[
            *plan.scratch(),
            pltpu.VMEM(layer_terms.shape, BF),
            pltpu.VMEM(gain_terms.shape, F32),
            pltpu.VMEM((8, gains), F32),
            pltpu.VMEM((n_c, 8, gains), F32),
            pltpu.SemaphoreType.DMA((1, n_w)),
            pltpu.SemaphoreType.DMA((1, n_w)),
            pltpu.SemaphoreType.DMA((n_w + n_c,)),
            pltpu.SemaphoreType.DMA((n_w + n_c,)),
        ],
        compiler_params=params(collective, 60),
    )(*plan.terms(), gain_terms, first_gain_terms, layer_terms, resid)
    return plan.row_shards(sums[:count]), sums[-2], sums[-1]


def norm_back(g, m, feed_ref, resid_ref, gain_ref, cot_ref, land, proj_own, proj_in, d_resid, d_gain, ticks):
    for i in range(g.n_w):
        m.to_source(0, i, feed_ref.at[i], land.at[g.w])
    ticks(3)
    for j in range(g.n_w):
        m.arrived(0, j, land.at[j])
    d_h = land[0].astype(F32)
    for j in range(1, g.n_w):
        d_h += land[j].astype(F32)
    resid = resid_ref[...]
    scale = inv_rms(resid)
    normal = resid * scale
    d_gain[...] = jnp.broadcast_to(jnp.sum(d_h * normal, axis=0, keepdims=True), d_gain.shape)
    total = cot_ref[...].astype(F32) + rms_back(d_h * gain_ref[...], normal, scale)
    d_resid[...] = total
    proj_own[...] = total.astype(BF)
    for j in range(g.n_w):
        m.to_target(1, j, proj_own, proj_in.at[g.slot])
    ticks(3)
    for i in range(g.n_w):
        m.arrived(1, i, proj_in.at[i])


def norm_back_ends(m, feed_ref, proj_own):
    m.sent(0, lambda i: feed_ref.at[i], False)
    m.sent(1, lambda j: proj_own, True)


NORM_SEMAPHORES, BACK_SEMAPHORES = 2, 6


def norm_back_kernel(
    n_w, n_c, feed_ref, resid_ref, gain_ref, cot_ref, proj_all, d_resid, d_gain, land, proj_own, send, recv
):
    g = Group(n_w, n_c)
    m = Moves(g, send, recv)
    g.greet(False)
    norm_back(g, m, feed_ref, resid_ref, gain_ref, cot_ref, land, proj_own, proj_all, d_resid, d_gain, lambda n: None)
    norm_back_ends(m, feed_ref, proj_own)


def attend_back(
    g, m,
    bounds_ref, proj_ref, d_resid_ref, out_ref, queries_ref, kv_ref, cos_ref, sin_ref, up_ref, latent_ref,
    query_gain_ref, down_ref, key_ref, value_ref, x_in_ref, r_in_ref, gain_ref, x_ref,
    d_q_out, low_out, slope_out, d_query_gain, d_gain,
    d_kv, kv_parts, kv_land, kv_column, kv_z, q_parts, q_land,
    low_own, low_in, n_parts, n_land, z_send, z_recv, out_sem, ticks,
):
    tokens, seqlen, depth = x_ref.shape[0], kv_ref.shape[1], kv_ref.shape[2] // 2
    rank, half, cols = down_ref.shape[1], tokens // 2, x_in_ref.shape[2]
    n_w = g.n_w
    mirror = g.n_z - 1 - g.z
    scale = 1.0 / math.sqrt(depth)

    def kv_part(stream, core, part):
        return kv_parts.at[stream, part, :, 1 - core if part else core]

    def one_stream(stream):
        d_kv[...] = jnp.zeros_like(d_kv)
        for core in range(2):
            i = 2 * stream + core
            visible = visible_keys(bounds_ref, g.core * g.per + stream, g.base + core, tokens, seqlen)
            slopes = dot_nt(proj_ref[i], out_ref[...]).astype(BF)
            d_keys = jnp.zeros((seqlen, depth), F32)
            d_values = jnp.zeros((seqlen, depth), F32)
            for cut in range(0, up_ref.shape[1], depth):
                span = slice(cut, cut + depth)
                q, slope = queries_ref[i, :, span], slopes[:, span]
                probs = probabilities(q, kv_ref[stream, :, :depth], visible)
                d_probs = dot_nt(slope, kv_ref[stream, :, depth:])
                delta = jnp.sum(probs * d_probs, axis=-1, keepdims=True)
                d_scores = (probs * (d_probs - delta)).astype(BF)
                d_q = dot(d_scores, kv_ref[stream, :, :depth])
                d_q_out[i, :, span] = (rotate(d_q, cos_ref[core], -sin_ref[core]) * scale).astype(BF)
                d_keys += dot_tn(d_scores, q)
                d_values += dot_tn(probs.astype(BF), slope)
            shaped = (2, g.n_z, 2, half, depth)
            d_kv[:, :, :, :, :depth] += d_keys.reshape(shaped)
            d_kv[:, :, :, :, depth:] += d_values.reshape(shaped)
            q_parts[i] = dot_nt(d_q_out[i], up_ref[...]).astype(BF)
            m.to_source(0, i, q_parts.at[i], q_land.at[g.w])
            ticks(2)
        kv_parts[stream] = d_kv[...].astype(BF)
        for core in range(2):
            for part in range(2):
                m.to_source(1 + part, 2 * stream + core, kv_part(stream, core, part), kv_land.at[g.w, part])

    if n_w <= 4:
        for stream in range(g.per):
            one_stream(stream)
    else:
        lax.fori_loop(0, g.per, lambda stream, carry: (one_stream(stream), carry)[1], 0)
    ticks(1)
    for j in range(n_w):
        m.arrived(0, j, q_land.at[j])
    d_n = q_land[0].astype(F32)
    for j in range(1, n_w):
        d_n += q_land[j].astype(F32)
    latent = latent_ref[...]
    r_query = inv_rms(latent)
    n_query = latent * r_query
    d_query_gain[...] = jnp.broadcast_to(jnp.sum(d_n * n_query, axis=0, keepdims=True), d_query_gain.shape)
    low_own[:, :rank] = rms_back(d_n * query_gain_ref[...], n_query, r_query).astype(BF)
    lead = pl.ds(0, rank)
    for j in range(n_w):
        m.to_target(3, j, low_own.at[:, lead], low_in.at[g.slot, :, lead])
    ticks(1)

    for j in range(n_w):
        for part in range(2):
            m.arrived(1 + part, j, kv_land.at[j, part])
    total = kv_land[0].astype(F32)
    for j in range(1, n_w):
        total += kv_land[j].astype(F32)
    kv_column[...] = total.astype(BF)

    def over_z(part, step):
        z = lax.rem(g.z + step, g.n_z)
        return column_copy(
            g, part, step, kv_column.at[part, g.n_z - 1 - z if part else z], kv_z.at[step, part], z_send, z_recv
        )

    for step in range(1, g.n_z):
        for part in range(2):
            over_z(part, step).start()
    ticks(2)
    own = [kv_column[0, g.z].astype(F32), kv_column[1, mirror].astype(F32)]
    for step in range(1, g.n_z):
        for part in range(2):
            over_z(part, step).wait_recv()
            own[part] += kv_z[step, part].astype(F32)
    own = jnp.concatenate(own, axis=0)
    low_own[:, rank : rank + depth] = rotate(own[:, :depth], cos_ref[g.core], -sin_ref[g.core]).astype(BF)
    low_own[:, rank + depth :] = own[:, depth:].astype(BF)
    tail = pl.ds(rank, 2 * depth)
    for j in range(n_w):
        m.to_target(4, j, low_own.at[:, tail], low_in.at[g.slot, :, tail])

    d_first = jnp.zeros((1, cols), F32)
    for i in range(n_w):
        m.arrived(3, i, low_in.at[i, :, lead])
        d_h = dot_nt(low_in[i, :, :rank], down_ref[...])
        m.arrived(4, i, low_in.at[i, :, tail])
        d_h += dot_nt(low_in[i, :, rank : rank + depth], key_ref[...])
        d_h += dot_nt(low_in[i, :, rank + depth :], value_ref[...])
        normal = x_in_ref[i].astype(F32) * r_in_ref[i, :, :1]
        d_first += jnp.sum(d_h * normal, axis=0, keepdims=True)
        n_parts[i] = (d_h * gain_ref[...]).astype(BF)
        m.to_source(5, i, n_parts.at[i], n_land.at[g.w])
    d_gain[...] = jnp.broadcast_to(d_first, d_gain.shape)
    keep = pltpu.make_async_copy(low_in, low_out, out_sem.at[0])
    keep.start()
    ticks(2)
    for j in range(n_w):
        m.arrived(5, j, n_land.at[j])
    d_n = jnp.concatenate([n_land[j].astype(F32) for j in range(n_w)], axis=1)
    x = x_ref[...].astype(F32)
    r_first = inv_rms(x)
    slope_out[...] = (d_resid_ref[...] + rms_back(d_n, x * r_first, r_first)).astype(BF)

    keep.wait()
    m.sent(0, lambda i: q_parts.at[i], False)
    m.sent(3, lambda j: low_own.at[:, lead], True)
    m.sent(4, lambda j: low_own.at[:, tail], True)
    m.sent(5, lambda i: n_parts.at[i], False)
    for part in range(2):
        m.sent(1 + part, lambda i: kv_part(i // 2, i % 2, part), False)
        for step in range(1, g.n_z):
            over_z(part, step).wait_send()


def attend_back_kernel(n_w, n_c, *refs):
    *refs, send, recv, z_send, z_recv, out_sem = refs
    g = Group(n_w, n_c)
    g.greet(True)
    attend_back(g, Moves(g, send, recv), *refs, z_send, z_recv, out_sem, lambda n: None)


def late_kernel(n_w, n_c, plan, *refs):
    count = len(plan.arrays)
    bounds_ref, feed_ref, resid_ref, gain_ref, cot_ref, *refs = refs
    rest, terms, refs = refs[:15], refs[15 : 15 + count], refs[15 + count :]
    sums, refs = refs[:count], refs[count:]
    (proj_out, *back_outs), norm_gain, refs = refs[:6], refs[6], refs[7:]
    scratch, refs = refs[: plan.scratch_count()], refs[plan.scratch_count() :]
    land, proj_own, proj_in, d_resid, norm_send, norm_recv, proj_sem, *refs = refs
    *back_scratch, send, recv, z_send, z_recv, out_sem = refs
    g = Group(n_w, n_c)
    norm_moves = Moves(g, norm_send, norm_recv)
    chain = Chain(plan, n_c, terms, sums, scratch)
    g.greet(True)
    norm_back(g, norm_moves, feed_ref, resid_ref, gain_ref, cot_ref, land, proj_own, proj_in, d_resid, norm_gain, chain.ticks)
    keep = pltpu.make_async_copy(proj_in, proj_out, proj_sem.at[0])
    keep.start()
    attend_back(
        g, Moves(g, send, recv), bounds_ref, proj_in, d_resid, *rest, *back_outs, *back_scratch,
        z_send, z_recv, out_sem, chain.ticks,
    )
    chain.finish()
    keep.wait()
    norm_back_ends(norm_moves, feed_ref, proj_own)


def bytes_of(shapes):
    return sum(math.prod(v.shape) * jnp.dtype(v.dtype).itemsize for v in shapes)


def late_part(n_w, n_c, plan, bounds, late, rest):
    feed, resid, gain, cot = late
    kv, up_cols, x = rest[2], rest[5], rest[14]
    (tokens, width), (rank, features) = x.shape, up_cols.shape
    per, seqlen, both = kv.shape
    n_z, half, cols, low = n_c // 2, tokens // 2, width // n_w, rank + both
    proj = shape_of(n_w, tokens, width)
    d_resid, norm_gain = shape_of(tokens, width, dtype=F32), shape_of(8, width, dtype=F32)
    back_outs = [
        shape_of(n_w, tokens, features),
        shape_of(n_w, tokens, low),
        shape_of(tokens, width),
        shape_of(8, rank, dtype=F32),
        shape_of(8, cols, dtype=F32),
    ]
    back_specs = [VMEM, ANY] + [VMEM] * 3
    norm_scratch = [pltpu.VMEM((n_w, tokens, width), BF), pltpu.VMEM((tokens, width), BF)]
    norm_semaphores = [pltpu.SemaphoreType.DMA((NORM_SEMAPHORES, n_w))] * 2
    back_scratch = [
        pltpu.VMEM((2, n_z, 2, half, both), F32),
        pltpu.VMEM((per, 2, n_z, 2, half, both), BF),
        pltpu.VMEM((n_w, 2, n_z, half, both), BF),
        pltpu.VMEM((2, n_z, half, both), BF),
        pltpu.VMEM((n_z, 2, half, both), BF),
        pltpu.VMEM((n_w, tokens, rank), BF),
        pltpu.VMEM((n_w, tokens, rank), BF),
        pltpu.VMEM((tokens, low), BF),
        pltpu.VMEM((n_w, tokens, low), BF),
        pltpu.VMEM((n_w, tokens, cols), BF),
        pltpu.VMEM((n_w, tokens, cols), BF),
    ]
    back_semaphores = [
        pltpu.SemaphoreType.DMA((BACK_SEMAPHORES, n_w)),
        pltpu.SemaphoreType.DMA((BACK_SEMAPHORES, n_w)),
        pltpu.SemaphoreType.DMA((2, n_z)),
        pltpu.SemaphoreType.DMA((2, n_z)),
        pltpu.SemaphoreType.DMA((1,)),
    ]
    merged_scratch = [
        *plan.scratch(), *norm_scratch, pltpu.VMEM(proj.shape, BF), pltpu.VMEM(d_resid.shape, F32), *norm_semaphores,
        pltpu.SemaphoreType.DMA((1,)), *back_scratch, *back_semaphores,
    ]
    buffers = [v for v in merged_scratch if v.dtype in (BF, F32)]
    if bytes_of([*buffers, *rest, *late[1:], *back_outs, norm_gain]) < 60 * MIB:
        count = len(plan.arrays)
        done = pl.pallas_call(
            functools.partial(late_kernel, n_w, n_c, plan),
            out_shape=[*plan.out_shapes(), proj, *back_outs, norm_gain],
            in_specs=[SMEM, ANY, VMEM, VMEM, VMEM] + [VMEM] * len(rest) + [ANY] * count,
            out_specs=[ANY] * count + [ANY] + back_specs + [VMEM],
            scratch_shapes=merged_scratch,
            compiler_params=params(3, 62),
        )(bounds, feed, resid, gain, cot, *rest, *plan.terms())
        d_proj, d_q_raw, d_low, slope, d_query_gain, d_first_gain, d_norm_gain = done[count:]
        return plan.row_shards(done[:count]), d_proj, d_q_raw, d_low, slope, d_norm_gain, d_query_gain, d_first_gain
    d_proj, d_resid, d_norm_gain = pl.pallas_call(
        functools.partial(norm_back_kernel, n_w, n_c),
        out_shape=[proj, d_resid, norm_gain],
        in_specs=[ANY, VMEM, VMEM, VMEM],
        out_specs=[ANY, VMEM, VMEM],
        scratch_shapes=[*norm_scratch, *norm_semaphores],
        compiler_params=params(5, 40),
    )(feed, resid, gain, cot)
    d_q_raw, d_low, slope, d_query_gain, d_first_gain = pl.pallas_call(
        functools.partial(attend_back_kernel, n_w, n_c),
        out_shape=back_outs,
        in_specs=[SMEM] + [VMEM] * (2 + len(rest)),
        out_specs=back_specs,
        scratch_shapes=[*back_scratch, *back_semaphores],
        compiler_params=params(6, 60),
    )(bounds, d_proj, d_resid, *rest)
    return None, d_proj, d_q_raw, d_low, slope, d_norm_gain, d_query_gain, d_first_gain


def tables(positions, width):
    exponent = jnp.arange(width // 2, dtype=F32) * (-2.0 / width)
    angles = positions.astype(F32)[..., None] * (10000.0**exponent)
    return jnp.cos(angles), jnp.sin(angles)


def whole_columns(part, rows):
    whole = lax.all_gather(part, "ctx", axis=1)
    return whole.reshape(rows, part.shape[-1])


def on_device(
    inputs,
    boundaries,
    first_gain,
    query_down,
    query_gain,
    query_up,
    key_weights,
    value_weights,
    output_weights,
    second_gain,
    gate_weights,
    up_weights,
    down_weights,
    cotangent,
):
    n_w, n_c, c = lax.axis_size("wt"), lax.axis_size("ctx"), lax.axis_index("ctx")
    width, half = inputs.shape[-1], inputs.shape[2]
    tokens, seqlen = 2 * half, 2 * half * n_c
    depth, rank = key_weights.shape[1], query_down.shape[1]
    hidden_cols = down_weights.shape[0]

    def for_columns(weight):
        rows = weight.shape[0] // n_c
        part = lax.dynamic_slice_in_dim(weight, c * rows, rows, 0)
        return part.reshape(rows, n_w, -1).swapaxes(0, 1)

    wide_bounds = jnp.zeros((8, 128), jnp.int32).at[0, : boundaries.shape[1]].set(boundaries[0])
    gains = jnp.concatenate([query_gain, second_gain]).astype(F32)
    gains = jnp.broadcast_to(gains[None], (8, gains.shape[0]))
    bounds, gains, up_part, gate_part, upper_part = exchange(
        [wide_bounds, gains, for_columns(query_up), for_columns(gate_weights), for_columns(up_weights)],
        (False, False, True, True, True), n_w, 0,
    )
    bounds = bounds[:, 0, : boundaries.shape[1]]
    gain_query = gains[:, 0, : rank // n_w].reshape(1, rank)
    gain_two = gains[:, 0, rank // n_w :].reshape(1, width)
    gain_one = first_gain.astype(F32)[None]
    up_cols = whole_columns(up_part, rank)
    gate_cols = whole_columns(gate_part, width)
    upper_cols = whole_columns(upper_part, width)

    ctx = jnp.stack([c - c % 2, c - c % 2 + 1])[:, None]
    offsets = jnp.arange(half, dtype=jnp.int32)[None]
    positions = jnp.concatenate([ctx * half + offsets, seqlen - (ctx + 1) * half + offsets], axis=1)
    cosine, sine = tables(positions, depth)
    x = inputs.reshape(tokens, width)
    cot = cotangent.reshape(tokens, width)
    h_cols, x_in, r_in, latent, q_all, kv, cot_all = first_part(
        n_w, n_c, x, cot, gain_one, gain_query, query_down, key_weights, value_weights,
        lax.dynamic_index_in_dim(cosine, c % 2, keepdims=False), lax.dynamic_index_in_dim(sine, c % 2, keepdims=False),
    )
    kv = kv.reshape(n_w // 2, seqlen, 2 * depth)
    queries, attn, resid, h_all = attend_part(
        n_w, n_c, bounds, q_all, up_cols, kv, cosine, sine, output_weights, x, gain_two
    )

    h_second = h_all.reshape(n_w * tokens, width)
    slope = cot_all.reshape(n_w * tokens, width)
    gate = dot(h_second, gate_cols)
    upper = dot(h_second, upper_cols)
    sigma = jax.nn.sigmoid(gate)
    silu = gate * sigma
    hidden = (silu * upper).astype(BF)
    d_hidden = dot_nt(slope, down_weights)
    d_gate = (d_hidden * upper * sigma * (1.0 + gate * (1.0 - sigma))).astype(BF)
    d_upper = (d_hidden * silu).astype(BF)
    out_part = dot(hidden, down_weights).astype(BF)
    d_down = dot_tn(hidden, slope).astype(BF)
    d_gate_weights = dot_tn(h_second, d_gate).astype(BF)
    d_up_weights = dot_tn(h_second, d_upper).astype(BF)
    feed = (dot_nt(d_gate, gate_cols) + dot_nt(d_upper, upper_cols)).astype(BF)

    def grouped(v):
        return v.reshape(n_w, tokens, v.shape[-1])

    def flat(v):
        return v.reshape(n_w * tokens, v.shape[-1])

    plan = Plan([d_down, d_gate_weights, d_up_weights], (False, True, True), n_w, 6, 380_000)
    late = (grouped(feed), resid, gain_two, cot)
    rest = (
        output_weights, queries, kv, cosine, sine, up_cols, latent, gain_query, query_down, key_weights, value_weights,
        x_in, r_in, gain_one, x,
    )
    feed_sums, d_proj, d_q_raw, d_low, input_gradient, d_gain_two, d_gain_query, d_gain_one = late_part(
        n_w, n_c, plan, bounds, late, rest
    )
    d_output = dot_tn(flat(attn), flat(d_proj)).astype(BF)
    d_up_cols = dot_tn(flat(q_all), flat(d_q_raw)).astype(BF)
    d_first_weights = dot_tn(flat(h_cols), flat(d_low)).astype(BF)
    spread = [v.reshape(8, n_w, -1).swapaxes(0, 1) for v in (d_gain_two, d_gain_query)]
    terms, turned = [d_output, d_up_cols, d_first_weights], (False, True, False)
    if feed_sums is None:
        terms, turned = [*plan.arrays, *terms], (*plan.turned, *turned)
    sums, gains, layer_output = sum_over_ctx(
        Plan(terms, turned, n_w, 6, 380_000), n_c, 4,
        jnp.concatenate(spread, axis=2), d_gain_one, grouped(out_part), resid,
    )
    sums = [s.astype(F32) for s in [*(feed_sums or ()), *sums]]
    d_down, d_gate_weights, d_up_weights, d_output, d_query_up, d_first_weights = sums
    one, two = width // n_w, 2 * (width // n_w)
    return (
        layer_output.reshape(inputs.shape),
        input_gradient.reshape(inputs.shape),
        gains[0, :one],
        d_first_weights[:, :rank],
        gains[0, two:],
        d_query_up,
        d_first_weights[:, rank : rank + depth],
        d_first_weights[:, rank + depth :],
        d_output,
        gains[0, one:two],
        d_gate_weights,
        d_up_weights,
        d_down,
    )


def solution(mesh):
    token = P("wt", None, "ctx", None)
    row, vec = P("wt", None), P("wt")
    in_specs = (token, row, vec, row, vec, row, row, row, row, vec, row, row, row, token)
    out_specs = (token, token, vec, row, vec, row, row, row, row, vec, row, row, row)
    return jax.shard_map(
        on_device, mesh=mesh, in_specs=in_specs, out_specs=out_specs, check_vma=False
    )
```

```python
import functools
import math

import jax
import jax.numpy as jnp
from jax import lax
from jax.experimental import pallas as pl
from jax.experimental.pallas import tpu as pltpu
from jax.sharding import PartitionSpec as P

EPS = 1e-06
NEG = -1e30
F32 = jnp.float32
BF = jnp.bfloat16
VMEM = pl.BlockSpec(memory_space=pltpu.VMEM)
SMEM = pl.BlockSpec(memory_space=pltpu.SMEM)
ANY = pl.BlockSpec(memory_space=pl.ANY)
MIB = 1 << 20
MESH = pl.DeviceIdType.MESH


def dot(a, b):
    return jnp.dot(a, b, preferred_element_type=F32)


def dot_nt(a, b):
    return lax.dot_general(a, b, (((1,), (1,)), ((), ())), preferred_element_type=F32)


def dot_tn(a, b):
    return lax.dot_general(a, b, (((0,), (0,)), ((), ())), preferred_element_type=F32)


def inv_rms(v):
    return lax.rsqrt(jnp.mean(v * v, axis=-1, keepdims=True) + EPS)


def rms_back(slope, normal, scale):
    return scale * (slope - normal * jnp.mean(slope * normal, axis=-1, keepdims=True))


def rotate(v, cosine, sine):
    middle = v.shape[-1] // 2
    a, b = v[..., :middle], v[..., middle:]
    return jnp.concatenate([a * cosine - b * sine, b * cosine + a * sine], axis=-1)


def shape_of(*shape, dtype=BF):
    return jax.ShapeDtypeStruct(shape, dtype)


def params(collective, mib):
    return pltpu.CompilerParams(collective_id=collective, has_side_effects=True, vmem_limit_bytes=mib * MIB)


class Group:
    def __init__(self, n_w, n_c):
        self.n_w, self.n_z, self.per = n_w, n_c // 2, n_w // 2
        c, w = lax.axis_index("ctx"), lax.axis_index("wt")
        self.core = lax.rem(c, 2)
        self.z, self.w, self.base = c // 2, w, c - self.core
        self.home = w // self.per
        self.at_home = self.core == self.home
        self.stream = w - self.home * self.per
        self.slot = self.stream * 2 + self.core

    def target(self, j):
        return {"ctx": self.base + self.home, "wt": j}

    def source(self, i):
        return {"ctx": self.base + lax.rem(i, 2), "wt": self.core * self.per + i // 2}

    def column(self, step):
        return {"ctx": 2 * lax.rem(self.z + step, self.n_z) + self.core, "wt": self.w}

    def greet(self, column):
        barrier = pltpu.get_barrier_semaphore()
        others = [
            {"ctx": self.base + lax.rem(self.core + q, 2), "wt": lax.rem(self.w + r, self.n_w)}
            for q in range(2)
            for r in range(self.n_w)
        ][1:]
        if column:
            others += [{"ctx": 2 * lax.rem(self.z + s, self.n_z) + q, "wt": self.w} for s in range(1, self.n_z) for q in range(2)]
        for there in others:
            pl.semaphore_signal(barrier, inc=1, device_id=there, device_id_type=MESH)
        pl.semaphore_wait(barrier, len(others))


class Moves:
    def __init__(self, group, send, recv):
        self.group, self.send, self.recv = group, send, recv

    def start(self, kind, src, dst, there, index, slot, here):
        remote = pltpu.make_async_remote_copy(
            src_ref=src, dst_ref=dst, send_sem=self.send.at[kind, index], recv_sem=self.recv.at[kind, slot],
            device_id=there, device_id_type=MESH,
        )
        local = pltpu.make_async_copy(src, dst, self.recv.at[kind, slot])
        pl.when(jnp.logical_not(here))(remote.start)
        pl.when(here)(local.start)

    def to_target(self, kind, j, src, dst):
        g = self.group
        self.start(kind, src, dst, g.target(j), j, g.slot, g.at_home & (g.w == j))

    def to_source(self, kind, i, src, dst):
        g = self.group
        self.start(kind, src, dst, g.source(i), i, g.w, g.at_home & (g.slot == i))

    def arrived(self, kind, index, dst):
        pltpu.make_async_copy(dst, dst, self.recv.at[kind, index]).wait()

    def sent(self, kind, src, by_target):
        g = self.group
        for i in range(g.n_w):
            at = src(i)
            copy = pltpu.make_async_remote_copy(
                src_ref=at, dst_ref=at, send_sem=self.send.at[kind, i], recv_sem=self.recv.at[kind, i],
                device_id=g.target(i) if by_target else g.source(i), device_id_type=MESH,
            )
            here = g.at_home & ((g.w if by_target else g.slot) == i)
            pl.when(jnp.logical_not(here))(copy.wait_send)


def column_copy(group, part, step, src, dst, send, recv):
    return pltpu.make_async_remote_copy(
        src_ref=src, dst_ref=dst, send_sem=send.at[part, step], recv_sem=recv.at[part, step],
        device_id=group.column(step), device_id_type=MESH,
    )


def exchange_kernel(n_w, split, *refs):
    count = len(split)
    ins, outs = refs[:count], refs[count : 2 * count]
    send, recv, local = refs[2 * count :]
    c, w = lax.axis_index("ctx"), lax.axis_index("wt")
    barrier = pltpu.get_barrier_semaphore()
    for step in range(1, n_w):
        pl.semaphore_signal(
            barrier, inc=1, device_id={"ctx": c, "wt": lax.rem(w + step, n_w)}, device_id_type=MESH
        )
    pl.semaphore_wait(barrier, n_w - 1)
    copies = []
    for a in range(count):
        for step in range(1, n_w):
            there = lax.rem(w + step, n_w)
            copies.append(
                pltpu.make_async_remote_copy(
                    src_ref=ins[a].at[there] if split[a] else ins[a], dst_ref=outs[a].at[w],
                    send_sem=send.at[a, step], recv_sem=recv.at[a, step],
                    device_id={"ctx": c, "wt": there}, device_id_type=MESH,
                )
            )
        copies.append(pltpu.make_async_copy(ins[a].at[w] if split[a] else ins[a], outs[a].at[w], local.at[a]))
    for copy in copies:
        copy.start()
    for copy in copies:
        copy.wait()


def exchange(arrays, split, n_w, collective):
    return pl.pallas_call(
        functools.partial(exchange_kernel, n_w, split),
        out_shape=[
            jax.ShapeDtypeStruct(v.shape if s else (n_w, *v.shape), v.dtype) for v, s in zip(arrays, split, strict=True)
        ],
        in_specs=[ANY] * len(arrays),
        out_specs=[ANY] * len(arrays),
        scratch_shapes=[
            pltpu.SemaphoreType.DMA((len(arrays), n_w)),
            pltpu.SemaphoreType.DMA((len(arrays), n_w)),
            pltpu.SemaphoreType.DMA((len(arrays),)),
        ],
        compiler_params=params(collective, 16),
    )(*arrays)


def first_kernel(
    n_w, n_c,
    x_ref, cot_ref, gain_ref, query_gain_ref, down_ref, key_ref, value_ref, cos_ref, sin_ref,
    h_out, x_out, r_out, latent_out, q_all, kv_all, cot_all,
    x_in, r_in, r_own, parts, low, q_own, kv_own, kv_column, send, recv, z_send, z_recv,
):
    g = Group(n_w, n_c)
    m = Moves(g, send, recv)
    tokens, cols = x_in.shape[1:]
    rank, depth = down_ref.shape[1], key_ref.shape[1]
    r_own[...] = jnp.broadcast_to(inv_rms(x_ref[...].astype(F32)), r_own.shape)
    g.greet(True)
    for j in range(n_w):
        m.to_target(0, j, x_ref.at[:, pl.ds(j * cols, cols)], x_in.at[g.slot])
        m.to_target(1, j, r_own, r_in.at[g.slot])

    for i in range(n_w):
        m.arrived(0, i, x_in.at[i])
        m.arrived(1, i, r_in.at[i])
        x_out[i] = x_in[i]
        r_out[i] = r_in[i]
        h = (x_in[i].astype(F32) * r_in[i, :, :1] * gain_ref[...]).astype(BF)
        h_out[i] = h
        parts[i, :, :rank] = dot(h, down_ref[...]).astype(BF)
        parts[i, :, rank : rank + depth] = dot(h, key_ref[...]).astype(BF)
        parts[i, :, rank + depth :] = dot(h, value_ref[...]).astype(BF)
        m.to_source(2, i, parts.at[i], low.at[g.w])

    for j in range(n_w):
        m.arrived(2, j, low.at[j])
    total = low[0].astype(F32)
    for j in range(1, n_w):
        total += low[j].astype(F32)
    keys = rotate(total[:, rank : rank + depth], cos_ref[...], sin_ref[...]).astype(BF)
    kv = jnp.concatenate([keys, total[:, rank + depth :].astype(BF)], axis=1)
    half = tokens // 2
    mirror = g.n_z - 1 - g.z
    for part in range(2):
        kv_own[part] = kv[part * half : (part + 1) * half]

    def over_z(part, step):
        return column_copy(
            g, part, step, kv_own.at[part], kv_column.at[part, mirror if part else g.z], z_send, z_recv
        )

    for step in range(1, g.n_z):
        for part in range(2):
            over_z(part, step).start()
    kv_column[0, g.z] = kv_own[0]
    kv_column[1, mirror] = kv_own[1]
    latent = total[:, :rank]
    latent_out[...] = latent
    q_own[...] = (latent * inv_rms(latent) * query_gain_ref[...]).astype(BF)
    for j in range(n_w):
        m.to_target(3, j, q_own, q_all.at[g.slot])
    for j in range(n_w):
        m.to_target(4, j, cot_ref, cot_all.at[g.slot])
    for step in range(1, g.n_z):
        for part in range(2):
            over_z(part, step).wait_recv()

    def kv_place(part):
        return kv_all.at[g.stream, part, :, 1 - g.core if part else g.core]

    for part in range(2):
        for j in range(n_w):
            m.to_target(5 + part, j, kv_column.at[part], kv_place(part))
    for i in range(n_w):
        m.arrived(3, i, q_all.at[i])
        m.arrived(4, i, cot_all.at[i])
        for part in range(2):
            m.arrived(5 + part, i, kv_all.at[i // 2, part, :, 1 - i % 2 if part else i % 2])
    m.sent(0, lambda j: x_ref.at[:, pl.ds(j * cols, cols)], True)
    m.sent(1, lambda j: r_own, True)
    m.sent(2, lambda i: parts.at[i], False)
    m.sent(3, lambda j: q_own, True)
    m.sent(4, lambda j: cot_ref, True)
    for part in range(2):
        m.sent(5 + part, lambda j: kv_column.at[part], True)
        for step in range(1, g.n_z):
            over_z(part, step).wait_send()


def first_part(n_w, n_c, x, cot, gain, query_gain, down, key, value, cosine, sine):
    tokens, width = x.shape
    cols, rank, depth = width // n_w, down.shape[1], key.shape[1]
    n_z, half, low = n_c // 2, tokens // 2, rank + 2 * depth
    return pl.pallas_call(
        functools.partial(first_kernel, n_w, n_c),
        out_shape=[
            shape_of(n_w, tokens, cols),
            shape_of(n_w, tokens, cols),
            shape_of(n_w, tokens, 128, dtype=F32),
            shape_of(tokens, rank, dtype=F32),
            shape_of(n_w, tokens, rank),
            shape_of(n_w // 2, 2, n_z, 2, half, 2 * depth),
            shape_of(n_w, tokens, width),
        ],
        in_specs=[VMEM, ANY] + [VMEM] * 7,
        out_specs=[VMEM] * 4 + [ANY] * 3,
        scratch_shapes=[
            pltpu.VMEM((n_w, tokens, cols), BF),
            pltpu.VMEM((n_w, tokens, 128), F32),
            pltpu.VMEM((tokens, 128), F32),
            pltpu.VMEM((n_w, tokens, low), BF),
            pltpu.VMEM((n_w, tokens, low), BF),
            pltpu.VMEM((tokens, rank), BF),
            pltpu.VMEM((2, half, 2 * depth), BF),
            pltpu.VMEM((2, n_z, half, 2 * depth), BF),
            pltpu.SemaphoreType.DMA((7, n_w)),
            pltpu.SemaphoreType.DMA((7, n_w)),
            pltpu.SemaphoreType.DMA((2, n_z)),
            pltpu.SemaphoreType.DMA((2, n_z)),
        ],
        compiler_params=params(1, 40),
    )(x, cot, gain, query_gain, down, key, value, cosine, sine)


def visible_keys(bounds_ref, stream, c, tokens, seqlen):
    half = tokens // 2
    row = lax.broadcasted_iota(jnp.int32, (tokens, 1), 0)
    pos = row + jnp.where(row < half, c * half, seqlen - (c + 1) * half - half)
    begin = jnp.zeros((tokens, 1), jnp.int32)
    for j in range(bounds_ref.shape[1]):
        start = bounds_ref[stream, j]
        begin = jnp.where(pos >= start, jnp.maximum(begin, start), begin)
    key = lax.broadcasted_iota(jnp.int32, (tokens, seqlen), 1)
    return (key >= begin) & (key <= pos)


def probabilities(q, keys, visible):
    scores = jnp.where(visible, dot_nt(q, keys), NEG)
    peak = jnp.max(scores, axis=-1, keepdims=True)
    weight = jnp.where(visible, jnp.exp(scores - peak), 0.0)
    return weight * (1.0 / jnp.sum(weight, axis=-1, keepdims=True))


def attend_kernel(
    n_w, n_c,
    bounds_ref, q_ref, up_ref, kv_ref, cos_ref, sin_ref, out_ref, x_ref, gain_ref,
    queries, attn, resid, h_all,
    parts, land, h_own, send, recv,
):
    g = Group(n_w, n_c)
    m = Moves(g, send, recv)
    tokens, seqlen, depth = q_ref.shape[1], kv_ref.shape[1], kv_ref.shape[2] // 2
    scale = 1.0 / math.sqrt(depth)
    g.greet(False)

    def one(i, carry):
        stream, core = i // 2, lax.rem(i, 2)
        visible = visible_keys(bounds_ref, g.core * g.per + stream, g.base + core, tokens, seqlen)
        raw = dot(q_ref[i], up_ref[...])
        for cut in range(0, up_ref.shape[1], depth):
            span = slice(cut, cut + depth)
            q = (rotate(raw[:, span], cos_ref[core], sin_ref[core]) * scale).astype(BF)
            queries[i, :, span] = q
            probs = probabilities(q, kv_ref[stream, :, :depth], visible).astype(BF)
            attn[i, :, span] = dot(probs, kv_ref[stream, :, depth:]).astype(BF)
        parts[i] = dot(attn[i], out_ref[...]).astype(BF)
        m.to_source(0, i, parts.at[i], land.at[g.w])
        return carry

    lax.fori_loop(0, n_w, one, 0)
    total = x_ref[...].astype(F32)
    for j in range(n_w):
        m.arrived(0, j, land.at[j])
        total += land[j].astype(F32)
    resid[...] = total
    h_own[...] = (total * inv_rms(total) * gain_ref[...]).astype(BF)
    for j in range(n_w):
        m.to_target(1, j, h_own, h_all.at[g.slot])
    for i in range(n_w):
        m.arrived(1, i, h_all.at[i])
    m.sent(0, lambda i: parts.at[i], False)
    m.sent(1, lambda j: h_own, True)


def attend_part(n_w, n_c, bounds, q_all, up_cols, kv, cosine, sine, output, x, gain):
    tokens, width = x.shape
    features = up_cols.shape[1]
    return pl.pallas_call(
        functools.partial(attend_kernel, n_w, n_c),
        out_shape=[
            shape_of(n_w, tokens, features),
            shape_of(n_w, tokens, features),
            shape_of(tokens, width, dtype=F32),
            shape_of(n_w, tokens, width),
        ],
        in_specs=[SMEM] + [VMEM] * 8,
        out_specs=[VMEM] * 3 + [ANY],
        scratch_shapes=[
            pltpu.VMEM((n_w, tokens, width), BF),
            pltpu.VMEM((n_w, tokens, width), BF),
            pltpu.VMEM((tokens, width), BF),
            pltpu.SemaphoreType.DMA((2, n_w)),
            pltpu.SemaphoreType.DMA((2, n_w)),
        ],
        compiler_params=params(2, 50),
    )(bounds, q_all, up_cols, kv, cosine, sine, output, x, gain)


class Plan:
    def __init__(self, shapes, turned, n_w, slots, limit):
        self.n_w, self.arrays, self.turned = n_w, shapes, turned
        self.wide = all(cols % 128 == 0 for (_, cols), turn in zip(shapes, turned, strict=True) if turn)
        self.shaped, self.pieces, self.members, self.ring_shapes = [], [], [[], []], [None, None]
        for (rows, cols), turn in zip(shapes, turned, strict=True):
            self.shaped.append((n_w, 2, 2, rows // n_w // 4, cols) if turn else (2, 2, rows // 4, cols))
        for kind in range(2):
            mine = [v for v, turn in zip(self.shaped, turned, strict=True) if turn == bool(kind)]
            if mine:
                lead, cols = (n_w, 2) if kind else (2,), max(v[-1] for v in mine)
                rows = 16
                common = math.gcd(*(v[-2] for v in mine))
                for more in range(16, common + 1, 16):
                    if common % more == 0 and math.prod(lead) * more * cols * 2 <= limit:
                        rows = more
                self.ring_shapes[kind] = (*lead, rows, cols)
        for a, (v, turn) in enumerate(zip(self.shaped, turned, strict=True)):
            rows = self.ring_shapes[int(turn)][-2]
            for row in range(0, v[-2], rows):
                self.members[int(turn)].append(len(self.pieces))
                self.pieces.append((a, int(turn), len(self.members[int(turn)]) - 1, row, rows, v[-1]))
        self.slots = [min(slots, len(members)) for members in self.members]

    def __len__(self):
        return len(self.pieces)

    def slot(self, q):
        return self.pieces[q][2] % self.slots[self.pieces[q][1]]

    def before(self, q):
        _, kind, index = self.pieces[q][:3]
        return self.members[kind][index - self.slots[kind]] if index >= self.slots[kind] else None

    def after(self, q):
        _, kind, index = self.pieces[q][:3]
        later = index + self.slots[kind]
        return self.members[kind][later] if later < len(self.members[kind]) else None

    def scratch(self):
        shapes = [v or (16, 128) for v in self.ring_shapes]
        slots = [max(v, 1) for v in self.slots]
        rings = [pltpu.VMEM((n, *v), BF) for n, v in zip(slots, shapes, strict=True)]
        rows, turned = shapes
        halves = [pltpu.VMEM((slots[0], *rows[-2:]), BF), pltpu.VMEM((slots[1], self.n_w, *turned[-2:]), BF)]
        moved = (turned[-2], self.n_w * turned[-1]) if self.wide else (self.n_w, *turned[-2:])
        kinds, count = 5 + self.n_w, len(self)
        return [
            *rings, *rings, *rings, *halves, pltpu.VMEM((slots[1], *moved), BF),
            pltpu.SemaphoreType.DMA((count,)),
            pltpu.SemaphoreType.DMA((count,)),
            pltpu.SemaphoreType.DMA((kinds, count)),
            pltpu.SemaphoreType.DMA((kinds, count)),
            pltpu.SemaphoreType.REGULAR((4, count)),
        ]

    def out_shapes(self):
        return [
            shape_of(2, 2, v[-2], self.n_w * v[-1]) if turn and self.wide else shape_of(*v)
            for v, turn in zip(self.shaped, self.turned, strict=True)
        ]

    def row_shards(self, sums):
        done = []
        for s, (rows, cols), turn in zip(sums, self.arrays, self.turned, strict=True):
            if self.wide or not turn:
                done.append(s.reshape(-1, s.shape[-1]))
            else:
                done.append(s.reshape(self.n_w, rows // self.n_w, cols).swapaxes(0, 1).reshape(rows // self.n_w, -1))
        return done


CHAIN_SCRATCH = 14


class Chain:
    AHEAD, LAG = 2, 8

    def __init__(self, plan, n_c, terms, outs, scratch):
        self.plan, self.n_w, self.terms, self.outs = plan, plan.n_w, terms, outs
        self.own, self.mates, self.ups, self.halves = (scratch[2 * i : 2 * i + 2] for i in range(4))
        self.moved, self.load, self.place, self.send, self.recv, self.credit = scratch[8:]
        c, w = lax.axis_index("ctx"), lax.axis_index("wt")
        chain, k = n_c // 2, c // 2
        self.w, self.core = w, lax.rem(c, 2)
        left = k < chain // 2
        self.side = jnp.where(left, 0, 1)
        far = jnp.where(left, k, chain - 1 - k)
        self.middle, self.outside = far == chain // 2 - 1, far > 0
        self.mate = {"ctx": c + 1 - 2 * self.core, "wt": w}
        self.inner = {"ctx": jnp.where(left, c + 2, c - 2), "wt": w}
        self.outer = {"ctx": jnp.where(left, c - 2, c + 2), "wt": w}
        self.peers = [{"ctx": c, "wt": lax.rem(w + r, self.n_w)} for r in range(1, self.n_w)]
        self.now, self.ready = 0, len(plan)

    def turned(self, q):
        return self.plan.turned[self.plan.pieces[q][0]]

    def every(self, q):
        return (slice(None),) if self.turned(q) else ()

    def term(self, q, core):
        a, _, _, row, rows, _ = self.plan.pieces[q]
        return self.terms[a].at[(*self.every(q), core, slice(None), pl.ds(row, rows))]

    def fitting(self, q, buffer):
        cols = self.plan.pieces[q][5]
        lead = (slice(None),) * (len(buffer.shape) - 2)
        return buffer.at[(self.plan.slot(q), *lead, pl.ds(0, cols))]

    def ring(self, q, buffers):
        return self.fitting(q, buffers[self.plan.pieces[q][1]])

    def half_buffer(self, q):
        return self.ring(q, self.halves)

    def remote(self, kind, q, src, dst, there):
        return pltpu.make_async_remote_copy(
            src_ref=src, dst_ref=dst, send_sem=self.send.at[kind, q], recv_sem=self.recv.at[kind, q], device_id=there,
            device_id_type=MESH,
        )

    def own_load(self, q):
        return pltpu.make_async_copy(self.term(q, self.core), self.ring(q, self.own), self.load.at[q])

    def to_mate(self, q):
        return self.remote(0, q, self.term(q, 1 - self.core), self.ring(q, self.mates), self.mate)

    def along(self, q, there):
        return self.remote(1, q, self.ring(q, self.own), self.ring(q, self.ups), there)

    def to_across(self, q):
        side = self.ring(q, self.own).at[(*self.every(q), 1 - self.side)]
        return self.remote(5, q, side, self.half_buffer(q), self.inner)

    def moved_part(self, q, source):
        cols = self.plan.pieces[q][5]
        if not self.plan.wide:
            return self.moved.at[self.plan.slot(q), source, :, pl.ds(0, cols)]
        return self.moved.at[self.plan.slot(q), :, pl.ds(pl.multiple_of(source * cols, 128), cols)]

    def to_peer(self, q, r, slot):
        there = self.peers[r]
        return self.remote(6 + r, q, self.half_buffer(q).at[there["wt"]], self.moved_part(q, slot), there)

    def finished(self, q):
        if not self.turned(q):
            return self.half_buffer(q)
        if self.plan.wide:
            return self.moved.at[self.plan.slot(q), :, pl.ds(0, self.n_w * self.plan.pieces[q][5])]
        return self.fitting(q, self.moved)

    def result(self, q, *lead):
        a, kind, _, row, rows, _ = self.plan.pieces[q]
        every = () if self.plan.wide else self.every(q)
        return self.outs[a].at[(*every, *lead, pl.ds(row, rows))]

    def half_place(self, q):
        return pltpu.make_async_copy(self.finished(q), self.result(q, self.core, self.side), self.place.at[q])

    def half_across(self, q, side):
        return self.remote(2, q, self.finished(q), self.result(q, self.core, side), self.inner)

    def down(self, kind, q, there):
        here = self.result(q, self.core, slice(None))
        return self.remote(kind, q, here, here, there)

    def add(self, q, ins, out):
        rows = out.shape[-2]
        step = 16 if rows % 16 == 0 else rows
        lead = (slice(None),) * (len(out.shape) - 2)

        def body(i, carry):
            at = (*lead, pl.ds(i * step, step))
            total = ins[0][at].astype(F32)
            for ref in ins[1:]:
                total += ref[at].astype(F32)
            out[at] = total.astype(BF)
            return carry

        lax.fori_loop(0, rows // step, body, 0)

    def grant(self, kind, q, there):
        pl.semaphore_signal(self.credit.at[kind, q], inc=1, device_id=there, device_id_type=MESH)

    def prefetch(self, q):
        before = self.plan.before(q)
        if before is not None:
            pl.when(self.middle)(self.to_across(before).wait_send)
            pl.when(jnp.logical_not(self.middle))(self.along(before, self.inner).wait_send)
            pl.semaphore_wait(self.credit.at[0, q], 1)
        self.own_load(q).start()
        self.to_mate(q).start()

    def up(self, q):
        self.own_load(q).wait()
        self.to_mate(q).wait_recv()
        after, before = self.plan.after(q), self.plan.before(q)
        own, mates, ups = (self.ring(q, b) for b in (self.own, self.mates, self.ups))

        @pl.when(self.outside)
        def _():
            self.along(q, self.outer).wait_recv()
            self.add(q, [own, mates, ups], own)
            if after is not None:
                self.grant(1, after, self.outer)

        @pl.when(jnp.logical_not(self.outside))
        def _():
            self.add(q, [own, mates], own)

        if after is not None:
            self.grant(0, after, self.mate)

        @pl.when(self.middle)
        def _():
            if before is not None:
                pl.semaphore_wait(self.credit.at[2, q], 1)
            self.to_across(q).start()

        @pl.when(jnp.logical_not(self.middle))
        def _():
            if before is not None:
                pl.semaphore_wait(self.credit.at[1, q], 1)
            self.along(q, self.inner).start()

    def finish_half(self, q):
        self.to_across(q).wait_recv()
        half = self.half_buffer(q)
        self.add(q, [self.ring(q, self.own).at[(*self.every(q), self.side)], half], half)
        if self.turned(q):
            if self.plan.before(q) is not None:
                pl.semaphore_wait(self.credit.at[3, q], self.n_w - 1)
            for r in range(self.n_w - 1):
                self.to_peer(q, r, self.w).start()
            self.moved_part(q, self.w)[...] = half[self.w]
        else:
            self.spread(q)

    def spread(self, q):
        self.half_place(q).start()
        self.half_across(q, self.side).start()

    def move(self, q):
        if self.turned(q):
            for r in range(self.n_w - 1):
                self.to_peer(q, r, lax.rem(self.w + self.n_w - r - 1, self.n_w)).wait_recv()
            self.spread(q)

    def pass_down(self, q):
        pl.when(self.outside)(self.down(3, q, self.outer).start)
        self.down(4, q, self.mate).start()

    def free(self, q):
        after = self.plan.after(q)
        if after is not None:
            self.half_across(q, self.side).wait_send()
            if self.turned(q):
                for r in range(self.n_w - 1):
                    self.to_peer(q, r, self.w).wait_send()
                for there in self.peers:
                    self.grant(3, after, there)
            self.grant(2, after, self.inner)

    def tick(self):
        t, count = self.now, len(self.plan)
        self.now += 1
        if t == 0:
            for q in range(min(self.AHEAD, count)):
                self.prefetch(q)
        if t < count:
            self.up(t)

        @pl.when(self.middle)
        def _():
            if 0 <= t - 1 < count:
                self.finish_half(t - 1)
            if 0 <= t - 2 < count:
                self.move(t - 2)
            if 0 <= t - 3 < count:
                self.half_place(t - 3).wait()
                self.half_across(t - 3, 1 - self.side).wait_recv()
                self.pass_down(t - 3)
                self.free(t - 3)

        if 0 <= t - self.LAG < count:

            @pl.when(jnp.logical_not(self.middle))
            def _():
                self.down(3, t - self.LAG, self.inner).wait_recv()
                self.pass_down(t - self.LAG)

        if self.AHEAD <= t + self.AHEAD < count:
            self.prefetch(t + self.AHEAD)

    def ticks(self, number):
        for _ in range(number):
            if self.now + self.AHEAD < self.ready or self.now < len(self.plan) + self.LAG and self.ready == len(self.plan):
                self.tick()

    def have(self, arrays):
        self.ready = sum(piece[0] < arrays for piece in self.plan.pieces)

    def finish(self):
        self.ticks(len(self.plan) + self.LAG)
        for q in range(len(self.plan)):
            last = self.plan.after(q) is None

            @pl.when(self.middle)
            def _():
                if last:
                    self.to_across(q).wait_send()
                    self.half_across(q, self.side).wait_send()
                    for r in range(self.n_w - 1 if self.turned(q) else 0):
                        self.to_peer(q, r, self.w).wait_send()

            if last:
                pl.when(jnp.logical_not(self.middle))(self.along(q, self.inner).wait_send)
            self.to_mate(q).wait_send()
            pl.when(self.outside)(self.down(3, q, self.outer).wait_send)
            other = self.result(q, 1 - self.core, slice(None))
            self.remote(4, q, other, other, self.mate).wait_recv()
            self.down(4, q, self.mate).wait_send()


class Small:
    def __init__(self, group, n_c, moves, terms, first_terms, layer_terms, resid, out, layer_out, layer_land, scratch):
        self.g, self.n_c, self.m = group, n_c, moves
        self.terms, self.first_terms, self.layer_terms, self.resid = terms, first_terms, layer_terms, resid
        self.out, self.layer_out, self.layer_land = out, layer_out, layer_land
        self.land, self.own, self.all, self.send, self.recv = scratch
        self.c = lax.axis_index("ctx")

    def block(self, step):
        n_w, j = self.g.n_w, lax.rem(self.g.w + step, self.g.n_w)
        return pltpu.make_async_remote_copy(
            src_ref=self.terms.at[j], dst_ref=self.land.at[step], send_sem=self.send.at[step],
            recv_sem=self.recv.at[step], device_id={"ctx": self.c, "wt": j}, device_id_type=MESH,
        )

    def total(self, step):
        at = self.g.n_w + step
        return pltpu.make_async_remote_copy(
            src_ref=self.own, dst_ref=self.all.at[step], send_sem=self.send.at[at], recv_sem=self.recv.at[at],
            device_id={"ctx": lax.rem(self.c + step, self.n_c), "wt": self.g.w}, device_id_type=MESH,
        )

    def begin(self):
        for step in range(1, self.g.n_w):
            self.block(step).start()
        for i in range(self.g.n_w):
            self.m.to_source(0, i, self.layer_terms.at[i], self.layer_land.at[self.g.w])

    def middle(self):
        first = self.first_terms.shape[1]
        total = self.terms[self.g.w]
        for step in range(1, self.g.n_w):
            self.block(step).wait_recv()
            total += self.land[step]
        self.own[:, :first] = self.first_terms[...]
        self.own[:, first:] = total
        for step in range(1, self.n_c):
            self.total(step).start()
        total = self.resid[...]
        for j in range(self.g.n_w):
            self.m.arrived(0, j, self.layer_land.at[j])
            total += self.layer_land[j].astype(F32)
        self.layer_out[...] = total.astype(BF)

    def end(self):
        total = self.own[...]
        for step in range(1, self.n_c):
            self.total(step).wait_recv()
            total += self.all[step]
        self.out[...] = total
        for step in range(1, self.g.n_w):
            self.block(step).wait_send()
        for step in range(1, self.n_c):
            self.total(step).wait_send()
        self.m.sent(0, lambda i: self.layer_terms.at[i], False)


SMALL_SCRATCH = 5


def small_scratch(n_w, n_c, width, first):
    return [
        pltpu.VMEM((n_w, 8, width), F32),
        pltpu.VMEM((8, width + first), F32),
        pltpu.VMEM((n_c, 8, width + first), F32),
        pltpu.SemaphoreType.DMA((n_w + n_c,)),
        pltpu.SemaphoreType.DMA((n_w + n_c,)),
    ]


def sum_kernel(plan, n_c, *refs):
    count = len(plan.arrays)
    terms, (gain_terms, first_terms, layer_terms, resid_ref), refs = refs[:count], refs[count : count + 4], refs[count + 4 :]
    outs, (gains_out, layer_out), refs = refs[:count], refs[count : count + 2], refs[count + 2 :]
    layer_land, group_send, group_recv = refs[CHAIN_SCRATCH + SMALL_SCRATCH :]
    g = Group(plan.n_w, n_c)
    chain = Chain(plan, n_c, terms, outs, refs[:CHAIN_SCRATCH])
    small = Small(
        g, n_c, Moves(g, group_send, group_recv), gain_terms, first_terms, layer_terms, resid_ref, gains_out, layer_out,
        layer_land, refs[CHAIN_SCRATCH : CHAIN_SCRATCH + SMALL_SCRATCH],
    )
    g.greet(True)
    chain.ticks(2)
    small.begin()
    chain.ticks(4)
    small.middle()
    chain.finish()
    small.end()


def sum_over_ctx(plan, terms, n_c, collective, gain_terms, first_terms, layer_terms, resid):
    n_w, count = plan.n_w, len(plan.arrays)
    width, first = gain_terms.shape[-1], first_terms.shape[-1]
    sums = pl.pallas_call(
        functools.partial(sum_kernel, plan, n_c),
        out_shape=[*plan.out_shapes(), shape_of(8, width + first, dtype=F32), shape_of(*resid.shape)],
        in_specs=[ANY] * count + [VMEM, VMEM, ANY, VMEM],
        out_specs=[ANY] * count + [VMEM, VMEM],
        scratch_shapes=[
            *plan.scratch(),
            *small_scratch(n_w, n_c, width, first),
            pltpu.VMEM(layer_terms.shape, BF),
            pltpu.SemaphoreType.DMA((1, n_w)),
            pltpu.SemaphoreType.DMA((1, n_w)),
        ],
        compiler_params=params(collective, 60),
    )(*(v.reshape(s) for v, s in zip(terms, plan.shaped, strict=True)), gain_terms, first_terms, layer_terms, resid)
    return plan.row_shards(sums[:count]), sums[-2], sums[-1]


def norm_back(g, m, feed_ref, resid_ref, gain_ref, cot_ref, land, proj_own, proj_in, d_resid, d_gain, ticks):
    for i in range(g.n_w):
        m.to_source(0, i, feed_ref.at[i], land.at[g.w])
    ticks(3)
    for j in range(g.n_w):
        m.arrived(0, j, land.at[j])
    d_h = land[0].astype(F32)
    for j in range(1, g.n_w):
        d_h += land[j].astype(F32)
    resid = resid_ref[...]
    scale = inv_rms(resid)
    normal = resid * scale
    d_gain[...] = jnp.broadcast_to(jnp.sum(d_h * normal, axis=0, keepdims=True), d_gain.shape)
    total = cot_ref[...].astype(F32) + rms_back(d_h * gain_ref[...], normal, scale)
    d_resid[...] = total
    proj_own[...] = total.astype(BF)
    for j in range(g.n_w):
        m.to_target(1, j, proj_own, proj_in.at[g.slot])
    ticks(3)
    for i in range(g.n_w):
        m.arrived(1, i, proj_in.at[i])


def norm_back_ends(m, feed_ref, proj_own):
    m.sent(0, lambda i: feed_ref.at[i], False)
    m.sent(1, lambda j: proj_own, True)


NORM_SEMAPHORES, BACK_SEMAPHORES = 2, 6


def norm_back_kernel(
    n_w, n_c, feed_ref, resid_ref, gain_ref, cot_ref, proj_all, d_resid, d_gain, land, proj_own, send, recv
):
    g = Group(n_w, n_c)
    m = Moves(g, send, recv)
    g.greet(False)
    norm_back(g, m, feed_ref, resid_ref, gain_ref, cot_ref, land, proj_own, proj_all, d_resid, d_gain, lambda n: None)
    norm_back_ends(m, feed_ref, proj_own)


def attend_back(
    g, m,
    bounds_ref, proj_ref, d_resid_ref, out_ref, queries_ref, kv_ref, cos_ref, sin_ref, up_ref, latent_ref,
    query_gain_ref, down_ref, key_ref, value_ref, x_in_ref, r_in_ref, gain_ref, x_ref,
    d_q_out, low_out, slope_out, d_query_gain, d_gain,
    d_kv, kv_parts, kv_land, kv_column, kv_z, q_parts, q_land,
    low_own, low_in, n_parts, n_land, z_send, z_recv, out_sem, work,
):
    tokens, seqlen, depth = x_ref.shape[0], kv_ref.shape[1], kv_ref.shape[2] // 2
    rank, half, cols = down_ref.shape[1], tokens // 2, x_in_ref.shape[2]
    n_w = g.n_w
    mirror = g.n_z - 1 - g.z
    scale = 1.0 / math.sqrt(depth)

    def kv_part(stream, core, part):
        return kv_parts.at[stream, part, :, 1 - core if part else core]

    def one_stream(stream):
        d_kv[...] = jnp.zeros_like(d_kv)
        for core in range(2):
            i = 2 * stream + core
            visible = visible_keys(bounds_ref, g.core * g.per + stream, g.base + core, tokens, seqlen)
            slopes = dot_nt(proj_ref[i], out_ref[...]).astype(BF)
            d_keys = jnp.zeros((seqlen, depth), F32)
            d_values = jnp.zeros((seqlen, depth), F32)
            for cut in range(0, up_ref.shape[1], depth):
                span = slice(cut, cut + depth)
                q, slope = queries_ref[i, :, span], slopes[:, span]
                probs = probabilities(q, kv_ref[stream, :, :depth], visible)
                d_probs = dot_nt(slope, kv_ref[stream, :, depth:])
                delta = jnp.sum(probs * d_probs, axis=-1, keepdims=True)
                d_scores = (probs * (d_probs - delta)).astype(BF)
                d_q = dot(d_scores, kv_ref[stream, :, :depth])
                d_q_out[i, :, span] = (rotate(d_q, cos_ref[core], -sin_ref[core]) * scale).astype(BF)
                d_keys += dot_tn(d_scores, q)
                d_values += dot_tn(probs.astype(BF), slope)
            shaped = (2, g.n_z, 2, half, depth)
            d_kv[:, :, :, :, :depth] += d_keys.reshape(shaped)
            d_kv[:, :, :, :, depth:] += d_values.reshape(shaped)
            q_parts[i] = dot_nt(d_q_out[i], up_ref[...]).astype(BF)
            m.to_source(0, i, q_parts.at[i], q_land.at[g.w])
            work.ticks(2)
        kv_parts[stream] = d_kv[...].astype(BF)
        for core in range(2):
            for part in range(2):
                m.to_source(1 + part, 2 * stream + core, kv_part(stream, core, part), kv_land.at[g.w, part])

    if n_w <= 4:
        for stream in range(g.per):
            one_stream(stream)
    else:
        lax.fori_loop(0, g.per, lambda stream, carry: (one_stream(stream), carry)[1], 0)
    work.after_attention(d_q_out)
    for j in range(n_w):
        m.arrived(0, j, q_land.at[j])
    d_n = q_land[0].astype(F32)
    for j in range(1, n_w):
        d_n += q_land[j].astype(F32)
    latent = latent_ref[...]
    r_query = inv_rms(latent)
    n_query = latent * r_query
    d_query_gain[...] = jnp.broadcast_to(jnp.sum(d_n * n_query, axis=0, keepdims=True), d_query_gain.shape)
    low_own[:, :rank] = rms_back(d_n * query_gain_ref[...], n_query, r_query).astype(BF)
    lead = pl.ds(0, rank)
    for j in range(n_w):
        m.to_target(3, j, low_own.at[:, lead], low_in.at[g.slot, :, lead])
    work.ticks(2)

    for j in range(n_w):
        for part in range(2):
            m.arrived(1 + part, j, kv_land.at[j, part])
    total = kv_land[0].astype(F32)
    for j in range(1, n_w):
        total += kv_land[j].astype(F32)
    kv_column[...] = total.astype(BF)

    def over_z(part, step):
        z = lax.rem(g.z + step, g.n_z)
        return column_copy(
            g, part, step, kv_column.at[part, g.n_z - 1 - z if part else z], kv_z.at[step, part], z_send, z_recv
        )

    for step in range(1, g.n_z):
        for part in range(2):
            over_z(part, step).start()
    work.ticks(2)
    own = [kv_column[0, g.z].astype(F32), kv_column[1, mirror].astype(F32)]
    for step in range(1, g.n_z):
        for part in range(2):
            over_z(part, step).wait_recv()
            own[part] += kv_z[step, part].astype(F32)
    own = jnp.concatenate(own, axis=0)
    low_own[:, rank : rank + depth] = rotate(own[:, :depth], cos_ref[g.core], -sin_ref[g.core]).astype(BF)
    low_own[:, rank + depth :] = own[:, depth:].astype(BF)
    tail = pl.ds(rank, 2 * depth)
    for j in range(n_w):
        m.to_target(4, j, low_own.at[:, tail], low_in.at[g.slot, :, tail])

    d_first = jnp.zeros((1, cols), F32)
    for i in range(n_w):
        m.arrived(3, i, low_in.at[i, :, lead])
        d_h = dot_nt(low_in[i, :, :rank], down_ref[...])
        m.arrived(4, i, low_in.at[i, :, tail])
        d_h += dot_nt(low_in[i, :, rank : rank + depth], key_ref[...])
        d_h += dot_nt(low_in[i, :, rank + depth :], value_ref[...])
        normal = x_in_ref[i].astype(F32) * r_in_ref[i, :, :1]
        d_first += jnp.sum(d_h * normal, axis=0, keepdims=True)
        n_parts[i] = (d_h * gain_ref[...]).astype(BF)
        m.to_source(5, i, n_parts.at[i], n_land.at[g.w])
    d_gain[...] = jnp.broadcast_to(d_first, d_gain.shape)
    work.after_low(low_in, low_out, out_sem)
    for j in range(n_w):
        m.arrived(5, j, n_land.at[j])
    d_n = jnp.concatenate([n_land[j].astype(F32) for j in range(n_w)], axis=1)
    x = x_ref[...].astype(F32)
    r_first = inv_rms(x)
    slope_out[...] = (d_resid_ref[...] + rms_back(d_n, x * r_first, r_first)).astype(BF)

    work.at_end(low_in, low_out, out_sem)
    m.sent(0, lambda i: q_parts.at[i], False)
    m.sent(3, lambda j: low_own.at[:, lead], True)
    m.sent(4, lambda j: low_own.at[:, tail], True)
    m.sent(5, lambda i: n_parts.at[i], False)
    for part in range(2):
        m.sent(1 + part, lambda i: kv_part(i // 2, i % 2, part), False)
        for step in range(1, g.n_z):
            over_z(part, step).wait_send()


class Alone:
    def ticks(self, number):
        pass

    def after_attention(self, d_q):
        pass

    def after_low(self, low_in, low_out, sem):
        pltpu.make_async_copy(low_in, low_out, sem.at[0]).start()

    def at_end(self, low_in, low_out, sem):
        pltpu.make_async_copy(low_in, low_out, sem.at[0]).wait()


class Products:
    TILE = 512

    def __init__(self, chain, first, attn, proj, q_all, h_cols, stages, sems):
        self.chain, self.ticks, self.first = chain, chain.ticks, first
        self.attn, self.proj, self.q_all, self.h_cols = attn, proj, q_all, h_cols
        self.stages, self.sems = stages, sems

    def product(self, which, left, right, ticks):
        terms, stage = self.chain.terms[self.first + which], self.stages[which]
        cols, lead = terms.shape[-1], (slice(None),) * (len(terms.shape) - 1)
        tile = stage.shape[-1]
        rows = left.shape[0]

        def out(at):
            return pltpu.make_async_copy(stage, terms.at[(*lead, pl.ds(at, tile))], self.sems.at[which])

        for at in range(0, cols, tile):
            made = dot_tn(left[...], right[:, :, at : at + tile].reshape(rows, tile)).astype(BF)
            if at > 0:
                out(at - tile).wait()
            stage[...] = made.reshape(stage.shape)
            out(at).start()
            if at % (2 * tile) == 0:
                self.ticks(ticks)
        out(cols - tile).wait()
        self.chain.have(self.first + which + 1)

    def after_attention(self, d_q):
        self.product(0, self.attn, self.proj, 1)
        self.product(1, self.q_all, d_q, 1)

    def after_low(self, low_in, low_out, sem):
        self.product(2, self.h_cols, low_in, 1)

    def at_end(self, low_in, low_out, sem):
        pass


def attend_back_kernel(n_w, n_c, *refs):
    *refs, send, recv, z_send, z_recv, out_sem = refs
    g = Group(n_w, n_c)
    g.greet(True)
    attend_back(g, Moves(g, send, recv), *refs, z_send, z_recv, out_sem, Alone())


def late_kernel(n_w, n_c, plan, *refs):
    bounds_ref, feed_ref, resid_ref, gain_ref, cot_ref, *refs = refs
    rest, (layer_terms, attn, q_all, h_cols), given, refs = refs[:15], refs[15:19], refs[19:22], refs[22:]
    count = len(plan.arrays)
    sums, made, (d_q_out, slope_out, gains_out, layer_out), refs = (
        refs[:count], refs[count : count + 3], refs[count + 3 : count + 7], refs[count + 7 :]
    )
    chain_scratch, small_refs, refs = (
        refs[:CHAIN_SCRATCH], refs[CHAIN_SCRATCH : CHAIN_SCRATCH + SMALL_SCRATCH], refs[CHAIN_SCRATCH + SMALL_SCRATCH :]
    )
    land, proj_own, proj_in, d_resid, gain_terms, first_terms, norm_gain, query_gain, *refs = refs
    *stages, product_sems, small_send, small_recv, norm_send, norm_recv = refs[:8]
    *back_scratch, send, recv, z_send, z_recv, out_sem = refs[8:]
    g = Group(n_w, n_c)
    norm_moves = Moves(g, norm_send, norm_recv)
    chain = Chain(plan, n_c, [*given, *made], sums, chain_scratch)
    chain.have(3)
    work = Products(chain, 3, attn, proj_in, q_all, h_cols, stages, product_sems)
    g.greet(True)
    norm_back(g, norm_moves, feed_ref, resid_ref, gain_ref, cot_ref, land, proj_own, proj_in, d_resid, norm_gain, chain.ticks)
    attend_back(
        g, Moves(g, send, recv), bounds_ref, proj_in, d_resid, *rest, d_q_out, None, slope_out, query_gain, first_terms,
        *back_scratch, z_send, z_recv, out_sem, work,
    )
    width, rank = norm_gain.shape[1] // n_w, query_gain.shape[1] // n_w
    for j in range(n_w):
        gain_terms[j, :, :width] = norm_gain[:, j * width : (j + 1) * width]
        gain_terms[j, :, width:] = query_gain[:, j * rank : (j + 1) * rank]
    small = Small(
        g, n_c, Moves(g, small_send, small_recv), gain_terms, first_terms, layer_terms, resid_ref, gains_out, layer_out,
        land, small_refs,
    )
    small.begin()
    chain.ticks(4)
    small.middle()
    chain.finish()
    small.end()
    norm_back_ends(norm_moves, feed_ref, proj_own)


def bytes_of(shapes):
    return sum(math.prod(v.shape) * jnp.dtype(v.dtype).itemsize for v in shapes)


def late_part(n_w, n_c, shapes, turned, bounds, late, rest, out_part, given, attn, q_all, h_cols):
    feed, resid, gain, cot = late
    kv, up_cols, x = rest[2], rest[5], rest[14]
    (tokens, width), (rank, features) = x.shape, up_cols.shape
    per, seqlen, both = kv.shape
    n_z, half, cols, low = n_c // 2, tokens // 2, width // n_w, rank + both
    plan = Plan(shapes, turned, n_w, 6, 380_000)
    proj, d_q, slope = shape_of(n_w, tokens, width), shape_of(n_w, tokens, features), shape_of(tokens, width)
    d_resid, norm_gain = shape_of(tokens, width, dtype=F32), shape_of(8, width, dtype=F32)
    query_gain, first_gain = shape_of(8, rank, dtype=F32), shape_of(8, cols, dtype=F32)
    norm_scratch = [pltpu.VMEM((n_w, tokens, width), BF), pltpu.VMEM((tokens, width), BF)]
    norm_semaphores = [pltpu.SemaphoreType.DMA((NORM_SEMAPHORES, n_w))] * 2
    back_scratch = [
        pltpu.VMEM((2, n_z, 2, half, both), F32),
        pltpu.VMEM((per, 2, n_z, 2, half, both), BF),
        pltpu.VMEM((n_w, 2, n_z, half, both), BF),
        pltpu.VMEM((2, n_z, half, both), BF),
        pltpu.VMEM((n_z, 2, half, both), BF),
        pltpu.VMEM((n_w, tokens, rank), BF),
        pltpu.VMEM((n_w, tokens, rank), BF),
        pltpu.VMEM((tokens, low), BF),
        pltpu.VMEM((n_w, tokens, low), BF),
        pltpu.VMEM((n_w, tokens, cols), BF),
        pltpu.VMEM((n_w, tokens, cols), BF),
    ]
    back_semaphores = [
        pltpu.SemaphoreType.DMA((BACK_SEMAPHORES, n_w)),
        pltpu.SemaphoreType.DMA((BACK_SEMAPHORES, n_w)),
        pltpu.SemaphoreType.DMA((2, n_z)),
        pltpu.SemaphoreType.DMA((2, n_z)),
        pltpu.SemaphoreType.DMA((1,)),
    ]
    stages = [pltpu.VMEM((*v[:-1], math.gcd(v[-1], Products.TILE)), BF) for v in plan.shaped[3:]]
    gains = cols + rank // n_w
    merged_scratch = [
        *plan.scratch(),
        *small_scratch(n_w, n_c, gains, cols),
        *norm_scratch,
        *(pltpu.VMEM(v.shape, v.dtype) for v in (proj, d_resid)),
        pltpu.VMEM((n_w, 8, gains), F32),
        *(pltpu.VMEM(v.shape, v.dtype) for v in (first_gain, norm_gain, query_gain)),
        *stages,
        pltpu.SemaphoreType.DMA((3,)),
        *[pltpu.SemaphoreType.DMA((1, n_w))] * 2,
        *norm_semaphores,
        *back_scratch,
        *back_semaphores,
    ]
    buffers = [v for v in merged_scratch if v.dtype in (BF, F32)]
    if bytes_of([*buffers, *rest, *late[1:], attn, q_all, h_cols, d_q, slope, slope]) < 60 * MIB:
        count = len(plan.arrays)
        done = pl.pallas_call(
            functools.partial(late_kernel, n_w, n_c, plan),
            out_shape=[
                *plan.out_shapes(), *(shape_of(*v) for v in plan.shaped[3:]), d_q, slope,
                shape_of(8, gains + cols, dtype=F32), slope,
            ],
            in_specs=[SMEM, ANY, VMEM, VMEM, VMEM] + [VMEM] * len(rest) + [ANY, VMEM, VMEM, VMEM] + [ANY] * 3,
            out_specs=[ANY] * (count + 3) + [VMEM] * 4,
            scratch_shapes=merged_scratch,
            compiler_params=params(3, 62),
        )(
            bounds, feed, resid, gain, cot, *rest, out_part, attn, q_all, h_cols,
            *(v.reshape(s) for v, s in zip(given, plan.shaped, strict=False)),
        )
        return plan.row_shards(done[:count]), done[-2], done[-1], done[-3]
    d_proj, d_resid, d_norm_gain = pl.pallas_call(
        functools.partial(norm_back_kernel, n_w, n_c),
        out_shape=[proj, d_resid, norm_gain],
        in_specs=[ANY, VMEM, VMEM, VMEM],
        out_specs=[ANY, VMEM, VMEM],
        scratch_shapes=[*norm_scratch, *norm_semaphores],
        compiler_params=params(5, 40),
    )(feed, resid, gain, cot)
    d_q_raw, d_low, d_x, d_query_gain, d_first_gain = pl.pallas_call(
        functools.partial(attend_back_kernel, n_w, n_c),
        out_shape=[d_q, shape_of(n_w, tokens, low), slope, query_gain, first_gain],
        in_specs=[SMEM] + [VMEM] * (2 + len(rest)),
        out_specs=[VMEM, ANY] + [VMEM] * 3,
        scratch_shapes=[*back_scratch, *back_semaphores],
        compiler_params=params(6, 60),
    )(bounds, d_proj, d_resid, *rest)
    pairs = ((attn, d_proj), (q_all, d_q_raw), (h_cols, d_low))
    terms = [*given, *(dot_tn(a, b.reshape(n_w * tokens, -1)).astype(BF) for a, b in pairs)]
    spread = [v.reshape(8, n_w, -1).swapaxes(0, 1) for v in (d_norm_gain, d_query_gain)]
    sums, gains, layer_output = sum_over_ctx(
        plan, terms, n_c, 4, jnp.concatenate(spread, axis=2), d_first_gain, out_part, resid
    )
    return sums, gains, layer_output, d_x


def tables(positions, width):
    exponent = jnp.arange(width // 2, dtype=F32) * (-2.0 / width)
    angles = positions.astype(F32)[..., None] * (10000.0**exponent)
    return jnp.cos(angles), jnp.sin(angles)


def whole_columns(part, rows):
    whole = lax.all_gather(part, "ctx", axis=1)
    return whole.reshape(rows, part.shape[-1])


def on_device(
    inputs,
    boundaries,
    first_gain,
    query_down,
    query_gain,
    query_up,
    key_weights,
    value_weights,
    output_weights,
    second_gain,
    gate_weights,
    up_weights,
    down_weights,
    cotangent,
):
    n_w, n_c, c = lax.axis_size("wt"), lax.axis_size("ctx"), lax.axis_index("ctx")
    width, half = inputs.shape[-1], inputs.shape[2]
    tokens, seqlen = 2 * half, 2 * half * n_c
    depth, rank = key_weights.shape[1], query_down.shape[1]
    hidden_cols = down_weights.shape[0]

    def for_columns(weight):
        rows = weight.shape[0] // n_c
        part = lax.dynamic_slice_in_dim(weight, c * rows, rows, 0)
        return part.reshape(rows, n_w, -1).swapaxes(0, 1)

    wide_bounds = jnp.zeros((8, 128), jnp.int32).at[0, : boundaries.shape[1]].set(boundaries[0])
    gains = jnp.concatenate([query_gain, second_gain]).astype(F32)
    gains = jnp.broadcast_to(gains[None], (8, gains.shape[0]))
    bounds, gains, up_part, gate_part, upper_part = exchange(
        [wide_bounds, gains, for_columns(query_up), for_columns(gate_weights), for_columns(up_weights)],
        (False, False, True, True, True), n_w, 0,
    )
    bounds = bounds[:, 0, : boundaries.shape[1]]
    gain_query = gains[:, 0, : rank // n_w].reshape(1, rank)
    gain_two = gains[:, 0, rank // n_w :].reshape(1, width)
    gain_one = first_gain.astype(F32)[None]
    up_cols = whole_columns(up_part, rank)
    gate_cols = whole_columns(gate_part, width)
    upper_cols = whole_columns(upper_part, width)

    ctx = jnp.stack([c - c % 2, c - c % 2 + 1])[:, None]
    offsets = jnp.arange(half, dtype=jnp.int32)[None]
    positions = jnp.concatenate([ctx * half + offsets, seqlen - (ctx + 1) * half + offsets], axis=1)
    cosine, sine = tables(positions, depth)
    x = inputs.reshape(tokens, width)
    cot = cotangent.reshape(tokens, width)
    h_cols, x_in, r_in, latent, q_all, kv, cot_all = first_part(
        n_w, n_c, x, cot, gain_one, gain_query, query_down, key_weights, value_weights,
        lax.dynamic_index_in_dim(cosine, c % 2, keepdims=False), lax.dynamic_index_in_dim(sine, c % 2, keepdims=False),
    )
    kv = kv.reshape(n_w // 2, seqlen, 2 * depth)
    queries, attn, resid, h_all = attend_part(
        n_w, n_c, bounds, q_all, up_cols, kv, cosine, sine, output_weights, x, gain_two
    )

    h_second = h_all.reshape(n_w * tokens, width)
    slope = cot_all.reshape(n_w * tokens, width)
    gate = dot(h_second, gate_cols)
    upper = dot(h_second, upper_cols)
    sigma = jax.nn.sigmoid(gate)
    silu = gate * sigma
    hidden = (silu * upper).astype(BF)
    d_hidden = dot_nt(slope, down_weights)
    d_gate = (d_hidden * upper * sigma * (1.0 + gate * (1.0 - sigma))).astype(BF)
    d_upper = (d_hidden * silu).astype(BF)
    out_part = dot(hidden, down_weights).astype(BF)
    d_down = dot_tn(hidden, slope).astype(BF)
    d_gate_weights = dot_tn(h_second, d_gate).astype(BF)
    d_up_weights = dot_tn(h_second, d_upper).astype(BF)
    feed = (dot_nt(d_gate, gate_cols) + dot_nt(d_upper, upper_cols)).astype(BF)

    def grouped(v):
        return v.reshape(n_w, tokens, v.shape[-1])

    def flat(v):
        return v.reshape(n_w * tokens, v.shape[-1])

    rest = (
        output_weights, queries, kv, cosine, sine, up_cols, latent, gain_query, query_down, key_weights, value_weights,
        x_in, r_in, gain_one, x,
    )
    given = (d_down, d_gate_weights, d_up_weights)
    shapes = [v.shape for v in given]
    shapes += [output_weights.shape, up_cols.shape, (query_down.shape[0], rank + 2 * depth)]
    sums, gains, layer_output, input_gradient = late_part(
        n_w, n_c, shapes, (False, True, True, False, True, False), bounds, (grouped(feed), resid, gain_two, cot), rest,
        grouped(out_part), given, flat(attn), flat(q_all), flat(h_cols),
    )
    d_down, d_gate_weights, d_up_weights, d_output, d_query_up, d_first_weights = (s.astype(F32) for s in sums)
    one, two = width // n_w, 2 * (width // n_w)
    return (
        layer_output.reshape(inputs.shape),
        input_gradient.reshape(inputs.shape),
        gains[0, :one],
        d_first_weights[:, :rank],
        gains[0, two:],
        d_query_up,
        d_first_weights[:, rank : rank + depth],
        d_first_weights[:, rank + depth :],
        d_output,
        gains[0, one:two],
        d_gate_weights,
        d_up_weights,
        d_down,
    )


def solution(mesh):
    token = P("wt", None, "ctx", None)
    row, vec = P("wt", None), P("wt")
    in_specs = (token, row, vec, row, vec, row, row, row, row, vec, row, row, row, token)
    out_specs = (token, token, vec, row, vec, row, row, row, row, vec, row, row, row)
    return jax.shard_map(
        on_device, mesh=mesh, in_specs=in_specs, out_specs=out_specs, check_vma=False
    )
```

```python
import functools
import math

import jax
import jax.numpy as jnp
from jax import lax
from jax.experimental import pallas as pl
from jax.experimental.pallas import tpu as pltpu
from jax.sharding import PartitionSpec as P

EPS = 1e-06
NEG = -1e30
F32 = jnp.float32
BF = jnp.bfloat16
VMEM = pl.BlockSpec(memory_space=pltpu.VMEM)
SMEM = pl.BlockSpec(memory_space=pltpu.SMEM)
ANY = pl.BlockSpec(memory_space=pl.ANY)
MIB = 1 << 20
MESH = pl.DeviceIdType.MESH


def dot(a, b):
    return jnp.dot(a, b, preferred_element_type=F32)


def dot_nt(a, b):
    return lax.dot_general(a, b, (((1,), (1,)), ((), ())), preferred_element_type=F32)


def dot_tn(a, b):
    return lax.dot_general(a, b, (((0,), (0,)), ((), ())), preferred_element_type=F32)


def inv_rms(v):
    return lax.rsqrt(jnp.mean(v * v, axis=-1, keepdims=True) + EPS)


def rms_back(slope, normal, scale):
    return scale * (slope - normal * jnp.mean(slope * normal, axis=-1, keepdims=True))


def rotate(v, cosine, sine):
    middle = v.shape[-1] // 2
    a, b = v[..., :middle], v[..., middle:]
    return jnp.concatenate([a * cosine - b * sine, b * cosine + a * sine], axis=-1)


def shape_of(*shape, dtype=BF):
    return jax.ShapeDtypeStruct(shape, dtype)


def params(collective, mib):
    return pltpu.CompilerParams(collective_id=collective, has_side_effects=True, vmem_limit_bytes=mib * MIB)


class Group:
    def __init__(self, n_w, n_c):
        self.n_w, self.n_z, self.per = n_w, n_c // 2, n_w // 2
        c, w = lax.axis_index("ctx"), lax.axis_index("wt")
        self.core = lax.rem(c, 2)
        self.z, self.w, self.base = c // 2, w, c - self.core
        self.home = w // self.per
        self.at_home = self.core == self.home
        self.stream = w - self.home * self.per
        self.slot = self.stream * 2 + self.core

    def target(self, j):
        return {"ctx": self.base + self.home, "wt": j}

    def source(self, i):
        return {"ctx": self.base + lax.rem(i, 2), "wt": self.core * self.per + i // 2}

    def column(self, step):
        return {"ctx": 2 * lax.rem(self.z + step, self.n_z) + self.core, "wt": self.w}

    def greet(self, column):
        barrier = pltpu.get_barrier_semaphore()
        others = [
            {"ctx": self.base + lax.rem(self.core + q, 2), "wt": lax.rem(self.w + r, self.n_w)}
            for q in range(2)
            for r in range(self.n_w)
        ][1:]
        if column:
            others += [{"ctx": 2 * lax.rem(self.z + s, self.n_z) + q, "wt": self.w} for s in range(1, self.n_z) for q in range(2)]
        for there in others:
            pl.semaphore_signal(barrier, inc=1, device_id=there, device_id_type=MESH)
        pl.semaphore_wait(barrier, len(others))


class Moves:
    def __init__(self, group, send, recv):
        self.group, self.send, self.recv = group, send, recv

    def start(self, kind, src, dst, there, index, slot, here):
        remote = pltpu.make_async_remote_copy(
            src_ref=src, dst_ref=dst, send_sem=self.send.at[kind, index], recv_sem=self.recv.at[kind, slot],
            device_id=there, device_id_type=MESH,
        )
        local = pltpu.make_async_copy(src, dst, self.recv.at[kind, slot])
        pl.when(jnp.logical_not(here))(remote.start)
        pl.when(here)(local.start)

    def to_target(self, kind, j, src, dst):
        g = self.group
        self.start(kind, src, dst, g.target(j), j, g.slot, g.at_home & (g.w == j))

    def to_source(self, kind, i, src, dst):
        g = self.group
        self.start(kind, src, dst, g.source(i), i, g.w, g.at_home & (g.slot == i))

    def arrived(self, kind, index, dst):
        pltpu.make_async_copy(dst, dst, self.recv.at[kind, index]).wait()

    def sent(self, kind, src, by_target):
        g = self.group
        for i in range(g.n_w):
            at = src(i)
            copy = pltpu.make_async_remote_copy(
                src_ref=at, dst_ref=at, send_sem=self.send.at[kind, i], recv_sem=self.recv.at[kind, i],
                device_id=g.target(i) if by_target else g.source(i), device_id_type=MESH,
            )
            here = g.at_home & ((g.w if by_target else g.slot) == i)
            pl.when(jnp.logical_not(here))(copy.wait_send)


def column_copy(group, part, step, src, dst, send, recv):
    return pltpu.make_async_remote_copy(
        src_ref=src, dst_ref=dst, send_sem=send.at[part, step], recv_sem=recv.at[part, step],
        device_id=group.column(step), device_id_type=MESH,
    )


def exchange_kernel(n_w, split, *refs):
    count = len(split)
    ins, outs = refs[:count], refs[count : 2 * count]
    send, recv, local = refs[2 * count :]
    c, w = lax.axis_index("ctx"), lax.axis_index("wt")
    barrier = pltpu.get_barrier_semaphore()
    for step in range(1, n_w):
        pl.semaphore_signal(
            barrier, inc=1, device_id={"ctx": c, "wt": lax.rem(w + step, n_w)}, device_id_type=MESH
        )
    pl.semaphore_wait(barrier, n_w - 1)
    copies = []
    for a in range(count):
        for step in range(1, n_w):
            there = lax.rem(w + step, n_w)
            copies.append(
                pltpu.make_async_remote_copy(
                    src_ref=ins[a].at[there] if split[a] else ins[a], dst_ref=outs[a].at[w],
                    send_sem=send.at[a, step], recv_sem=recv.at[a, step],
                    device_id={"ctx": c, "wt": there}, device_id_type=MESH,
                )
            )
        copies.append(pltpu.make_async_copy(ins[a].at[w] if split[a] else ins[a], outs[a].at[w], local.at[a]))
    for copy in copies:
        copy.start()
    for copy in copies:
        copy.wait()


def exchange(arrays, split, n_w, collective):
    return pl.pallas_call(
        functools.partial(exchange_kernel, n_w, split),
        out_shape=[
            jax.ShapeDtypeStruct(v.shape if s else (n_w, *v.shape), v.dtype) for v, s in zip(arrays, split, strict=True)
        ],
        in_specs=[ANY] * len(arrays),
        out_specs=[ANY] * len(arrays),
        scratch_shapes=[
            pltpu.SemaphoreType.DMA((len(arrays), n_w)),
            pltpu.SemaphoreType.DMA((len(arrays), n_w)),
            pltpu.SemaphoreType.DMA((len(arrays),)),
        ],
        compiler_params=params(collective, 16),
    )(*arrays)


def first_kernel(
    n_w, n_c,
    x_ref, cot_ref, gain_ref, query_gain_ref, down_ref, key_ref, value_ref, cos_ref, sin_ref,
    h_out, x_out, r_out, latent_out, q_all, kv_all, cot_all,
    x_in, r_in, r_own, parts, low, q_own, kv_own, kv_column, send, recv, z_send, z_recv,
):
    g = Group(n_w, n_c)
    m = Moves(g, send, recv)
    tokens, cols = x_in.shape[1:]
    rank, depth = down_ref.shape[1], key_ref.shape[1]
    r_own[...] = jnp.broadcast_to(inv_rms(x_ref[...].astype(F32)), r_own.shape)
    g.greet(True)
    for j in range(n_w):
        m.to_target(0, j, x_ref.at[:, pl.ds(j * cols, cols)], x_in.at[g.slot])
        m.to_target(1, j, r_own, r_in.at[g.slot])

    for i in range(n_w):
        m.arrived(0, i, x_in.at[i])
        m.arrived(1, i, r_in.at[i])
        x_out[i] = x_in[i]
        r_out[i] = r_in[i]
        h = (x_in[i].astype(F32) * r_in[i, :, :1] * gain_ref[...]).astype(BF)
        h_out[i] = h
        parts[i, :, :rank] = dot(h, down_ref[...]).astype(BF)
        parts[i, :, rank : rank + depth] = dot(h, key_ref[...]).astype(BF)
        parts[i, :, rank + depth :] = dot(h, value_ref[...]).astype(BF)
        m.to_source(2, i, parts.at[i], low.at[g.w])

    for j in range(n_w):
        m.arrived(2, j, low.at[j])
    total = low[0].astype(F32)
    for j in range(1, n_w):
        total += low[j].astype(F32)
    keys = rotate(total[:, rank : rank + depth], cos_ref[...], sin_ref[...]).astype(BF)
    kv = jnp.concatenate([keys, total[:, rank + depth :].astype(BF)], axis=1)
    half = tokens // 2
    mirror = g.n_z - 1 - g.z
    for part in range(2):
        kv_own[part] = kv[part * half : (part + 1) * half]

    def over_z(part, step):
        return column_copy(
            g, part, step, kv_own.at[part], kv_column.at[part, mirror if part else g.z], z_send, z_recv
        )

    for step in range(1, g.n_z):
        for part in range(2):
            over_z(part, step).start()
    kv_column[0, g.z] = kv_own[0]
    kv_column[1, mirror] = kv_own[1]
    latent = total[:, :rank]
    latent_out[...] = latent
    q_own[...] = (latent * inv_rms(latent) * query_gain_ref[...]).astype(BF)
    for j in range(n_w):
        m.to_target(3, j, q_own, q_all.at[g.slot])
    for j in range(n_w):
        m.to_target(4, j, cot_ref, cot_all.at[g.slot])
    for step in range(1, g.n_z):
        for part in range(2):
            over_z(part, step).wait_recv()

    def kv_place(part):
        return kv_all.at[g.stream, part, :, 1 - g.core if part else g.core]

    for part in range(2):
        for j in range(n_w):
            m.to_target(5 + part, j, kv_column.at[part], kv_place(part))
    for i in range(n_w):
        m.arrived(3, i, q_all.at[i])
        m.arrived(4, i, cot_all.at[i])
        for part in range(2):
            m.arrived(5 + part, i, kv_all.at[i // 2, part, :, 1 - i % 2 if part else i % 2])
    m.sent(0, lambda j: x_ref.at[:, pl.ds(j * cols, cols)], True)
    m.sent(1, lambda j: r_own, True)
    m.sent(2, lambda i: parts.at[i], False)
    m.sent(3, lambda j: q_own, True)
    m.sent(4, lambda j: cot_ref, True)
    for part in range(2):
        m.sent(5 + part, lambda j: kv_column.at[part], True)
        for step in range(1, g.n_z):
            over_z(part, step).wait_send()


def first_part(n_w, n_c, x, cot, gain, query_gain, down, key, value, cosine, sine):
    tokens, width = x.shape
    cols, rank, depth = width // n_w, down.shape[1], key.shape[1]
    n_z, half, low = n_c // 2, tokens // 2, rank + 2 * depth
    return pl.pallas_call(
        functools.partial(first_kernel, n_w, n_c),
        out_shape=[
            shape_of(n_w, tokens, cols),
            shape_of(n_w, tokens, cols),
            shape_of(n_w, tokens, 128, dtype=F32),
            shape_of(tokens, rank, dtype=F32),
            shape_of(n_w, tokens, rank),
            shape_of(n_w // 2, 2, n_z, 2, half, 2 * depth),
            shape_of(n_w, tokens, width),
        ],
        in_specs=[VMEM, ANY] + [VMEM] * 7,
        out_specs=[VMEM] * 4 + [ANY] * 3,
        scratch_shapes=[
            pltpu.VMEM((n_w, tokens, cols), BF),
            pltpu.VMEM((n_w, tokens, 128), F32),
            pltpu.VMEM((tokens, 128), F32),
            pltpu.VMEM((n_w, tokens, low), BF),
            pltpu.VMEM((n_w, tokens, low), BF),
            pltpu.VMEM((tokens, rank), BF),
            pltpu.VMEM((2, half, 2 * depth), BF),
            pltpu.VMEM((2, n_z, half, 2 * depth), BF),
            pltpu.SemaphoreType.DMA((7, n_w)),
            pltpu.SemaphoreType.DMA((7, n_w)),
            pltpu.SemaphoreType.DMA((2, n_z)),
            pltpu.SemaphoreType.DMA((2, n_z)),
        ],
        compiler_params=params(1, 40),
    )(x, cot, gain, query_gain, down, key, value, cosine, sine)


def visible_keys(bounds_ref, stream, c, tokens, seqlen):
    half = tokens // 2
    row = lax.broadcasted_iota(jnp.int32, (tokens, 1), 0)
    pos = row + jnp.where(row < half, c * half, seqlen - (c + 1) * half - half)
    begin = jnp.zeros((tokens, 1), jnp.int32)
    for j in range(bounds_ref.shape[1]):
        start = bounds_ref[stream, j]
        begin = jnp.where(pos >= start, jnp.maximum(begin, start), begin)
    key = lax.broadcasted_iota(jnp.int32, (tokens, seqlen), 1)
    return (key >= begin) & (key <= pos)


def probabilities(q, keys, visible):
    scores = jnp.where(visible, dot_nt(q, keys), NEG)
    peak = jnp.max(scores, axis=-1, keepdims=True)
    weight = jnp.where(visible, jnp.exp(scores - peak), 0.0)
    return weight * (1.0 / jnp.sum(weight, axis=-1, keepdims=True))


def attend_kernel(
    n_w, n_c,
    bounds_ref, q_ref, up_ref, kv_ref, cos_ref, sin_ref, out_ref, x_ref, gain_ref,
    queries, attn, resid, h_all,
    parts, land, h_own, send, recv,
):
    g = Group(n_w, n_c)
    m = Moves(g, send, recv)
    tokens, seqlen, depth = q_ref.shape[1], kv_ref.shape[1], kv_ref.shape[2] // 2
    scale = 1.0 / math.sqrt(depth)
    g.greet(False)

    def one(i, carry):
        stream, core = i // 2, lax.rem(i, 2)
        visible = visible_keys(bounds_ref, g.core * g.per + stream, g.base + core, tokens, seqlen)
        raw = dot(q_ref[i], up_ref[...])
        for cut in range(0, up_ref.shape[1], depth):
            span = slice(cut, cut + depth)
            q = (rotate(raw[:, span], cos_ref[core], sin_ref[core]) * scale).astype(BF)
            queries[i, :, span] = q
            probs = probabilities(q, kv_ref[stream, :, :depth], visible).astype(BF)
            attn[i, :, span] = dot(probs, kv_ref[stream, :, depth:]).astype(BF)
        parts[i] = dot(attn[i], out_ref[...]).astype(BF)
        m.to_source(0, i, parts.at[i], land.at[g.w])
        return carry

    lax.fori_loop(0, n_w, one, 0)
    total = x_ref[...].astype(F32)
    for j in range(n_w):
        m.arrived(0, j, land.at[j])
        total += land[j].astype(F32)
    resid[...] = total
    h_own[...] = (total * inv_rms(total) * gain_ref[...]).astype(BF)
    for j in range(n_w):
        m.to_target(1, j, h_own, h_all.at[g.slot])
    for i in range(n_w):
        m.arrived(1, i, h_all.at[i])
    m.sent(0, lambda i: parts.at[i], False)
    m.sent(1, lambda j: h_own, True)


def attend_part(n_w, n_c, bounds, q_all, up_cols, kv, cosine, sine, output, x, gain):
    tokens, width = x.shape
    features = up_cols.shape[1]
    return pl.pallas_call(
        functools.partial(attend_kernel, n_w, n_c),
        out_shape=[
            shape_of(n_w, tokens, features),
            shape_of(n_w, tokens, features),
            shape_of(tokens, width, dtype=F32),
            shape_of(n_w, tokens, width),
        ],
        in_specs=[SMEM] + [VMEM] * 8,
        out_specs=[VMEM] * 3 + [ANY],
        scratch_shapes=[
            pltpu.VMEM((n_w, tokens, width), BF),
            pltpu.VMEM((n_w, tokens, width), BF),
            pltpu.VMEM((tokens, width), BF),
            pltpu.SemaphoreType.DMA((2, n_w)),
            pltpu.SemaphoreType.DMA((2, n_w)),
        ],
        compiler_params=params(2, 50),
    )(bounds, q_all, up_cols, kv, cosine, sine, output, x, gain)


class Plan:
    def __init__(self, shapes, turned, n_w, slots, limit):
        self.n_w, self.arrays, self.turned = n_w, shapes, turned
        self.wide = all(cols % 128 == 0 for (_, cols), turn in zip(shapes, turned, strict=True) if turn)
        self.shaped, self.pieces, self.members, self.ring_shapes = [], [], [[], []], [None, None]
        for (rows, cols), turn in zip(shapes, turned, strict=True):
            self.shaped.append((n_w, 2, 2, rows // n_w // 4, cols) if turn else (2, 2, rows // 4, cols))
        for kind in range(2):
            mine = [v for v, turn in zip(self.shaped, turned, strict=True) if turn == bool(kind)]
            if mine:
                lead, cols = (n_w, 2) if kind else (2,), max(v[-1] for v in mine)
                rows = 16
                common = math.gcd(*(v[-2] for v in mine))
                for more in range(16, common + 1, 16):
                    if common % more == 0 and math.prod(lead) * more * cols * 2 <= limit:
                        rows = more
                self.ring_shapes[kind] = (*lead, rows, cols)
        for a, (v, turn) in enumerate(zip(self.shaped, turned, strict=True)):
            rows = self.ring_shapes[int(turn)][-2]
            for row in range(0, v[-2], rows):
                self.members[int(turn)].append(len(self.pieces))
                self.pieces.append((a, int(turn), len(self.members[int(turn)]) - 1, row, rows, v[-1]))
        self.slots = [min(slots, len(members)) for members in self.members]

    def __len__(self):
        return len(self.pieces)

    def slot(self, q):
        return self.pieces[q][2] % self.slots[self.pieces[q][1]]

    def before(self, q):
        _, kind, index = self.pieces[q][:3]
        return self.members[kind][index - self.slots[kind]] if index >= self.slots[kind] else None

    def after(self, q):
        _, kind, index = self.pieces[q][:3]
        later = index + self.slots[kind]
        return self.members[kind][later] if later < len(self.members[kind]) else None

    def scratch(self):
        shapes = [v or (16, 128) for v in self.ring_shapes]
        slots = [max(v, 1) for v in self.slots]
        rings = [pltpu.VMEM((n, *v), BF) for n, v in zip(slots, shapes, strict=True)]
        rows, turned = shapes
        halves = [pltpu.VMEM((slots[0], *rows[-2:]), BF), pltpu.VMEM((slots[1], self.n_w, *turned[-2:]), BF)]
        moved = (turned[-2], self.n_w * turned[-1]) if self.wide else (self.n_w, *turned[-2:])
        kinds, count = 5 + self.n_w, len(self)
        return [
            *rings, *rings, *rings, *halves, pltpu.VMEM((slots[1], *moved), BF),
            pltpu.SemaphoreType.DMA((count,)),
            pltpu.SemaphoreType.DMA((count,)),
            pltpu.SemaphoreType.DMA((kinds, count)),
            pltpu.SemaphoreType.DMA((kinds, count)),
            pltpu.SemaphoreType.REGULAR((4, count)),
        ]

    def out_shapes(self):
        return [
            shape_of(2, 2, v[-2], self.n_w * v[-1]) if turn and self.wide else shape_of(*v)
            for v, turn in zip(self.shaped, self.turned, strict=True)
        ]

    def row_shards(self, sums):
        done = []
        for s, (rows, cols), turn in zip(sums, self.arrays, self.turned, strict=True):
            if self.wide or not turn:
                done.append(s.reshape(-1, s.shape[-1]))
            else:
                done.append(s.reshape(self.n_w, rows // self.n_w, cols).swapaxes(0, 1).reshape(rows // self.n_w, -1))
        return done


CHAIN_SCRATCH = 14


class Chain:
    AHEAD, LEAD, HALF, MOVE, DONE, LAG = 2, 3, 1, 2, 3, 9

    def __init__(self, plan, n_c, terms, outs, scratch):
        self.plan, self.n_w, self.terms, self.outs = plan, plan.n_w, terms, outs
        self.own, self.mates, self.ups, self.halves = (scratch[2 * i : 2 * i + 2] for i in range(4))
        self.moved, self.load, self.place, self.send, self.recv, self.credit = scratch[8:]
        c, w = lax.axis_index("ctx"), lax.axis_index("wt")
        chain, k = n_c // 2, c // 2
        self.w, self.core = w, lax.rem(c, 2)
        left = k < chain // 2
        self.side = jnp.where(left, 0, 1)
        far = jnp.where(left, k, chain - 1 - k)
        self.middle, self.outside = far == chain // 2 - 1, far > 0
        self.mate = {"ctx": c + 1 - 2 * self.core, "wt": w}
        self.inner = {"ctx": jnp.where(left, c + 2, c - 2), "wt": w}
        self.outer = {"ctx": jnp.where(left, c - 2, c + 2), "wt": w}
        self.peers = [{"ctx": c, "wt": lax.rem(w + r, self.n_w)} for r in range(1, self.n_w)]
        self.now, self.ready = 0, len(plan)

    def turned(self, q):
        return self.plan.turned[self.plan.pieces[q][0]]

    def every(self, q):
        return (slice(None),) if self.turned(q) else ()

    def term(self, q, core):
        a, _, _, row, rows, _ = self.plan.pieces[q]
        return self.terms[a].at[(*self.every(q), core, slice(None), pl.ds(row, rows))]

    def fitting(self, q, buffer):
        cols = self.plan.pieces[q][5]
        lead = (slice(None),) * (len(buffer.shape) - 2)
        return buffer.at[(self.plan.slot(q), *lead, pl.ds(0, cols))]

    def ring(self, q, buffers):
        return self.fitting(q, buffers[self.plan.pieces[q][1]])

    def half_buffer(self, q):
        return self.ring(q, self.halves)

    def remote(self, kind, q, src, dst, there):
        return pltpu.make_async_remote_copy(
            src_ref=src, dst_ref=dst, send_sem=self.send.at[kind, q], recv_sem=self.recv.at[kind, q], device_id=there,
            device_id_type=MESH,
        )

    def own_load(self, q):
        return pltpu.make_async_copy(self.term(q, self.core), self.ring(q, self.own), self.load.at[q])

    def to_mate(self, q):
        return self.remote(0, q, self.term(q, 1 - self.core), self.ring(q, self.mates), self.mate)

    def along(self, q, there):
        return self.remote(1, q, self.ring(q, self.own), self.ring(q, self.ups), there)

    def to_across(self, q):
        side = self.ring(q, self.own).at[(*self.every(q), 1 - self.side)]
        return self.remote(5, q, side, self.half_buffer(q), self.inner)

    def moved_part(self, q, source):
        cols = self.plan.pieces[q][5]
        if not self.plan.wide:
            return self.moved.at[self.plan.slot(q), source, :, pl.ds(0, cols)]
        return self.moved.at[self.plan.slot(q), :, pl.ds(pl.multiple_of(source * cols, 128), cols)]

    def to_peer(self, q, r, slot):
        there = self.peers[r]
        return self.remote(6 + r, q, self.half_buffer(q).at[there["wt"]], self.moved_part(q, slot), there)

    def finished(self, q):
        if not self.turned(q):
            return self.half_buffer(q)
        if self.plan.wide:
            return self.moved.at[self.plan.slot(q), :, pl.ds(0, self.n_w * self.plan.pieces[q][5])]
        return self.fitting(q, self.moved)

    def result(self, q, *lead):
        a, kind, _, row, rows, _ = self.plan.pieces[q]
        every = () if self.plan.wide else self.every(q)
        return self.outs[a].at[(*every, *lead, pl.ds(row, rows))]

    def half_place(self, q):
        return pltpu.make_async_copy(self.finished(q), self.result(q, self.core, self.side), self.place.at[q])

    def half_across(self, q, side):
        return self.remote(2, q, self.finished(q), self.result(q, self.core, side), self.inner)

    def down(self, kind, q, there):
        here = self.result(q, self.core, slice(None))
        return self.remote(kind, q, here, here, there)

    def add(self, q, ins, out):
        rows = out.shape[-2]
        step = 16 if rows % 16 == 0 else rows
        lead = (slice(None),) * (len(out.shape) - 2)

        def body(i, carry):
            at = (*lead, pl.ds(i * step, step))
            total = ins[0][at].astype(F32)
            for ref in ins[1:]:
                total += ref[at].astype(F32)
            out[at] = total.astype(BF)
            return carry

        lax.fori_loop(0, rows // step, body, 0)

    def grant(self, kind, q, there):
        pl.semaphore_signal(self.credit.at[kind, q], inc=1, device_id=there, device_id_type=MESH)

    def prefetch(self, q):
        before = self.plan.before(q)
        if before is not None:
            pl.when(self.middle)(self.to_across(before).wait_send)
            pl.when(jnp.logical_not(self.middle))(self.along(before, self.inner).wait_send)
            pl.semaphore_wait(self.credit.at[0, q], 1)
        self.own_load(q).start()
        self.to_mate(q).start()

    def up(self, q):
        self.own_load(q).wait()
        self.to_mate(q).wait_recv()
        after, before = self.plan.after(q), self.plan.before(q)
        own, mates, ups = (self.ring(q, b) for b in (self.own, self.mates, self.ups))

        @pl.when(self.outside)
        def _():
            self.along(q, self.outer).wait_recv()
            self.add(q, [own, mates, ups], own)
            if after is not None:
                self.grant(1, after, self.outer)

        @pl.when(jnp.logical_not(self.outside))
        def _():
            self.add(q, [own, mates], own)

        if after is not None:
            self.grant(0, after, self.mate)

        @pl.when(self.middle)
        def _():
            if before is not None:
                pl.semaphore_wait(self.credit.at[2, q], 1)
            self.to_across(q).start()

        @pl.when(jnp.logical_not(self.middle))
        def _():
            if before is not None:
                pl.semaphore_wait(self.credit.at[1, q], 1)
            self.along(q, self.inner).start()

    def finish_half(self, q):
        self.to_across(q).wait_recv()
        half = self.half_buffer(q)
        self.add(q, [self.ring(q, self.own).at[(*self.every(q), self.side)], half], half)
        if self.turned(q):
            if self.plan.before(q) is not None:
                pl.semaphore_wait(self.credit.at[3, q], self.n_w - 1)
            for r in range(self.n_w - 1):
                self.to_peer(q, r, self.w).start()
            self.moved_part(q, self.w)[...] = half[self.w]
        else:
            self.spread(q)

    def spread(self, q):
        self.half_place(q).start()
        self.half_across(q, self.side).start()

    def move(self, q):
        if self.turned(q):
            for r in range(self.n_w - 1):
                self.to_peer(q, r, lax.rem(self.w + self.n_w - r - 1, self.n_w)).wait_recv()
            self.spread(q)

    def pass_down(self, q):
        pl.when(self.outside)(self.down(3, q, self.outer).start)
        self.down(4, q, self.mate).start()

    def free(self, q):
        after = self.plan.after(q)
        if after is not None:
            self.half_across(q, self.side).wait_send()
            if self.turned(q):
                for r in range(self.n_w - 1):
                    self.to_peer(q, r, self.w).wait_send()
                for there in self.peers:
                    self.grant(3, after, there)
            self.grant(2, after, self.inner)

    def tick(self):
        t, count = self.now, len(self.plan)
        self.now += 1
        inside, outside = self.middle, jnp.logical_not(self.middle)

        @pl.when(outside)
        def _():
            if t == 0:
                for q in range(min(self.AHEAD, count)):
                    self.prefetch(q)
            for q in range(0 if t == 0 else t + self.LEAD, t + self.LEAD + 1):
                if q < count:
                    self.up(q)
                if q + self.AHEAD < count:
                    self.prefetch(q + self.AHEAD)
            if 0 <= t - self.LAG < count:
                self.down(3, t - self.LAG, self.inner).wait_recv()
                self.pass_down(t - self.LAG)

        @pl.when(inside)
        def _():
            if t == 0:
                for q in range(min(self.AHEAD, count)):
                    self.prefetch(q)
            if t < count:
                self.up(t)
            if 0 <= t - self.HALF < count:
                self.finish_half(t - self.HALF)
            if 0 <= t - self.MOVE < count:
                self.move(t - self.MOVE)
            done = t - self.DONE
            if 0 <= done < count:
                self.half_place(done).wait()
                self.half_across(done, 1 - self.side).wait_recv()
                self.pass_down(done)
                self.free(done)
            if t + self.AHEAD < count:
                self.prefetch(t + self.AHEAD)

    def ticks(self, number):
        for _ in range(number):
            if self.now + self.AHEAD + self.LEAD < self.ready or self.now < len(self.plan) + self.LAG and self.ready == len(self.plan):
                self.tick()

    def have(self, arrays):
        self.ready = sum(piece[0] < arrays for piece in self.plan.pieces)

    def finish(self):
        self.ticks(len(self.plan) + self.LAG)
        for q in range(len(self.plan)):
            last = self.plan.after(q) is None

            @pl.when(self.middle)
            def _():
                if last:
                    self.to_across(q).wait_send()
                    self.half_across(q, self.side).wait_send()
                    for r in range(self.n_w - 1 if self.turned(q) else 0):
                        self.to_peer(q, r, self.w).wait_send()

            if last:
                pl.when(jnp.logical_not(self.middle))(self.along(q, self.inner).wait_send)
            self.to_mate(q).wait_send()
            pl.when(self.outside)(self.down(3, q, self.outer).wait_send)
            other = self.result(q, 1 - self.core, slice(None))
            self.remote(4, q, other, other, self.mate).wait_recv()
            self.down(4, q, self.mate).wait_send()


class Small:
    def __init__(self, group, n_c, moves, terms, first_terms, layer_terms, resid, out, layer_out, layer_land, scratch):
        self.g, self.n_c, self.m = group, n_c, moves
        self.terms, self.first_terms, self.layer_terms, self.resid = terms, first_terms, layer_terms, resid
        self.out, self.layer_out, self.layer_land = out, layer_out, layer_land
        self.land, self.own, self.all, self.send, self.recv = scratch
        self.c = lax.axis_index("ctx")

    def block(self, step):
        n_w, j = self.g.n_w, lax.rem(self.g.w + step, self.g.n_w)
        return pltpu.make_async_remote_copy(
            src_ref=self.terms.at[j], dst_ref=self.land.at[step], send_sem=self.send.at[step],
            recv_sem=self.recv.at[step], device_id={"ctx": self.c, "wt": j}, device_id_type=MESH,
        )

    def total(self, step):
        at = self.g.n_w + step
        return pltpu.make_async_remote_copy(
            src_ref=self.own, dst_ref=self.all.at[step], send_sem=self.send.at[at], recv_sem=self.recv.at[at],
            device_id={"ctx": lax.rem(self.c + step, self.n_c), "wt": self.g.w}, device_id_type=MESH,
        )

    def begin(self):
        for step in range(1, self.g.n_w):
            self.block(step).start()
        for i in range(self.g.n_w):
            self.m.to_source(0, i, self.layer_terms.at[i], self.layer_land.at[self.g.w])

    def middle(self):
        first = self.first_terms.shape[1]
        total = self.terms[self.g.w]
        for step in range(1, self.g.n_w):
            self.block(step).wait_recv()
            total += self.land[step]
        self.own[:, :first] = self.first_terms[...]
        self.own[:, first:] = total
        for step in range(1, self.n_c):
            self.total(step).start()
        total = self.resid[...]
        for j in range(self.g.n_w):
            self.m.arrived(0, j, self.layer_land.at[j])
            total += self.layer_land[j].astype(F32)
        self.layer_out[...] = total.astype(BF)

    def end(self):
        total = self.own[...]
        for step in range(1, self.n_c):
            self.total(step).wait_recv()
            total += self.all[step]
        self.out[...] = total
        for step in range(1, self.g.n_w):
            self.block(step).wait_send()
        for step in range(1, self.n_c):
            self.total(step).wait_send()
        self.m.sent(0, lambda i: self.layer_terms.at[i], False)


SMALL_SCRATCH = 5


def small_scratch(n_w, n_c, width, first):
    return [
        pltpu.VMEM((n_w, 8, width), F32),
        pltpu.VMEM((8, width + first), F32),
        pltpu.VMEM((n_c, 8, width + first), F32),
        pltpu.SemaphoreType.DMA((n_w + n_c,)),
        pltpu.SemaphoreType.DMA((n_w + n_c,)),
    ]


def sum_kernel(plan, n_c, *refs):
    count = len(plan.arrays)
    terms, (gain_terms, first_terms, layer_terms, resid_ref), refs = refs[:count], refs[count : count + 4], refs[count + 4 :]
    outs, (gains_out, layer_out), refs = refs[:count], refs[count : count + 2], refs[count + 2 :]
    layer_land, group_send, group_recv = refs[CHAIN_SCRATCH + SMALL_SCRATCH :]
    g = Group(plan.n_w, n_c)
    chain = Chain(plan, n_c, terms, outs, refs[:CHAIN_SCRATCH])
    small = Small(
        g, n_c, Moves(g, group_send, group_recv), gain_terms, first_terms, layer_terms, resid_ref, gains_out, layer_out,
        layer_land, refs[CHAIN_SCRATCH : CHAIN_SCRATCH + SMALL_SCRATCH],
    )
    g.greet(True)
    chain.ticks(2)
    small.begin()
    chain.ticks(4)
    small.middle()
    chain.finish()
    small.end()


def sum_over_ctx(plan, terms, n_c, collective, gain_terms, first_terms, layer_terms, resid):
    n_w, count = plan.n_w, len(plan.arrays)
    width, first = gain_terms.shape[-1], first_terms.shape[-1]
    sums = pl.pallas_call(
        functools.partial(sum_kernel, plan, n_c),
        out_shape=[*plan.out_shapes(), shape_of(8, width + first, dtype=F32), shape_of(*resid.shape)],
        in_specs=[ANY] * count + [VMEM, VMEM, ANY, VMEM],
        out_specs=[ANY] * count + [VMEM, VMEM],
        scratch_shapes=[
            *plan.scratch(),
            *small_scratch(n_w, n_c, width, first),
            pltpu.VMEM(layer_terms.shape, BF),
            pltpu.SemaphoreType.DMA((1, n_w)),
            pltpu.SemaphoreType.DMA((1, n_w)),
        ],
        compiler_params=params(collective, 60),
    )(*(v.reshape(s) for v, s in zip(terms, plan.shaped, strict=True)), gain_terms, first_terms, layer_terms, resid)
    return plan.row_shards(sums[:count]), sums[-2], sums[-1]


def norm_back(g, m, feed_ref, resid_ref, gain_ref, cot_ref, land, proj_own, proj_in, d_resid, d_gain, ticks):
    for i in range(g.n_w):
        m.to_source(0, i, feed_ref.at[i], land.at[g.w])
    ticks(3)
    for j in range(g.n_w):
        m.arrived(0, j, land.at[j])
    d_h = land[0].astype(F32)
    for j in range(1, g.n_w):
        d_h += land[j].astype(F32)
    resid = resid_ref[...]
    scale = inv_rms(resid)
    normal = resid * scale
    d_gain[...] = jnp.broadcast_to(jnp.sum(d_h * normal, axis=0, keepdims=True), d_gain.shape)
    total = cot_ref[...].astype(F32) + rms_back(d_h * gain_ref[...], normal, scale)
    d_resid[...] = total
    proj_own[...] = total.astype(BF)
    for j in range(g.n_w):
        m.to_target(1, j, proj_own, proj_in.at[g.slot])
    ticks(3)
    for i in range(g.n_w):
        m.arrived(1, i, proj_in.at[i])


def norm_back_ends(m, feed_ref, proj_own):
    m.sent(0, lambda i: feed_ref.at[i], False)
    m.sent(1, lambda j: proj_own, True)


NORM_SEMAPHORES, BACK_SEMAPHORES = 2, 6


def norm_back_kernel(
    n_w, n_c, feed_ref, resid_ref, gain_ref, cot_ref, proj_all, d_resid, d_gain, land, proj_own, send, recv
):
    g = Group(n_w, n_c)
    m = Moves(g, send, recv)
    g.greet(False)
    norm_back(g, m, feed_ref, resid_ref, gain_ref, cot_ref, land, proj_own, proj_all, d_resid, d_gain, lambda n: None)
    norm_back_ends(m, feed_ref, proj_own)


def attend_back(
    g, m,
    bounds_ref, proj_ref, d_resid_ref, out_ref, queries_ref, kv_ref, cos_ref, sin_ref, up_ref, latent_ref,
    query_gain_ref, down_ref, key_ref, value_ref, x_in_ref, r_in_ref, gain_ref, x_ref,
    d_q_out, low_out, slope_out, d_query_gain, d_gain,
    d_kv, kv_parts, kv_land, kv_column, kv_z, q_parts, q_land,
    low_own, low_in, n_parts, n_land, z_send, z_recv, out_sem, work,
):
    tokens, seqlen, depth = x_ref.shape[0], kv_ref.shape[1], kv_ref.shape[2] // 2
    rank, half, cols = down_ref.shape[1], tokens // 2, x_in_ref.shape[2]
    n_w = g.n_w
    mirror = g.n_z - 1 - g.z
    scale = 1.0 / math.sqrt(depth)

    def kv_part(stream, core, part):
        return kv_parts.at[stream, part, :, 1 - core if part else core]

    work.before_attention()

    def one_stream(stream):
        d_kv[...] = jnp.zeros_like(d_kv)
        for core in range(2):
            i = 2 * stream + core
            visible = visible_keys(bounds_ref, g.core * g.per + stream, g.base + core, tokens, seqlen)
            slopes = dot_nt(proj_ref[i], out_ref[...]).astype(BF)
            d_keys = jnp.zeros((seqlen, depth), F32)
            d_values = jnp.zeros((seqlen, depth), F32)
            for cut in range(0, up_ref.shape[1], depth):
                span = slice(cut, cut + depth)
                q, slope = queries_ref[i, :, span], slopes[:, span]
                probs = probabilities(q, kv_ref[stream, :, :depth], visible)
                d_probs = dot_nt(slope, kv_ref[stream, :, depth:])
                delta = jnp.sum(probs * d_probs, axis=-1, keepdims=True)
                d_scores = (probs * (d_probs - delta)).astype(BF)
                d_q = dot(d_scores, kv_ref[stream, :, :depth])
                d_q_out[i, :, span] = (rotate(d_q, cos_ref[core], -sin_ref[core]) * scale).astype(BF)
                d_keys += dot_tn(d_scores, q)
                d_values += dot_tn(probs.astype(BF), slope)
            shaped = (2, g.n_z, 2, half, depth)
            d_kv[:, :, :, :, :depth] += d_keys.reshape(shaped)
            d_kv[:, :, :, :, depth:] += d_values.reshape(shaped)
            q_parts[i] = dot_nt(d_q_out[i], up_ref[...]).astype(BF)
            m.to_source(0, i, q_parts.at[i], q_land.at[g.w])
            work.ticks(3)
        kv_parts[stream] = d_kv[...].astype(BF)
        for core in range(2):
            for part in range(2):
                m.to_source(1 + part, 2 * stream + core, kv_part(stream, core, part), kv_land.at[g.w, part])

    if n_w <= 4:
        for stream in range(g.per):
            one_stream(stream)
    else:
        lax.fori_loop(0, g.per, lambda stream, carry: (one_stream(stream), carry)[1], 0)
    work.after_attention(d_q_out)
    for j in range(n_w):
        m.arrived(0, j, q_land.at[j])
    d_n = q_land[0].astype(F32)
    for j in range(1, n_w):
        d_n += q_land[j].astype(F32)
    latent = latent_ref[...]
    r_query = inv_rms(latent)
    n_query = latent * r_query
    d_query_gain[...] = jnp.broadcast_to(jnp.sum(d_n * n_query, axis=0, keepdims=True), d_query_gain.shape)
    low_own[:, :rank] = rms_back(d_n * query_gain_ref[...], n_query, r_query).astype(BF)
    lead = pl.ds(0, rank)
    for j in range(n_w):
        m.to_target(3, j, low_own.at[:, lead], low_in.at[g.slot, :, lead])
    work.ticks(2)

    for j in range(n_w):
        for part in range(2):
            m.arrived(1 + part, j, kv_land.at[j, part])
    total = kv_land[0].astype(F32)
    for j in range(1, n_w):
        total += kv_land[j].astype(F32)
    kv_column[...] = total.astype(BF)

    def over_z(part, step):
        z = lax.rem(g.z + step, g.n_z)
        return column_copy(
            g, part, step, kv_column.at[part, g.n_z - 1 - z if part else z], kv_z.at[step, part], z_send, z_recv
        )

    for step in range(1, g.n_z):
        for part in range(2):
            over_z(part, step).start()
    work.ticks(2)
    own = [kv_column[0, g.z].astype(F32), kv_column[1, mirror].astype(F32)]
    for step in range(1, g.n_z):
        for part in range(2):
            over_z(part, step).wait_recv()
            own[part] += kv_z[step, part].astype(F32)
    own = jnp.concatenate(own, axis=0)
    low_own[:, rank : rank + depth] = rotate(own[:, :depth], cos_ref[g.core], -sin_ref[g.core]).astype(BF)
    low_own[:, rank + depth :] = own[:, depth:].astype(BF)
    tail = pl.ds(rank, 2 * depth)
    for j in range(n_w):
        m.to_target(4, j, low_own.at[:, tail], low_in.at[g.slot, :, tail])

    d_first = jnp.zeros((1, cols), F32)
    for i in range(n_w):
        m.arrived(3, i, low_in.at[i, :, lead])
        d_h = dot_nt(low_in[i, :, :rank], down_ref[...])
        m.arrived(4, i, low_in.at[i, :, tail])
        d_h += dot_nt(low_in[i, :, rank : rank + depth], key_ref[...])
        d_h += dot_nt(low_in[i, :, rank + depth :], value_ref[...])
        normal = x_in_ref[i].astype(F32) * r_in_ref[i, :, :1]
        d_first += jnp.sum(d_h * normal, axis=0, keepdims=True)
        n_parts[i] = (d_h * gain_ref[...]).astype(BF)
        m.to_source(5, i, n_parts.at[i], n_land.at[g.w])
        work.ticks(1)
    d_gain[...] = jnp.broadcast_to(d_first, d_gain.shape)
    work.after_low(low_in, low_out, out_sem)
    for j in range(n_w):
        m.arrived(5, j, n_land.at[j])
    d_n = jnp.concatenate([n_land[j].astype(F32) for j in range(n_w)], axis=1)
    x = x_ref[...].astype(F32)
    r_first = inv_rms(x)
    slope_out[...] = (d_resid_ref[...] + rms_back(d_n, x * r_first, r_first)).astype(BF)

    work.at_end(low_in, low_out, out_sem)
    m.sent(0, lambda i: q_parts.at[i], False)
    m.sent(3, lambda j: low_own.at[:, lead], True)
    m.sent(4, lambda j: low_own.at[:, tail], True)
    m.sent(5, lambda i: n_parts.at[i], False)
    for part in range(2):
        m.sent(1 + part, lambda i: kv_part(i // 2, i % 2, part), False)
        for step in range(1, g.n_z):
            over_z(part, step).wait_send()


class Alone:
    def ticks(self, number):
        pass

    def before_attention(self):
        pass

    def after_attention(self, d_q):
        pass

    def after_low(self, low_in, low_out, sem):
        pltpu.make_async_copy(low_in, low_out, sem.at[0]).start()

    def at_end(self, low_in, low_out, sem):
        pltpu.make_async_copy(low_in, low_out, sem.at[0]).wait()


class Products:
    TILE = 512

    def __init__(self, chain, first, attn, proj, q_all, h_cols, stages, sems):
        self.chain, self.ticks, self.first = chain, chain.ticks, first
        self.attn, self.proj, self.q_all, self.h_cols = attn, proj, q_all, h_cols
        self.stages, self.sems = stages, sems

    def product(self, which, left, right, ticks):
        terms, stage = self.chain.terms[self.first + which], self.stages[which]
        cols, lead = terms.shape[-1], (slice(None),) * (len(terms.shape) - 1)
        tile = stage.shape[-1]
        rows = left.shape[0]

        def out(at):
            return pltpu.make_async_copy(stage, terms.at[(*lead, pl.ds(at, tile))], self.sems.at[which])

        for at in range(0, cols, tile):
            made = dot_tn(left[...], right[:, :, at : at + tile].reshape(rows, tile)).astype(BF)
            if at > 0:
                out(at - tile).wait()
            stage[...] = made.reshape(stage.shape)
            out(at).start()
            self.ticks(ticks)
        out(cols - tile).wait()
        self.chain.have(self.first + which + 1)

    def before_attention(self):
        self.product(0, self.attn, self.proj, 1)

    def after_attention(self, d_q):
        self.product(1, self.q_all, d_q, 1)

    def after_low(self, low_in, low_out, sem):
        self.product(2, self.h_cols, low_in, 1)

    def at_end(self, low_in, low_out, sem):
        pass


def attend_back_kernel(n_w, n_c, *refs):
    *refs, send, recv, z_send, z_recv, out_sem = refs
    g = Group(n_w, n_c)
    g.greet(True)
    attend_back(g, Moves(g, send, recv), *refs, z_send, z_recv, out_sem, Alone())


def late_kernel(n_w, n_c, plan, *refs):
    bounds_ref, feed_ref, resid_ref, gain_ref, cot_ref, *refs = refs
    rest, (layer_terms, attn, q_all, h_cols), given, refs = refs[:15], refs[15:19], refs[19:22], refs[22:]
    count = len(plan.arrays)
    sums, made, (d_q_out, slope_out, gains_out, layer_out), refs = (
        refs[:count], refs[count : count + 3], refs[count + 3 : count + 7], refs[count + 7 :]
    )
    chain_scratch, small_refs, refs = (
        refs[:CHAIN_SCRATCH], refs[CHAIN_SCRATCH : CHAIN_SCRATCH + SMALL_SCRATCH], refs[CHAIN_SCRATCH + SMALL_SCRATCH :]
    )
    land, proj_own, proj_in, d_resid, gain_terms, first_terms, norm_gain, query_gain, *refs = refs
    *stages, product_sems, small_send, small_recv, norm_send, norm_recv = refs[:8]
    *back_scratch, send, recv, z_send, z_recv, out_sem = refs[8:]
    g = Group(n_w, n_c)
    norm_moves = Moves(g, norm_send, norm_recv)
    chain = Chain(plan, n_c, [*given, *made], sums, chain_scratch)
    chain.have(3)
    work = Products(chain, 3, attn, proj_in, q_all, h_cols, stages, product_sems)
    g.greet(True)
    norm_back(g, norm_moves, feed_ref, resid_ref, gain_ref, cot_ref, land, proj_own, proj_in, d_resid, norm_gain, chain.ticks)
    attend_back(
        g, Moves(g, send, recv), bounds_ref, proj_in, d_resid, *rest, d_q_out, None, slope_out, query_gain, first_terms,
        *back_scratch, z_send, z_recv, out_sem, work,
    )
    width, rank = norm_gain.shape[1] // n_w, query_gain.shape[1] // n_w
    for j in range(n_w):
        gain_terms[j, :, :width] = norm_gain[:, j * width : (j + 1) * width]
        gain_terms[j, :, width:] = query_gain[:, j * rank : (j + 1) * rank]
    small = Small(
        g, n_c, Moves(g, small_send, small_recv), gain_terms, first_terms, layer_terms, resid_ref, gains_out, layer_out,
        land, small_refs,
    )
    small.begin()
    chain.ticks(4)
    small.middle()
    chain.finish()
    small.end()
    norm_back_ends(norm_moves, feed_ref, proj_own)


def bytes_of(shapes):
    return sum(math.prod(v.shape) * jnp.dtype(v.dtype).itemsize for v in shapes)


def late_part(n_w, n_c, shapes, turned, bounds, late, rest, out_part, given, attn, q_all, h_cols):
    feed, resid, gain, cot = late
    kv, up_cols, x = rest[2], rest[5], rest[14]
    (tokens, width), (rank, features) = x.shape, up_cols.shape
    per, seqlen, both = kv.shape
    n_z, half, cols, low = n_c // 2, tokens // 2, width // n_w, rank + both
    plan = Plan(shapes, turned, n_w, 8, 380_000)
    proj, d_q, slope = shape_of(n_w, tokens, width), shape_of(n_w, tokens, features), shape_of(tokens, width)
    d_resid, norm_gain = shape_of(tokens, width, dtype=F32), shape_of(8, width, dtype=F32)
    query_gain, first_gain = shape_of(8, rank, dtype=F32), shape_of(8, cols, dtype=F32)
    norm_scratch = [pltpu.VMEM((n_w, tokens, width), BF), pltpu.VMEM((tokens, width), BF)]
    norm_semaphores = [pltpu.SemaphoreType.DMA((NORM_SEMAPHORES, n_w))] * 2
    back_scratch = [
        pltpu.VMEM((2, n_z, 2, half, both), F32),
        pltpu.VMEM((per, 2, n_z, 2, half, both), BF),
        pltpu.VMEM((n_w, 2, n_z, half, both), BF),
        pltpu.VMEM((2, n_z, half, both), BF),
        pltpu.VMEM((n_z, 2, half, both), BF),
        pltpu.VMEM((n_w, tokens, rank), BF),
        pltpu.VMEM((n_w, tokens, rank), BF),
        pltpu.VMEM((tokens, low), BF),
        pltpu.VMEM((n_w, tokens, low), BF),
        pltpu.VMEM((n_w, tokens, cols), BF),
        pltpu.VMEM((n_w, tokens, cols), BF),
    ]
    back_semaphores = [
        pltpu.SemaphoreType.DMA((BACK_SEMAPHORES, n_w)),
        pltpu.SemaphoreType.DMA((BACK_SEMAPHORES, n_w)),
        pltpu.SemaphoreType.DMA((2, n_z)),
        pltpu.SemaphoreType.DMA((2, n_z)),
        pltpu.SemaphoreType.DMA((1,)),
    ]
    stages = [pltpu.VMEM((*v[:-1], math.gcd(v[-1], Products.TILE)), BF) for v in plan.shaped[3:]]
    gains = cols + rank // n_w
    merged_scratch = [
        *plan.scratch(),
        *small_scratch(n_w, n_c, gains, cols),
        *norm_scratch,
        *(pltpu.VMEM(v.shape, v.dtype) for v in (proj, d_resid)),
        pltpu.VMEM((n_w, 8, gains), F32),
        *(pltpu.VMEM(v.shape, v.dtype) for v in (first_gain, norm_gain, query_gain)),
        *stages,
        pltpu.SemaphoreType.DMA((3,)),
        *[pltpu.SemaphoreType.DMA((1, n_w))] * 2,
        *norm_semaphores,
        *back_scratch,
        *back_semaphores,
    ]
    buffers = [v for v in merged_scratch if v.dtype in (BF, F32)]
    if bytes_of([*buffers, *rest, *late[1:], attn, q_all, h_cols, d_q, slope, slope]) < 60 * MIB:
        count = len(plan.arrays)
        done = pl.pallas_call(
            functools.partial(late_kernel, n_w, n_c, plan),
            out_shape=[
                *plan.out_shapes(), *(shape_of(*v) for v in plan.shaped[3:]), d_q, slope,
                shape_of(8, gains + cols, dtype=F32), slope,
            ],
            in_specs=[SMEM, ANY, VMEM, VMEM, VMEM] + [VMEM] * len(rest) + [ANY, VMEM, VMEM, VMEM] + [ANY] * 3,
            out_specs=[ANY] * (count + 3) + [VMEM] * 4,
            scratch_shapes=merged_scratch,
            compiler_params=params(3, 62),
        )(
            bounds, feed, resid, gain, cot, *rest, out_part, attn, q_all, h_cols,
            *(v.reshape(s) for v, s in zip(given, plan.shaped, strict=False)),
        )
        return plan.row_shards(done[:count]), done[-2], done[-1], done[-3]
    d_proj, d_resid, d_norm_gain = pl.pallas_call(
        functools.partial(norm_back_kernel, n_w, n_c),
        out_shape=[proj, d_resid, norm_gain],
        in_specs=[ANY, VMEM, VMEM, VMEM],
        out_specs=[ANY, VMEM, VMEM],
        scratch_shapes=[*norm_scratch, *norm_semaphores],
        compiler_params=params(5, 40),
    )(feed, resid, gain, cot)
    d_q_raw, d_low, d_x, d_query_gain, d_first_gain = pl.pallas_call(
        functools.partial(attend_back_kernel, n_w, n_c),
        out_shape=[d_q, shape_of(n_w, tokens, low), slope, query_gain, first_gain],
        in_specs=[SMEM] + [VMEM] * (2 + len(rest)),
        out_specs=[VMEM, ANY] + [VMEM] * 3,
        scratch_shapes=[*back_scratch, *back_semaphores],
        compiler_params=params(6, 60),
    )(bounds, d_proj, d_resid, *rest)
    pairs = ((attn, d_proj), (q_all, d_q_raw), (h_cols, d_low))
    terms = [*given, *(dot_tn(a, b.reshape(n_w * tokens, -1)).astype(BF) for a, b in pairs)]
    spread = [v.reshape(8, n_w, -1).swapaxes(0, 1) for v in (d_norm_gain, d_query_gain)]
    sums, gains, layer_output = sum_over_ctx(
        plan, terms, n_c, 4, jnp.concatenate(spread, axis=2), d_first_gain, out_part, resid
    )
    return sums, gains, layer_output, d_x


def tables(positions, width):
    exponent = jnp.arange(width // 2, dtype=F32) * (-2.0 / width)
    angles = positions.astype(F32)[..., None] * (10000.0**exponent)
    return jnp.cos(angles), jnp.sin(angles)


def whole_columns(part, rows):
    whole = lax.all_gather(part, "ctx", axis=1)
    return whole.reshape(rows, part.shape[-1])


def on_device(
    inputs,
    boundaries,
    first_gain,
    query_down,
    query_gain,
    query_up,
    key_weights,
    value_weights,
    output_weights,
    second_gain,
    gate_weights,
    up_weights,
    down_weights,
    cotangent,
):
    n_w, n_c, c = lax.axis_size("wt"), lax.axis_size("ctx"), lax.axis_index("ctx")
    width, half = inputs.shape[-1], inputs.shape[2]
    tokens, seqlen = 2 * half, 2 * half * n_c
    depth, rank = key_weights.shape[1], query_down.shape[1]
    hidden_cols = down_weights.shape[0]

    def for_columns(weight):
        rows = weight.shape[0] // n_c
        part = lax.dynamic_slice_in_dim(weight, c * rows, rows, 0)
        return part.reshape(rows, n_w, -1).swapaxes(0, 1)

    wide_bounds = jnp.zeros((8, 128), jnp.int32).at[0, : boundaries.shape[1]].set(boundaries[0])
    gains = jnp.concatenate([query_gain, second_gain]).astype(F32)
    gains = jnp.broadcast_to(gains[None], (8, gains.shape[0]))
    bounds, gains, up_part, gate_part, upper_part = exchange(
        [wide_bounds, gains, for_columns(query_up), for_columns(gate_weights), for_columns(up_weights)],
        (False, False, True, True, True), n_w, 0,
    )
    bounds = bounds[:, 0, : boundaries.shape[1]]
    gain_query = gains[:, 0, : rank // n_w].reshape(1, rank)
    gain_two = gains[:, 0, rank // n_w :].reshape(1, width)
    gain_one = first_gain.astype(F32)[None]
    up_cols = whole_columns(up_part, rank)
    gate_cols = whole_columns(gate_part, width)
    upper_cols = whole_columns(upper_part, width)

    ctx = jnp.stack([c - c % 2, c - c % 2 + 1])[:, None]
    offsets = jnp.arange(half, dtype=jnp.int32)[None]
    positions = jnp.concatenate([ctx * half + offsets, seqlen - (ctx + 1) * half + offsets], axis=1)
    cosine, sine = tables(positions, depth)
    x = inputs.reshape(tokens, width)
    cot = cotangent.reshape(tokens, width)
    h_cols, x_in, r_in, latent, q_all, kv, cot_all = first_part(
        n_w, n_c, x, cot, gain_one, gain_query, query_down, key_weights, value_weights,
        lax.dynamic_index_in_dim(cosine, c % 2, keepdims=False), lax.dynamic_index_in_dim(sine, c % 2, keepdims=False),
    )
    kv = kv.reshape(n_w // 2, seqlen, 2 * depth)
    queries, attn, resid, h_all = attend_part(
        n_w, n_c, bounds, q_all, up_cols, kv, cosine, sine, output_weights, x, gain_two
    )

    h_second = h_all.reshape(n_w * tokens, width)
    slope = cot_all.reshape(n_w * tokens, width)
    gate = dot(h_second, gate_cols)
    upper = dot(h_second, upper_cols)
    sigma = jax.nn.sigmoid(gate)
    silu = gate * sigma
    hidden = (silu * upper).astype(BF)
    d_hidden = dot_nt(slope, down_weights)
    d_gate = (d_hidden * upper * sigma * (1.0 + gate * (1.0 - sigma))).astype(BF)
    d_upper = (d_hidden * silu).astype(BF)
    out_part = dot(hidden, down_weights).astype(BF)
    d_down = dot_tn(hidden, slope).astype(BF)
    d_gate_weights = dot_tn(h_second, d_gate).astype(BF)
    d_up_weights = dot_tn(h_second, d_upper).astype(BF)
    feed = (dot_nt(d_gate, gate_cols) + dot_nt(d_upper, upper_cols)).astype(BF)

    def grouped(v):
        return v.reshape(n_w, tokens, v.shape[-1])

    def flat(v):
        return v.reshape(n_w * tokens, v.shape[-1])

    rest = (
        output_weights, queries, kv, cosine, sine, up_cols, latent, gain_query, query_down, key_weights, value_weights,
        x_in, r_in, gain_one, x,
    )
    given = (d_down, d_gate_weights, d_up_weights)
    shapes = [v.shape for v in given]
    shapes += [output_weights.shape, up_cols.shape, (query_down.shape[0], rank + 2 * depth)]
    sums, gains, layer_output, input_gradient = late_part(
        n_w, n_c, shapes, (False, True, True, False, True, False), bounds, (grouped(feed), resid, gain_two, cot), rest,
        grouped(out_part), given, flat(attn), flat(q_all), flat(h_cols),
    )
    *sums, firsts = sums
    d_down, d_gate_weights, d_up_weights, d_output, d_query_up = (s.astype(F32) for s in sums)
    one, two = width // n_w, 2 * (width // n_w)
    return (
        layer_output.reshape(inputs.shape),
        input_gradient.reshape(inputs.shape),
        gains[0, :one],
        firsts[:, :rank].astype(F32),
        gains[0, two:],
        d_query_up,
        firsts[:, rank : rank + depth].astype(F32),
        firsts[:, rank + depth :].astype(F32),
        d_output,
        gains[0, one:two],
        d_gate_weights,
        d_up_weights,
        d_down,
    )


def solution(mesh):
    token = P("wt", None, "ctx", None)
    row, vec = P("wt", None), P("wt")
    in_specs = (token, row, vec, row, vec, row, row, row, row, vec, row, row, row, token)
    out_specs = (token, token, vec, row, vec, row, row, row, row, vec, row, row, row)
    return jax.shard_map(
        on_device, mesh=mesh, in_specs=in_specs, out_specs=out_specs, check_vma=False
    )
```

```python
import functools
import math

import jax
import jax.numpy as jnp
from jax import lax
from jax.experimental import pallas as pl
from jax.experimental.pallas import tpu as pltpu
from jax.sharding import PartitionSpec as P

EPS = 1e-06
NEG = -1e30
F32 = jnp.float32
BF = jnp.bfloat16
VMEM = pl.BlockSpec(memory_space=pltpu.VMEM)
SMEM = pl.BlockSpec(memory_space=pltpu.SMEM)
ANY = pl.BlockSpec(memory_space=pl.ANY)
MIB = 1 << 20
MESH = pl.DeviceIdType.MESH


def dot(a, b):
    return jnp.dot(a, b, preferred_element_type=F32)


def dot_nt(a, b):
    return lax.dot_general(a, b, (((1,), (1,)), ((), ())), preferred_element_type=F32)


def dot_tn(a, b):
    return lax.dot_general(a, b, (((0,), (0,)), ((), ())), preferred_element_type=F32)


def inv_rms(v):
    return lax.rsqrt(jnp.mean(v * v, axis=-1, keepdims=True) + EPS)


def rms_back(slope, normal, scale):
    return scale * (slope - normal * jnp.mean(slope * normal, axis=-1, keepdims=True))


def rotate(v, cosine, sine):
    middle = v.shape[-1] // 2
    a, b = v[..., :middle], v[..., middle:]
    return jnp.concatenate([a * cosine - b * sine, b * cosine + a * sine], axis=-1)


def shape_of(*shape, dtype=BF):
    return jax.ShapeDtypeStruct(shape, dtype)


def params(collective, mib):
    return pltpu.CompilerParams(collective_id=collective, has_side_effects=True, vmem_limit_bytes=mib * MIB)


class Group:
    def __init__(self, n_w, n_c):
        self.n_w, self.n_z, self.per = n_w, n_c // 2, n_w // 2
        c, w = lax.axis_index("ctx"), lax.axis_index("wt")
        self.core = lax.rem(c, 2)
        self.z, self.w, self.base = c // 2, w, c - self.core
        self.home = w // self.per
        self.at_home = self.core == self.home
        self.stream = w - self.home * self.per
        self.slot = self.stream * 2 + self.core

    def target(self, j):
        return {"ctx": self.base + self.home, "wt": j}

    def source(self, i):
        return {"ctx": self.base + lax.rem(i, 2), "wt": self.core * self.per + i // 2}

    def column(self, step):
        return {"ctx": 2 * lax.rem(self.z + step, self.n_z) + self.core, "wt": self.w}

    def greet(self, column):
        barrier = pltpu.get_barrier_semaphore()
        others = [
            {"ctx": self.base + lax.rem(self.core + q, 2), "wt": lax.rem(self.w + r, self.n_w)}
            for q in range(2)
            for r in range(self.n_w)
        ][1:]
        if column:
            others += [{"ctx": 2 * lax.rem(self.z + s, self.n_z) + q, "wt": self.w} for s in range(1, self.n_z) for q in range(2)]
        for there in others:
            pl.semaphore_signal(barrier, inc=1, device_id=there, device_id_type=MESH)
        pl.semaphore_wait(barrier, len(others))


class Moves:
    def __init__(self, group, send, recv, passed=None):
        self.group, self.send, self.recv, self.passed = group, send, recv, passed
        self.relay = group.n_w == 4 and passed is not None
        self.across_x = group.w + 1 - 2 * lax.rem(group.w, 2)
        self.across_y = lax.rem(group.w + 2, 4)

    def start(self, kind, src, dst, there, index, slot, here):
        remote = pltpu.make_async_remote_copy(
            src_ref=src, dst_ref=dst, send_sem=self.send.at[kind, index], recv_sem=self.recv.at[kind, slot],
            device_id=there, device_id_type=MESH,
        )
        local = pltpu.make_async_copy(src, dst, self.recv.at[kind, slot])
        pl.when(jnp.logical_not(here))(remote.start)
        pl.when(here)(local.start)

    def to_target(self, kind, j, src, dst):
        g = self.group
        self.start(kind, src, dst, g.target(j), j, g.slot, g.at_home & (g.w == j))

    def to_source(self, kind, i, src, dst):
        g = self.group
        self.start(kind, src, dst, g.source(i), i, g.w, g.at_home & (g.slot == i))

    def gather(self, kind, src, dst):
        g = self.group
        for j in range(g.n_w):
            start = functools.partial(self.to_target, kind, j, src, dst)
            if self.relay:
                pl.when(g.w != g.n_w - 1 - j)(start)
            else:
                start()

    def relayed(self, kind, part, i, dst):
        g = self.group
        there = self.across_y if part == 0 else self.across_x
        return pltpu.make_async_remote_copy(
            src_ref=dst, dst_ref=dst, send_sem=self.passed.at[kind, i], recv_sem=self.recv.at[kind, i],
            device_id={"ctx": g.base + g.core, "wt": there}, device_id_type=MESH,
        )

    def passes(self, part, i):
        origin = self.group.core * self.group.per + i // 2
        return origin == (self.across_x if part == 0 else self.across_y)

    def pass_on(self, kinds):
        g = self.group
        if not self.relay:
            for kind, _, dst in kinds:
                for i in range(g.n_w):
                    self.arrived(kind, i, dst(i))
            return
        for far in (False, True):
            for kind, part, dst in kinds:
                for i in range(g.n_w):
                    opposite = g.core * g.per + i // 2 == g.n_w - 1 - g.w
                    wait = functools.partial(self.arrived, kind, i, dst(i))
                    pl.when(opposite if far else jnp.logical_not(opposite))(wait)
                    if not far:
                        pl.when(self.passes(part, i))(self.relayed(kind, part, i, dst(i)).start)

    def gathered(self, kind, part, src, dst):
        g = self.group
        if not self.relay:
            self.sent(kind, lambda j: src, True)
            return
        for i in range(g.n_w):
            copy = pltpu.make_async_remote_copy(
                src_ref=src, dst_ref=src, send_sem=self.send.at[kind, i], recv_sem=self.recv.at[kind, i],
                device_id=g.target(i), device_id_type=MESH,
            )
            skip = (g.at_home & (g.w == i)) | (g.w == g.n_w - 1 - i)
            pl.when(jnp.logical_not(skip))(copy.wait_send)
            pl.when(self.passes(part, i))(self.relayed(kind, part, i, dst(i)).wait_send)

    def arrived(self, kind, index, dst):
        pltpu.make_async_copy(dst, dst, self.recv.at[kind, index]).wait()

    def sent(self, kind, src, by_target):
        g = self.group
        for i in range(g.n_w):
            at = src(i)
            copy = pltpu.make_async_remote_copy(
                src_ref=at, dst_ref=at, send_sem=self.send.at[kind, i], recv_sem=self.recv.at[kind, i],
                device_id=g.target(i) if by_target else g.source(i), device_id_type=MESH,
            )
            here = g.at_home & ((g.w if by_target else g.slot) == i)
            pl.when(jnp.logical_not(here))(copy.wait_send)


class Loads:
    def __init__(self, operands, buffers, sems):
        self.copies = [
            pltpu.make_async_copy(src, dst, sems.at[i]) for i, (src, dst) in enumerate(zip(operands, buffers, strict=True))
        ]
        for copy in self.copies:
            copy.start()

    def wait(self, *which):
        for i in which:
            self.copies[i].wait()


def vmem_like(arrays):
    return [pltpu.VMEM(v.shape, v.dtype) for v in arrays]


def column_copy(group, part, step, src, dst, send, recv):
    return pltpu.make_async_remote_copy(
        src_ref=src, dst_ref=dst, send_sem=send.at[part, step], recv_sem=recv.at[part, step],
        device_id=group.column(step), device_id_type=MESH,
    )


def exchange_kernel(n_w, split, *refs):
    count = len(split)
    ins, outs = refs[:count], refs[count : 2 * count]
    send, recv, local = refs[2 * count :]
    c, w = lax.axis_index("ctx"), lax.axis_index("wt")
    barrier = pltpu.get_barrier_semaphore()
    for step in range(1, n_w):
        pl.semaphore_signal(
            barrier, inc=1, device_id={"ctx": c, "wt": lax.rem(w + step, n_w)}, device_id_type=MESH
        )
    pl.semaphore_wait(barrier, n_w - 1)
    copies = []
    for a in range(count):
        for step in range(1, n_w):
            there = lax.rem(w + step, n_w)
            copies.append(
                pltpu.make_async_remote_copy(
                    src_ref=ins[a].at[there] if split[a] else ins[a], dst_ref=outs[a].at[w],
                    send_sem=send.at[a, step], recv_sem=recv.at[a, step],
                    device_id={"ctx": c, "wt": there}, device_id_type=MESH,
                )
            )
        copies.append(pltpu.make_async_copy(ins[a].at[w] if split[a] else ins[a], outs[a].at[w], local.at[a]))
    for copy in copies:
        copy.start()
    for copy in copies:
        copy.wait()


def exchange(arrays, split, n_w, collective):
    return pl.pallas_call(
        functools.partial(exchange_kernel, n_w, split),
        out_shape=[
            jax.ShapeDtypeStruct(v.shape if s else (n_w, *v.shape), v.dtype) for v, s in zip(arrays, split, strict=True)
        ],
        in_specs=[ANY] * len(arrays),
        out_specs=[ANY] * len(arrays),
        scratch_shapes=[
            pltpu.SemaphoreType.DMA((len(arrays), n_w)),
            pltpu.SemaphoreType.DMA((len(arrays), n_w)),
            pltpu.SemaphoreType.DMA((len(arrays),)),
        ],
        compiler_params=params(collective, 16),
    )(*arrays)


def first_kernel(
    n_w, n_c,
    x_ref, cot_ref, gain_ref, query_gain_ref, down_ref, key_ref, value_ref, cos_ref, sin_ref,
    h_out, x_out, r_out, latent_out, q_all, kv_all, cot_all,
    x_in, r_in, r_own, parts, low, q_own, kv_own, kv_column, down_own, key_own, value_own,
    send, recv, passed, z_send, z_recv, loaded,
):
    g = Group(n_w, n_c)
    m = Moves(g, send, recv, passed)
    loads = Loads([down_ref, key_ref, value_ref], [down_own, key_own, value_own], loaded)
    down_ref, key_ref, value_ref = down_own, key_own, value_own
    tokens, cols = x_in.shape[1:]
    rank, depth = down_ref.shape[1], key_ref.shape[1]
    r_own[...] = jnp.broadcast_to(inv_rms(x_ref[...].astype(F32)), r_own.shape)
    g.greet(True)
    for j in range(n_w):
        m.to_target(0, j, x_ref.at[:, pl.ds(j * cols, cols)], x_in.at[g.slot])
        m.to_target(1, j, r_own, r_in.at[g.slot])

    loads.wait(0, 1, 2)
    for i in range(n_w):
        m.arrived(0, i, x_in.at[i])
        m.arrived(1, i, r_in.at[i])
        x_out[i] = x_in[i]
        r_out[i] = r_in[i]
        h = (x_in[i].astype(F32) * r_in[i, :, :1] * gain_ref[...]).astype(BF)
        h_out[i] = h
        parts[i, :, :rank] = dot(h, down_ref[...]).astype(BF)
        parts[i, :, rank : rank + depth] = dot(h, key_ref[...]).astype(BF)
        parts[i, :, rank + depth :] = dot(h, value_ref[...]).astype(BF)
        m.to_source(2, i, parts.at[i], low.at[g.w])

    for j in range(n_w):
        m.arrived(2, j, low.at[j])
    total = low[0].astype(F32)
    for j in range(1, n_w):
        total += low[j].astype(F32)
    keys = rotate(total[:, rank : rank + depth], cos_ref[...], sin_ref[...]).astype(BF)
    kv = jnp.concatenate([keys, total[:, rank + depth :].astype(BF)], axis=1)
    half = tokens // 2
    mirror = g.n_z - 1 - g.z
    for part in range(2):
        kv_own[part] = kv[part * half : (part + 1) * half]

    def over_z(part, step):
        return column_copy(
            g, part, step, kv_own.at[part], kv_column.at[part, mirror if part else g.z], z_send, z_recv
        )

    for step in range(1, g.n_z):
        for part in range(2):
            over_z(part, step).start()
    kv_column[0, g.z] = kv_own[0]
    kv_column[1, mirror] = kv_own[1]
    latent = total[:, :rank]
    latent_out[...] = latent
    q_own[...] = (latent * inv_rms(latent) * query_gain_ref[...]).astype(BF)

    def rows(ref, part, *lead):
        return ref.at[(*lead, pl.ds(part * half, half))]

    def kv_place(part, stream, core):
        return kv_all.at[stream, part, :, 1 - core if part else core]

    for part in range(2):
        m.gather(3 + part, rows(q_own, part), rows(q_all, part, g.slot))
    for part in range(2):
        m.gather(5 + part, rows(cot_ref, part), rows(cot_all, part, g.slot))
    for step in range(1, g.n_z):
        for part in range(2):
            over_z(part, step).wait_recv()
    for part in range(2):
        m.gather(7 + part, kv_column.at[part], kv_place(part, g.stream, g.core))
    gathers = [(3 + part, part, functools.partial(rows, q_all, part)) for part in range(2)]
    gathers += [(5 + part, part, functools.partial(rows, cot_all, part)) for part in range(2)]
    gathers += [(7 + part, part, lambda i, part=part: kv_place(part, i // 2, i % 2)) for part in range(2)]
    m.pass_on(gathers)
    m.sent(0, lambda j: x_ref.at[:, pl.ds(j * cols, cols)], True)
    m.sent(1, lambda j: r_own, True)
    m.sent(2, lambda i: parts.at[i], False)
    for part in range(2):
        for kind, src in ((3, rows(q_own, part)), (5, rows(cot_ref, part)), (7, kv_column.at[part])):
            m.gathered(kind + part, part, src, gathers[kind + part - 3][2])
        for step in range(1, g.n_z):
            over_z(part, step).wait_send()


def first_part(n_w, n_c, x, cot, gain, query_gain, down, key, value, cosine, sine):
    tokens, width = x.shape
    cols, rank, depth = width // n_w, down.shape[1], key.shape[1]
    n_z, half, low = n_c // 2, tokens // 2, rank + 2 * depth
    return pl.pallas_call(
        functools.partial(first_kernel, n_w, n_c),
        out_shape=[
            shape_of(n_w, tokens, cols),
            shape_of(n_w, tokens, cols),
            shape_of(n_w, tokens, 128, dtype=F32),
            shape_of(tokens, rank, dtype=F32),
            shape_of(n_w, tokens, rank),
            shape_of(n_w // 2, 2, n_z, 2, half, 2 * depth),
            shape_of(n_w, tokens, width),
        ],
        in_specs=[VMEM, ANY, VMEM, VMEM, ANY, ANY, ANY, VMEM, VMEM],
        out_specs=[VMEM] * 4 + [ANY] * 3,
        scratch_shapes=[
            pltpu.VMEM((n_w, tokens, cols), BF),
            pltpu.VMEM((n_w, tokens, 128), F32),
            pltpu.VMEM((tokens, 128), F32),
            pltpu.VMEM((n_w, tokens, low), BF),
            pltpu.VMEM((n_w, tokens, low), BF),
            pltpu.VMEM((tokens, rank), BF),
            pltpu.VMEM((2, half, 2 * depth), BF),
            pltpu.VMEM((2, n_z, half, 2 * depth), BF),
            *vmem_like((down, key, value)),
            *[pltpu.SemaphoreType.DMA((9, n_w))] * 3,
            pltpu.SemaphoreType.DMA((2, n_z)),
            pltpu.SemaphoreType.DMA((2, n_z)),
            pltpu.SemaphoreType.DMA((3,)),
        ],
        compiler_params=params(1, 60),
    )(x, cot, gain, query_gain, down, key, value, cosine, sine)


def visible_keys(bounds_ref, stream, c, tokens, seqlen):
    half = tokens // 2
    row = lax.broadcasted_iota(jnp.int32, (tokens, 1), 0)
    pos = row + jnp.where(row < half, c * half, seqlen - (c + 1) * half - half)
    begin = jnp.zeros((tokens, 1), jnp.int32)
    for j in range(bounds_ref.shape[1]):
        start = bounds_ref[stream, j]
        begin = jnp.where(pos >= start, jnp.maximum(begin, start), begin)
    key = lax.broadcasted_iota(jnp.int32, (tokens, seqlen), 1)
    return (key >= begin) & (key <= pos)


def probabilities(q, keys, visible):
    scores = jnp.where(visible, dot_nt(q, keys), NEG)
    peak = jnp.max(scores, axis=-1, keepdims=True)
    weight = jnp.where(visible, jnp.exp(scores - peak), 0.0)
    return weight * (1.0 / jnp.sum(weight, axis=-1, keepdims=True))


def attend_kernel(
    n_w, n_c,
    bounds_ref, q_ref, up_ref, kv_ref, cos_ref, sin_ref, out_ref, x_ref, gain_ref,
    queries, attn, resid, h_all,
    parts, land, h_own, q_own, up_own, kv_own, out_own, send, recv, passed, loaded,
):
    g = Group(n_w, n_c)
    m = Moves(g, send, recv, passed)
    loads = Loads([q_ref, up_ref, kv_ref, out_ref], [q_own, up_own, kv_own, out_own], loaded)
    q_ref, up_ref, kv_ref, out_ref = q_own, up_own, kv_own, out_own
    tokens, seqlen, depth = q_ref.shape[1], kv_ref.shape[1], kv_ref.shape[2] // 2
    scale = 1.0 / math.sqrt(depth)
    g.greet(False)

    def one(i, carry):
        stream, core = i // 2, lax.rem(i, 2)
        visible = visible_keys(bounds_ref, g.core * g.per + stream, g.base + core, tokens, seqlen)
        raw = dot(q_ref[i], up_ref[...])
        for cut in range(0, up_ref.shape[1], depth):
            span = slice(cut, cut + depth)
            q = (rotate(raw[:, span], cos_ref[core], sin_ref[core]) * scale).astype(BF)
            queries[i, :, span] = q
            probs = probabilities(q, kv_ref[stream, :, :depth], visible).astype(BF)
            attn[i, :, span] = dot(probs, kv_ref[stream, :, depth:]).astype(BF)
        parts[i] = dot(attn[i], out_ref[...]).astype(BF)
        m.to_source(0, i, parts.at[i], land.at[g.w])
        return carry

    loads.wait(0, 1, 2, 3)
    lax.fori_loop(0, n_w, one, 0)
    total = x_ref[...].astype(F32)
    for j in range(n_w):
        m.arrived(0, j, land.at[j])
        total += land[j].astype(F32)
    resid[...] = total
    h_own[...] = (total * inv_rms(total) * gain_ref[...]).astype(BF)
    half = tokens // 2

    def rows(ref, part, *lead):
        return ref.at[(*lead, pl.ds(part * half, half))]

    gathers = [(1 + part, part, functools.partial(rows, h_all, part)) for part in range(2)]
    for part in range(2):
        m.gather(1 + part, rows(h_own, part), rows(h_all, part, g.slot))
    m.pass_on(gathers)
    m.sent(0, lambda i: parts.at[i], False)
    for part in range(2):
        m.gathered(1 + part, part, rows(h_own, part), gathers[part][2])


def attend_part(n_w, n_c, bounds, q_all, up_cols, kv, cosine, sine, output, x, gain):
    tokens, width = x.shape
    features = up_cols.shape[1]
    return pl.pallas_call(
        functools.partial(attend_kernel, n_w, n_c),
        out_shape=[
            shape_of(n_w, tokens, features),
            shape_of(n_w, tokens, features),
            shape_of(tokens, width, dtype=F32),
            shape_of(n_w, tokens, width),
        ],
        in_specs=[SMEM, ANY, ANY, ANY, VMEM, VMEM, ANY, VMEM, VMEM],
        out_specs=[VMEM] * 3 + [ANY],
        scratch_shapes=[
            pltpu.VMEM((n_w, tokens, width), BF),
            pltpu.VMEM((n_w, tokens, width), BF),
            pltpu.VMEM((tokens, width), BF),
            *vmem_like((q_all, up_cols, kv, output)),
            *[pltpu.SemaphoreType.DMA((3, n_w))] * 3,
            pltpu.SemaphoreType.DMA((4,)),
        ],
        compiler_params=params(2, 60),
    )(bounds, q_all, up_cols, kv, cosine, sine, output, x, gain)


class Plan:
    def __init__(self, shapes, turned, n_w, slots, limit):
        self.n_w, self.arrays, self.turned = n_w, shapes, turned
        self.wide = all(cols % 128 == 0 for (_, cols), turn in zip(shapes, turned, strict=True) if turn)
        self.shaped, self.pieces, self.members, self.ring_shapes = [], [], [[], []], [None, None]
        for (rows, cols), turn in zip(shapes, turned, strict=True):
            self.shaped.append((n_w, 2, 2, rows // n_w // 4, cols) if turn else (2, 2, rows // 4, cols))
        for kind in range(2):
            mine = [v for v, turn in zip(self.shaped, turned, strict=True) if turn == bool(kind)]
            if mine:
                lead, cols = (n_w, 2) if kind else (2,), max(v[-1] for v in mine)
                rows = 16
                common = math.gcd(*(v[-2] for v in mine))
                for more in range(16, common + 1, 16):
                    if common % more == 0 and math.prod(lead) * more * cols * 2 <= limit:
                        rows = more
                self.ring_shapes[kind] = (*lead, rows, cols)
        for a, (v, turn) in enumerate(zip(self.shaped, turned, strict=True)):
            rows = self.ring_shapes[int(turn)][-2]
            for row in range(0, v[-2], rows):
                self.members[int(turn)].append(len(self.pieces))
                self.pieces.append((a, int(turn), len(self.members[int(turn)]) - 1, row, rows, v[-1]))
        self.slots = [min(slots, len(members)) for members in self.members]

    def __len__(self):
        return len(self.pieces)

    def slot(self, q):
        return self.pieces[q][2] % self.slots[self.pieces[q][1]]

    def before(self, q):
        _, kind, index = self.pieces[q][:3]
        return self.members[kind][index - self.slots[kind]] if index >= self.slots[kind] else None

    def after(self, q):
        _, kind, index = self.pieces[q][:3]
        later = index + self.slots[kind]
        return self.members[kind][later] if later < len(self.members[kind]) else None

    def scratch(self):
        shapes = [v or (16, 128) for v in self.ring_shapes]
        slots = [max(v, 1) for v in self.slots]
        rings = [pltpu.VMEM((n, *v), BF) for n, v in zip(slots, shapes, strict=True)]
        rows, turned = shapes
        halves = [pltpu.VMEM((slots[0], *rows[-2:]), BF), pltpu.VMEM((slots[1], self.n_w, *turned[-2:]), BF)]
        moved = (turned[-2], self.n_w * turned[-1]) if self.wide else (self.n_w, *turned[-2:])
        kinds, count = 5 + self.n_w, len(self)
        return [
            *rings, *rings, *rings, *halves, pltpu.VMEM((slots[1], *moved), BF),
            pltpu.SemaphoreType.DMA((count,)),
            pltpu.SemaphoreType.DMA((count,)),
            pltpu.SemaphoreType.DMA((kinds, count)),
            pltpu.SemaphoreType.DMA((kinds, count)),
            pltpu.SemaphoreType.REGULAR((4, count)),
        ]

    def out_shapes(self):
        return [
            shape_of(2, 2, v[-2], self.n_w * v[-1]) if turn and self.wide else shape_of(*v)
            for v, turn in zip(self.shaped, self.turned, strict=True)
        ]

    def row_shards(self, sums):
        done = []
        for s, (rows, cols), turn in zip(sums, self.arrays, self.turned, strict=True):
            if self.wide or not turn:
                done.append(s.reshape(-1, s.shape[-1]))
            else:
                done.append(s.reshape(self.n_w, rows // self.n_w, cols).swapaxes(0, 1).reshape(rows // self.n_w, -1))
        return done


CHAIN_SCRATCH = 14


class Chain:
    AHEAD, LEAD, HALF, MOVE, DONE, LAG = 2, 3, 1, 2, 3, 9

    def __init__(self, plan, n_c, terms, outs, scratch):
        self.plan, self.n_w, self.terms, self.outs = plan, plan.n_w, terms, outs
        self.own, self.mates, self.ups, self.halves = (scratch[2 * i : 2 * i + 2] for i in range(4))
        self.moved, self.load, self.place, self.send, self.recv, self.credit = scratch[8:]
        c, w = lax.axis_index("ctx"), lax.axis_index("wt")
        chain, k = n_c // 2, c // 2
        self.w, self.core = w, lax.rem(c, 2)
        left = k < chain // 2
        self.side = jnp.where(left, 0, 1)
        far = jnp.where(left, k, chain - 1 - k)
        self.middle, self.outside = far == chain // 2 - 1, far > 0
        self.mate = {"ctx": c + 1 - 2 * self.core, "wt": w}
        self.inner = {"ctx": jnp.where(left, c + 2, c - 2), "wt": w}
        self.outer = {"ctx": jnp.where(left, c - 2, c + 2), "wt": w}
        self.peers = [{"ctx": c, "wt": lax.rem(w + r, self.n_w)} for r in range(1, self.n_w)]
        self.now, self.ready = 0, len(plan)

    def turned(self, q):
        return self.plan.turned[self.plan.pieces[q][0]]

    def every(self, q):
        return (slice(None),) if self.turned(q) else ()

    def term(self, q, core):
        a, _, _, row, rows, _ = self.plan.pieces[q]
        return self.terms[a].at[(*self.every(q), core, slice(None), pl.ds(row, rows))]

    def fitting(self, q, buffer):
        cols = self.plan.pieces[q][5]
        lead = (slice(None),) * (len(buffer.shape) - 2)
        return buffer.at[(self.plan.slot(q), *lead, pl.ds(0, cols))]

    def ring(self, q, buffers):
        return self.fitting(q, buffers[self.plan.pieces[q][1]])

    def half_buffer(self, q):
        return self.ring(q, self.halves)

    def remote(self, kind, q, src, dst, there):
        return pltpu.make_async_remote_copy(
            src_ref=src, dst_ref=dst, send_sem=self.send.at[kind, q], recv_sem=self.recv.at[kind, q], device_id=there,
            device_id_type=MESH,
        )

    def own_load(self, q):
        return pltpu.make_async_copy(self.term(q, self.core), self.ring(q, self.own), self.load.at[q])

    def to_mate(self, q):
        return self.remote(0, q, self.term(q, 1 - self.core), self.ring(q, self.mates), self.mate)

    def along(self, q, there):
        return self.remote(1, q, self.ring(q, self.own), self.ring(q, self.ups), there)

    def to_across(self, q):
        side = self.ring(q, self.own).at[(*self.every(q), 1 - self.side)]
        return self.remote(5, q, side, self.half_buffer(q), self.inner)

    def moved_part(self, q, source):
        cols = self.plan.pieces[q][5]
        if not self.plan.wide:
            return self.moved.at[self.plan.slot(q), source, :, pl.ds(0, cols)]
        return self.moved.at[self.plan.slot(q), :, pl.ds(pl.multiple_of(source * cols, 128), cols)]

    def to_peer(self, q, r, slot):
        there = self.peers[r]
        return self.remote(6 + r, q, self.half_buffer(q).at[there["wt"]], self.moved_part(q, slot), there)

    def finished(self, q):
        if not self.turned(q):
            return self.half_buffer(q)
        if self.plan.wide:
            return self.moved.at[self.plan.slot(q), :, pl.ds(0, self.n_w * self.plan.pieces[q][5])]
        return self.fitting(q, self.moved)

    def result(self, q, *lead):
        a, kind, _, row, rows, _ = self.plan.pieces[q]
        every = () if self.plan.wide else self.every(q)
        return self.outs[a].at[(*every, *lead, pl.ds(row, rows))]

    def half_place(self, q):
        return pltpu.make_async_copy(self.finished(q), self.result(q, self.core, self.side), self.place.at[q])

    def half_across(self, q, side):
        return self.remote(2, q, self.finished(q), self.result(q, self.core, side), self.inner)

    def down(self, kind, q, there):
        here = self.result(q, self.core, slice(None))
        return self.remote(kind, q, here, here, there)

    def add(self, q, ins, out):
        rows = out.shape[-2]
        step = 16 if rows % 16 == 0 else rows
        lead = (slice(None),) * (len(out.shape) - 2)

        def body(i, carry):
            at = (*lead, pl.ds(i * step, step))
            total = ins[0][at].astype(F32)
            for ref in ins[1:]:
                total += ref[at].astype(F32)
            out[at] = total.astype(BF)
            return carry

        lax.fori_loop(0, rows // step, body, 0)

    def grant(self, kind, q, there):
        pl.semaphore_signal(self.credit.at[kind, q], inc=1, device_id=there, device_id_type=MESH)

    def prefetch(self, q):
        before = self.plan.before(q)
        if before is not None:
            pl.when(self.middle)(self.to_across(before).wait_send)
            pl.when(jnp.logical_not(self.middle))(self.along(before, self.inner).wait_send)
            pl.semaphore_wait(self.credit.at[0, q], 1)
        self.own_load(q).start()
        self.to_mate(q).start()

    def up(self, q):
        self.own_load(q).wait()
        self.to_mate(q).wait_recv()
        after, before = self.plan.after(q), self.plan.before(q)
        own, mates, ups = (self.ring(q, b) for b in (self.own, self.mates, self.ups))

        @pl.when(self.outside)
        def _():
            self.along(q, self.outer).wait_recv()
            self.add(q, [own, mates, ups], own)
            if after is not None:
                self.grant(1, after, self.outer)

        @pl.when(jnp.logical_not(self.outside))
        def _():
            self.add(q, [own, mates], own)

        if after is not None:
            self.grant(0, after, self.mate)

        @pl.when(self.middle)
        def _():
            if before is not None:
                pl.semaphore_wait(self.credit.at[2, q], 1)
            self.to_across(q).start()

        @pl.when(jnp.logical_not(self.middle))
        def _():
            if before is not None:
                pl.semaphore_wait(self.credit.at[1, q], 1)
            self.along(q, self.inner).start()

    def finish_half(self, q):
        self.to_across(q).wait_recv()
        half = self.half_buffer(q)
        self.add(q, [self.ring(q, self.own).at[(*self.every(q), self.side)], half], half)
        if self.turned(q):
            if self.plan.before(q) is not None:
                pl.semaphore_wait(self.credit.at[3, q], self.n_w - 1)
            for r in range(self.n_w - 1):
                self.to_peer(q, r, self.w).start()
            self.moved_part(q, self.w)[...] = half[self.w]
        else:
            self.spread(q)

    def spread(self, q):
        self.half_place(q).start()
        self.half_across(q, self.side).start()

    def move(self, q):
        if self.turned(q):
            for r in range(self.n_w - 1):
                self.to_peer(q, r, lax.rem(self.w + self.n_w - r - 1, self.n_w)).wait_recv()
            self.spread(q)

    def pass_down(self, q):
        pl.when(self.outside)(self.down(3, q, self.outer).start)
        self.down(4, q, self.mate).start()

    def free(self, q):
        after = self.plan.after(q)
        if after is not None:
            self.half_across(q, self.side).wait_send()
            if self.turned(q):
                for r in range(self.n_w - 1):
                    self.to_peer(q, r, self.w).wait_send()
                for there in self.peers:
                    self.grant(3, after, there)
            self.grant(2, after, self.inner)

    def tick(self):
        t, count = self.now, len(self.plan)
        self.now += 1
        inside, outside = self.middle, jnp.logical_not(self.middle)

        @pl.when(outside)
        def _():
            if t == 0:
                for q in range(min(self.AHEAD, count)):
                    self.prefetch(q)
            for q in range(0 if t == 0 else t + self.LEAD, t + self.LEAD + 1):
                if q < count:
                    self.up(q)
                if q + self.AHEAD < count:
                    self.prefetch(q + self.AHEAD)
            if 0 <= t - self.LAG < count:
                self.down(3, t - self.LAG, self.inner).wait_recv()
                self.pass_down(t - self.LAG)

        @pl.when(inside)
        def _():
            if t == 0:
                for q in range(min(self.AHEAD, count)):
                    self.prefetch(q)
            if t < count:
                self.up(t)
            if 0 <= t - self.HALF < count:
                self.finish_half(t - self.HALF)
            if 0 <= t - self.MOVE < count:
                self.move(t - self.MOVE)
            done = t - self.DONE
            if 0 <= done < count:
                self.half_place(done).wait()
                self.half_across(done, 1 - self.side).wait_recv()
                self.pass_down(done)
                self.free(done)
            if t + self.AHEAD < count:
                self.prefetch(t + self.AHEAD)

    def ticks(self, number):
        for _ in range(number):
            if self.now + self.AHEAD + self.LEAD < self.ready or self.now < len(self.plan) + self.LAG and self.ready == len(self.plan):
                self.tick()

    def have(self, arrays):
        self.ready = sum(piece[0] < arrays for piece in self.plan.pieces)

    def finish(self):
        self.ticks(len(self.plan) + self.LAG)
        for q in range(len(self.plan)):
            last = self.plan.after(q) is None

            @pl.when(self.middle)
            def _():
                if last:
                    self.to_across(q).wait_send()
                    self.half_across(q, self.side).wait_send()
                    for r in range(self.n_w - 1 if self.turned(q) else 0):
                        self.to_peer(q, r, self.w).wait_send()

            if last:
                pl.when(jnp.logical_not(self.middle))(self.along(q, self.inner).wait_send)
            self.to_mate(q).wait_send()
            pl.when(self.outside)(self.down(3, q, self.outer).wait_send)
            other = self.result(q, 1 - self.core, slice(None))
            self.remote(4, q, other, other, self.mate).wait_recv()
            self.down(4, q, self.mate).wait_send()


class Small:
    def __init__(self, group, n_c, moves, terms, first_terms, layer_terms, resid, out, layer_out, layer_land, scratch):
        self.g, self.n_c, self.m = group, n_c, moves
        self.terms, self.first_terms, self.layer_terms, self.resid = terms, first_terms, layer_terms, resid
        self.out, self.layer_out, self.layer_land = out, layer_out, layer_land
        self.land, self.own, self.all, self.send, self.recv = scratch
        self.c = lax.axis_index("ctx")

    def block(self, step):
        n_w, j = self.g.n_w, lax.rem(self.g.w + step, self.g.n_w)
        return pltpu.make_async_remote_copy(
            src_ref=self.terms.at[j], dst_ref=self.land.at[step], send_sem=self.send.at[step],
            recv_sem=self.recv.at[step], device_id={"ctx": self.c, "wt": j}, device_id_type=MESH,
        )

    def total(self, step):
        at = self.g.n_w + step
        return pltpu.make_async_remote_copy(
            src_ref=self.own, dst_ref=self.all.at[step], send_sem=self.send.at[at], recv_sem=self.recv.at[at],
            device_id={"ctx": lax.rem(self.c + step, self.n_c), "wt": self.g.w}, device_id_type=MESH,
        )

    def begin(self):
        for step in range(1, self.g.n_w):
            self.block(step).start()
        for i in range(self.g.n_w):
            self.m.to_source(0, i, self.layer_terms.at[i], self.layer_land.at[self.g.w])

    def middle(self):
        first = self.first_terms.shape[1]
        total = self.terms[self.g.w]
        for step in range(1, self.g.n_w):
            self.block(step).wait_recv()
            total += self.land[step]
        self.own[:, :first] = self.first_terms[...]
        self.own[:, first:] = total
        for step in range(1, self.n_c):
            self.total(step).start()
        total = self.resid[...]
        for j in range(self.g.n_w):
            self.m.arrived(0, j, self.layer_land.at[j])
            total += self.layer_land[j].astype(F32)
        self.layer_out[...] = total.astype(BF)

    def end(self):
        total = self.own[...]
        for step in range(1, self.n_c):
            self.total(step).wait_recv()
            total += self.all[step]
        self.out[...] = total
        for step in range(1, self.g.n_w):
            self.block(step).wait_send()
        for step in range(1, self.n_c):
            self.total(step).wait_send()
        self.m.sent(0, lambda i: self.layer_terms.at[i], False)


SMALL_SCRATCH = 5


def small_scratch(n_w, n_c, width, first):
    return [
        pltpu.VMEM((n_w, 8, width), F32),
        pltpu.VMEM((8, width + first), F32),
        pltpu.VMEM((n_c, 8, width + first), F32),
        pltpu.SemaphoreType.DMA((n_w + n_c,)),
        pltpu.SemaphoreType.DMA((n_w + n_c,)),
    ]


def sum_kernel(plan, n_c, *refs):
    count = len(plan.arrays)
    terms, (gain_terms, first_terms, layer_terms, resid_ref), refs = refs[:count], refs[count : count + 4], refs[count + 4 :]
    outs, (gains_out, layer_out), refs = refs[:count], refs[count : count + 2], refs[count + 2 :]
    layer_land, group_send, group_recv = refs[CHAIN_SCRATCH + SMALL_SCRATCH :]
    g = Group(plan.n_w, n_c)
    chain = Chain(plan, n_c, terms, outs, refs[:CHAIN_SCRATCH])
    small = Small(
        g, n_c, Moves(g, group_send, group_recv), gain_terms, first_terms, layer_terms, resid_ref, gains_out, layer_out,
        layer_land, refs[CHAIN_SCRATCH : CHAIN_SCRATCH + SMALL_SCRATCH],
    )
    g.greet(True)
    chain.ticks(2)
    small.begin()
    chain.ticks(4)
    small.middle()
    chain.finish()
    small.end()


def sum_over_ctx(plan, terms, n_c, collective, gain_terms, first_terms, layer_terms, resid):
    n_w, count = plan.n_w, len(plan.arrays)
    width, first = gain_terms.shape[-1], first_terms.shape[-1]
    sums = pl.pallas_call(
        functools.partial(sum_kernel, plan, n_c),
        out_shape=[*plan.out_shapes(), shape_of(8, width + first, dtype=F32), shape_of(*resid.shape)],
        in_specs=[ANY] * count + [VMEM, VMEM, ANY, VMEM],
        out_specs=[ANY] * count + [VMEM, VMEM],
        scratch_shapes=[
            *plan.scratch(),
            *small_scratch(n_w, n_c, width, first),
            pltpu.VMEM(layer_terms.shape, BF),
            pltpu.SemaphoreType.DMA((1, n_w)),
            pltpu.SemaphoreType.DMA((1, n_w)),
        ],
        compiler_params=params(collective, 60),
    )(*(v.reshape(s) for v, s in zip(terms, plan.shaped, strict=True)), gain_terms, first_terms, layer_terms, resid)
    return plan.row_shards(sums[:count]), sums[-2], sums[-1]


def norm_back(g, m, feed_ref, resid_ref, gain_ref, cot_ref, land, proj_own, proj_in, d_resid, d_gain, ticks):
    for i in range(g.n_w):
        m.to_source(0, i, feed_ref.at[i], land.at[g.w])
    ticks(3)
    for j in range(g.n_w):
        m.arrived(0, j, land.at[j])
    d_h = land[0].astype(F32)
    for j in range(1, g.n_w):
        d_h += land[j].astype(F32)
    resid = resid_ref[...]
    scale = inv_rms(resid)
    normal = resid * scale
    d_gain[...] = jnp.broadcast_to(jnp.sum(d_h * normal, axis=0, keepdims=True), d_gain.shape)
    total = cot_ref[...].astype(F32) + rms_back(d_h * gain_ref[...], normal, scale)
    d_resid[...] = total
    proj_own[...] = total.astype(BF)
    for j in range(g.n_w):
        m.to_target(1, j, proj_own, proj_in.at[g.slot])
    ticks(3)
    for i in range(g.n_w):
        m.arrived(1, i, proj_in.at[i])


def norm_back_ends(m, feed_ref, proj_own):
    m.sent(0, lambda i: feed_ref.at[i], False)
    m.sent(1, lambda j: proj_own, True)


NORM_SEMAPHORES, BACK_SEMAPHORES = 2, 6
LOADED = (0, 1, 2, 5, 8, 9, 10, 11, 12, 15, 16, 17)


def norm_back_kernel(
    n_w, n_c, feed_ref, resid_ref, gain_ref, cot_ref, proj_all, d_resid, d_gain, land, proj_own, send, recv
):
    g = Group(n_w, n_c)
    m = Moves(g, send, recv)
    g.greet(False)
    norm_back(g, m, feed_ref, resid_ref, gain_ref, cot_ref, land, proj_own, proj_all, d_resid, d_gain, lambda n: None)
    norm_back_ends(m, feed_ref, proj_own)


def attend_back(
    g, m,
    bounds_ref, proj_ref, d_resid_ref, out_ref, queries_ref, kv_ref, cos_ref, sin_ref, up_ref, latent_ref,
    query_gain_ref, down_ref, key_ref, value_ref, x_in_ref, r_in_ref, gain_ref, x_ref,
    d_q_out, low_out, slope_out, d_query_gain, d_gain,
    d_kv, kv_parts, kv_land, kv_column, kv_z, q_parts, q_land,
    low_own, low_in, n_parts, n_land, z_send, z_recv, out_sem, work,
):
    tokens, seqlen, depth = x_ref.shape[0], kv_ref.shape[1], kv_ref.shape[2] // 2
    rank, half, cols = down_ref.shape[1], tokens // 2, x_in_ref.shape[2]
    n_w = g.n_w
    mirror = g.n_z - 1 - g.z
    scale = 1.0 / math.sqrt(depth)

    def kv_part(stream, core, part):
        return kv_parts.at[stream, part, :, 1 - core if part else core]

    work.before_attention()

    def one_stream(stream):
        d_kv[...] = jnp.zeros_like(d_kv)
        for core in range(2):
            i = 2 * stream + core
            visible = visible_keys(bounds_ref, g.core * g.per + stream, g.base + core, tokens, seqlen)
            slopes = dot_nt(proj_ref[i], out_ref[...]).astype(BF)
            d_keys = jnp.zeros((seqlen, depth), F32)
            d_values = jnp.zeros((seqlen, depth), F32)
            for cut in range(0, up_ref.shape[1], depth):
                span = slice(cut, cut + depth)
                q, slope = queries_ref[i, :, span], slopes[:, span]
                probs = probabilities(q, kv_ref[stream, :, :depth], visible)
                d_probs = dot_nt(slope, kv_ref[stream, :, depth:])
                delta = jnp.sum(probs * d_probs, axis=-1, keepdims=True)
                d_scores = (probs * (d_probs - delta)).astype(BF)
                d_q = dot(d_scores, kv_ref[stream, :, :depth])
                d_q_out[i, :, span] = (rotate(d_q, cos_ref[core], -sin_ref[core]) * scale).astype(BF)
                d_keys += dot_tn(d_scores, q)
                d_values += dot_tn(probs.astype(BF), slope)
            shaped = (2, g.n_z, 2, half, depth)
            d_kv[:, :, :, :, :depth] += d_keys.reshape(shaped)
            d_kv[:, :, :, :, depth:] += d_values.reshape(shaped)
            q_parts[i] = dot_nt(d_q_out[i], up_ref[...]).astype(BF)
            m.to_source(0, i, q_parts.at[i], q_land.at[g.w])
            work.ticks(3)
        kv_parts[stream] = d_kv[...].astype(BF)
        for core in range(2):
            for part in range(2):
                m.to_source(1 + part, 2 * stream + core, kv_part(stream, core, part), kv_land.at[g.w, part])

    if n_w <= 4:
        for stream in range(g.per):
            one_stream(stream)
    else:
        lax.fori_loop(0, g.per, lambda stream, carry: (one_stream(stream), carry)[1], 0)
    work.after_attention(d_q_out)
    for j in range(n_w):
        m.arrived(0, j, q_land.at[j])
    d_n = q_land[0].astype(F32)
    for j in range(1, n_w):
        d_n += q_land[j].astype(F32)
    latent = latent_ref[...]
    r_query = inv_rms(latent)
    n_query = latent * r_query
    d_query_gain[...] = jnp.broadcast_to(jnp.sum(d_n * n_query, axis=0, keepdims=True), d_query_gain.shape)
    low_own[:, :rank] = rms_back(d_n * query_gain_ref[...], n_query, r_query).astype(BF)
    lead = pl.ds(0, rank)
    for j in range(n_w):
        m.to_target(3, j, low_own.at[:, lead], low_in.at[g.slot, :, lead])
    work.ticks(2)

    for j in range(n_w):
        for part in range(2):
            m.arrived(1 + part, j, kv_land.at[j, part])
    total = kv_land[0].astype(F32)
    for j in range(1, n_w):
        total += kv_land[j].astype(F32)
    kv_column[...] = total.astype(BF)

    def over_z(part, step):
        z = lax.rem(g.z + step, g.n_z)
        return column_copy(
            g, part, step, kv_column.at[part, g.n_z - 1 - z if part else z], kv_z.at[step, part], z_send, z_recv
        )

    for step in range(1, g.n_z):
        for part in range(2):
            over_z(part, step).start()
    work.ticks(2)
    own = [kv_column[0, g.z].astype(F32), kv_column[1, mirror].astype(F32)]
    for step in range(1, g.n_z):
        for part in range(2):
            over_z(part, step).wait_recv()
            own[part] += kv_z[step, part].astype(F32)
    own = jnp.concatenate(own, axis=0)
    low_own[:, rank : rank + depth] = rotate(own[:, :depth], cos_ref[g.core], -sin_ref[g.core]).astype(BF)
    low_own[:, rank + depth :] = own[:, depth:].astype(BF)
    tail = pl.ds(rank, 2 * depth)
    for j in range(n_w):
        m.to_target(4, j, low_own.at[:, tail], low_in.at[g.slot, :, tail])

    d_first = jnp.zeros((1, cols), F32)
    for i in range(n_w):
        m.arrived(3, i, low_in.at[i, :, lead])
        d_h = dot_nt(low_in[i, :, :rank], down_ref[...])
        m.arrived(4, i, low_in.at[i, :, tail])
        d_h += dot_nt(low_in[i, :, rank : rank + depth], key_ref[...])
        d_h += dot_nt(low_in[i, :, rank + depth :], value_ref[...])
        normal = x_in_ref[i].astype(F32) * r_in_ref[i, :, :1]
        d_first += jnp.sum(d_h * normal, axis=0, keepdims=True)
        n_parts[i] = (d_h * gain_ref[...]).astype(BF)
        m.to_source(5, i, n_parts.at[i], n_land.at[g.w])
        work.ticks(1)
    d_gain[...] = jnp.broadcast_to(d_first, d_gain.shape)
    work.after_low(low_in, low_out, out_sem)
    for j in range(n_w):
        m.arrived(5, j, n_land.at[j])
    d_n = jnp.concatenate([n_land[j].astype(F32) for j in range(n_w)], axis=1)
    x = x_ref[...].astype(F32)
    r_first = inv_rms(x)
    slope_out[...] = (d_resid_ref[...] + rms_back(d_n, x * r_first, r_first)).astype(BF)

    work.at_end(low_in, low_out, out_sem)
    m.sent(0, lambda i: q_parts.at[i], False)
    m.sent(3, lambda j: low_own.at[:, lead], True)
    m.sent(4, lambda j: low_own.at[:, tail], True)
    m.sent(5, lambda i: n_parts.at[i], False)
    for part in range(2):
        m.sent(1 + part, lambda i: kv_part(i // 2, i % 2, part), False)
        for step in range(1, g.n_z):
            over_z(part, step).wait_send()


class Alone:
    def ticks(self, number):
        pass

    def before_attention(self):
        pass

    def after_attention(self, d_q):
        pass

    def after_low(self, low_in, low_out, sem):
        pltpu.make_async_copy(low_in, low_out, sem.at[0]).start()

    def at_end(self, low_in, low_out, sem):
        pltpu.make_async_copy(low_in, low_out, sem.at[0]).wait()


class Products:
    TILE = 512

    def __init__(self, chain, first, attn, proj, q_all, h_cols, stages, sems):
        self.chain, self.ticks, self.first = chain, chain.ticks, first
        self.attn, self.proj, self.q_all, self.h_cols = attn, proj, q_all, h_cols
        self.stages, self.sems = stages, sems

    def product(self, which, left, right, ticks):
        terms, stage = self.chain.terms[self.first + which], self.stages[which]
        cols, lead = terms.shape[-1], (slice(None),) * (len(terms.shape) - 1)
        tile = stage.shape[-1]
        rows = left.shape[0]

        def out(at):
            return pltpu.make_async_copy(stage, terms.at[(*lead, pl.ds(at, tile))], self.sems.at[which])

        for at in range(0, cols, tile):
            made = dot_tn(left[...], right[:, :, at : at + tile].reshape(rows, tile)).astype(BF)
            if at > 0:
                out(at - tile).wait()
            stage[...] = made.reshape(stage.shape)
            out(at).start()
            self.ticks(ticks)
        out(cols - tile).wait()
        self.chain.have(self.first + which + 1)

    def before_attention(self):
        self.product(0, self.attn, self.proj, 1)

    def after_attention(self, d_q):
        self.product(1, self.q_all, d_q, 1)

    def after_low(self, low_in, low_out, sem):
        self.product(2, self.h_cols, low_in, 1)

    def at_end(self, low_in, low_out, sem):
        pass


def attend_back_kernel(n_w, n_c, *refs):
    *refs, send, recv, z_send, z_recv, out_sem = refs
    g = Group(n_w, n_c)
    g.greet(True)
    attend_back(g, Moves(g, send, recv), *refs, z_send, z_recv, out_sem, Alone())


def late_kernel(n_w, n_c, plan, *refs):
    bounds_ref, feed_ref, resid_ref, gain_ref, cot_ref, *refs = refs
    rest, (layer_terms, attn, q_all, h_cols), given, refs = refs[:15], refs[15:19], refs[19:22], refs[22:]
    count = len(plan.arrays)
    sums, made, (d_q_out, slope_out, gains_out, layer_out), refs = (
        refs[:count], refs[count : count + 3], refs[count + 3 : count + 7], refs[count + 7 :]
    )
    chain_scratch, small_refs, refs = (
        refs[:CHAIN_SCRATCH], refs[CHAIN_SCRATCH : CHAIN_SCRATCH + SMALL_SCRATCH], refs[CHAIN_SCRATCH + SMALL_SCRATCH :]
    )
    land, proj_own, proj_in, d_resid, gain_terms, first_terms, norm_gain, query_gain, *refs = refs
    *stages, product_sems, small_send, small_recv, norm_send, norm_recv = refs[:8]
    back_scratch, (send, recv, z_send, z_recv, out_sem), buffers, loaded = refs[8:19], refs[19:24], refs[24:-1], refs[-1]
    wanted = [*rest, attn, q_all, h_cols]
    loads = Loads([wanted[i] for i in LOADED], buffers, loaded)
    for i, buffer in zip(LOADED, buffers, strict=True):
        wanted[i] = buffer
    *rest, attn, q_all, h_cols = wanted
    g = Group(n_w, n_c)
    norm_moves = Moves(g, norm_send, norm_recv)
    chain = Chain(plan, n_c, [*given, *made], sums, chain_scratch)
    chain.have(3)
    work = Products(chain, 3, attn, proj_in, q_all, h_cols, stages, product_sems)
    g.greet(True)
    norm_back(g, norm_moves, feed_ref, resid_ref, gain_ref, cot_ref, land, proj_own, proj_in, d_resid, norm_gain, chain.ticks)
    loads.wait(*range(len(LOADED)))
    attend_back(
        g, Moves(g, send, recv), bounds_ref, proj_in, d_resid, *rest, d_q_out, None, slope_out, query_gain, first_terms,
        *back_scratch, z_send, z_recv, out_sem, work,
    )
    width, rank = norm_gain.shape[1] // n_w, query_gain.shape[1] // n_w
    for j in range(n_w):
        gain_terms[j, :, :width] = norm_gain[:, j * width : (j + 1) * width]
        gain_terms[j, :, width:] = query_gain[:, j * rank : (j + 1) * rank]
    small = Small(
        g, n_c, Moves(g, small_send, small_recv), gain_terms, first_terms, layer_terms, resid_ref, gains_out, layer_out,
        land, small_refs,
    )
    small.begin()
    chain.ticks(4)
    small.middle()
    chain.finish()
    small.end()
    norm_back_ends(norm_moves, feed_ref, proj_own)


def bytes_of(shapes):
    return sum(math.prod(v.shape) * jnp.dtype(v.dtype).itemsize for v in shapes)


def late_part(n_w, n_c, shapes, turned, bounds, late, rest, out_part, given, attn, q_all, h_cols):
    feed, resid, gain, cot = late
    kv, up_cols, x = rest[2], rest[5], rest[14]
    (tokens, width), (rank, features) = x.shape, up_cols.shape
    per, seqlen, both = kv.shape
    n_z, half, cols, low = n_c // 2, tokens // 2, width // n_w, rank + both
    plan = Plan(shapes, turned, n_w, 8, 380_000)
    proj, d_q, slope = shape_of(n_w, tokens, width), shape_of(n_w, tokens, features), shape_of(tokens, width)
    d_resid, norm_gain = shape_of(tokens, width, dtype=F32), shape_of(8, width, dtype=F32)
    query_gain, first_gain = shape_of(8, rank, dtype=F32), shape_of(8, cols, dtype=F32)
    norm_scratch = [pltpu.VMEM((n_w, tokens, width), BF), pltpu.VMEM((tokens, width), BF)]
    norm_semaphores = [pltpu.SemaphoreType.DMA((NORM_SEMAPHORES, n_w))] * 2
    back_scratch = [
        pltpu.VMEM((2, n_z, 2, half, both), F32),
        pltpu.VMEM((per, 2, n_z, 2, half, both), BF),
        pltpu.VMEM((n_w, 2, n_z, half, both), BF),
        pltpu.VMEM((2, n_z, half, both), BF),
        pltpu.VMEM((n_z, 2, half, both), BF),
        pltpu.VMEM((n_w, tokens, rank), BF),
        pltpu.VMEM((n_w, tokens, rank), BF),
        pltpu.VMEM((tokens, low), BF),
        pltpu.VMEM((n_w, tokens, low), BF),
        pltpu.VMEM((n_w, tokens, cols), BF),
        pltpu.VMEM((n_w, tokens, cols), BF),
    ]
    back_semaphores = [
        pltpu.SemaphoreType.DMA((BACK_SEMAPHORES, n_w)),
        pltpu.SemaphoreType.DMA((BACK_SEMAPHORES, n_w)),
        pltpu.SemaphoreType.DMA((2, n_z)),
        pltpu.SemaphoreType.DMA((2, n_z)),
        pltpu.SemaphoreType.DMA((1,)),
    ]
    stages = [pltpu.VMEM((*v[:-1], math.gcd(v[-1], Products.TILE)), BF) for v in plan.shaped[3:]]
    gains = cols + rank // n_w
    merged_scratch = [
        *plan.scratch(),
        *small_scratch(n_w, n_c, gains, cols),
        *norm_scratch,
        *(pltpu.VMEM(v.shape, v.dtype) for v in (proj, d_resid)),
        pltpu.VMEM((n_w, 8, gains), F32),
        *(pltpu.VMEM(v.shape, v.dtype) for v in (first_gain, norm_gain, query_gain)),
        *stages,
        pltpu.SemaphoreType.DMA((3,)),
        *[pltpu.SemaphoreType.DMA((1, n_w))] * 2,
        *norm_semaphores,
        *back_scratch,
        *back_semaphores,
    ]
    wanted = [*rest, attn, q_all, h_cols]
    specs = [ANY if i in LOADED else VMEM for i in range(len(wanted))]
    buffers = [v for v in merged_scratch if v.dtype in (BF, F32)]
    if bytes_of([*buffers, *rest, *late[1:], attn, q_all, h_cols, d_q, slope, slope]) < 60 * MIB:
        count = len(plan.arrays)
        done = pl.pallas_call(
            functools.partial(late_kernel, n_w, n_c, plan),
            out_shape=[
                *plan.out_shapes(), *(shape_of(*v) for v in plan.shaped[3:]), d_q, slope,
                shape_of(8, gains + cols, dtype=F32), slope,
            ],
            in_specs=[SMEM, ANY, VMEM, VMEM, VMEM, *specs[:-3], ANY, *specs[-3:]] + [ANY] * 3,
            out_specs=[ANY] * (count + 3) + [VMEM] * 4,
            scratch_shapes=[
                *merged_scratch, *vmem_like(wanted[i] for i in LOADED), pltpu.SemaphoreType.DMA((len(LOADED),))
            ],
            compiler_params=params(3, 62),
        )(
            bounds, feed, resid, gain, cot, *rest, out_part, attn, q_all, h_cols,
            *(v.reshape(s) for v, s in zip(given, plan.shaped, strict=False)),
        )
        return plan.row_shards(done[:count]), done[-2], done[-1], done[-3]
    d_proj, d_resid, d_norm_gain = pl.pallas_call(
        functools.partial(norm_back_kernel, n_w, n_c),
        out_shape=[proj, d_resid, norm_gain],
        in_specs=[ANY, VMEM, VMEM, VMEM],
        out_specs=[ANY, VMEM, VMEM],
        scratch_shapes=[*norm_scratch, *norm_semaphores],
        compiler_params=params(5, 40),
    )(feed, resid, gain, cot)
    d_q_raw, d_low, d_x, d_query_gain, d_first_gain = pl.pallas_call(
        functools.partial(attend_back_kernel, n_w, n_c),
        out_shape=[d_q, shape_of(n_w, tokens, low), slope, query_gain, first_gain],
        in_specs=[SMEM] + [VMEM] * (2 + len(rest)),
        out_specs=[VMEM, ANY] + [VMEM] * 3,
        scratch_shapes=[*back_scratch, *back_semaphores],
        compiler_params=params(6, 60),
    )(bounds, d_proj, d_resid, *rest)
    pairs = ((attn, d_proj), (q_all, d_q_raw), (h_cols, d_low))
    terms = [*given, *(dot_tn(a, b.reshape(n_w * tokens, -1)).astype(BF) for a, b in pairs)]
    spread = [v.reshape(8, n_w, -1).swapaxes(0, 1) for v in (d_norm_gain, d_query_gain)]
    sums, gains, layer_output = sum_over_ctx(
        plan, terms, n_c, 4, jnp.concatenate(spread, axis=2), d_first_gain, out_part, resid
    )
    return sums, gains, layer_output, d_x


def tables(positions, width):
    exponent = jnp.arange(width // 2, dtype=F32) * (-2.0 / width)
    angles = positions.astype(F32)[..., None] * (10000.0**exponent)
    return jnp.cos(angles), jnp.sin(angles)


def whole_columns(part, rows):
    whole = lax.all_gather(part, "ctx", axis=1)
    return whole.reshape(rows, part.shape[-1])


def on_device(
    inputs,
    boundaries,
    first_gain,
    query_down,
    query_gain,
    query_up,
    key_weights,
    value_weights,
    output_weights,
    second_gain,
    gate_weights,
    up_weights,
    down_weights,
    cotangent,
):
    n_w, n_c, c = lax.axis_size("wt"), lax.axis_size("ctx"), lax.axis_index("ctx")
    width, half = inputs.shape[-1], inputs.shape[2]
    tokens, seqlen = 2 * half, 2 * half * n_c
    depth, rank = key_weights.shape[1], query_down.shape[1]
    hidden_cols = down_weights.shape[0]

    def for_columns(weight):
        rows = weight.shape[0] // n_c
        part = lax.dynamic_slice_in_dim(weight, c * rows, rows, 0)
        return part.reshape(rows, n_w, -1).swapaxes(0, 1)

    wide_bounds = jnp.zeros((8, 128), jnp.int32).at[0, : boundaries.shape[1]].set(boundaries[0])
    gains = jnp.concatenate([query_gain, second_gain]).astype(F32)
    gains = jnp.broadcast_to(gains[None], (8, gains.shape[0]))
    bounds, gains, up_part, gate_part, upper_part = exchange(
        [wide_bounds, gains, for_columns(query_up), for_columns(gate_weights), for_columns(up_weights)],
        (False, False, True, True, True), n_w, 0,
    )
    bounds = bounds[:, 0, : boundaries.shape[1]]
    gain_query = gains[:, 0, : rank // n_w].reshape(1, rank)
    gain_two = gains[:, 0, rank // n_w :].reshape(1, width)
    gain_one = first_gain.astype(F32)[None]
    up_cols = whole_columns(up_part, rank)
    gate_cols = whole_columns(gate_part, width)
    upper_cols = whole_columns(upper_part, width)

    ctx = jnp.stack([c - c % 2, c - c % 2 + 1])[:, None]
    offsets = jnp.arange(half, dtype=jnp.int32)[None]
    positions = jnp.concatenate([ctx * half + offsets, seqlen - (ctx + 1) * half + offsets], axis=1)
    cosine, sine = tables(positions, depth)
    x = inputs.reshape(tokens, width)
    cot = cotangent.reshape(tokens, width)
    h_cols, x_in, r_in, latent, q_all, kv, cot_all = first_part(
        n_w, n_c, x, cot, gain_one, gain_query, query_down, key_weights, value_weights,
        lax.dynamic_index_in_dim(cosine, c % 2, keepdims=False), lax.dynamic_index_in_dim(sine, c % 2, keepdims=False),
    )
    kv = kv.reshape(n_w // 2, seqlen, 2 * depth)
    queries, attn, resid, h_all = attend_part(
        n_w, n_c, bounds, q_all, up_cols, kv, cosine, sine, output_weights, x, gain_two
    )

    h_second = h_all.reshape(n_w * tokens, width)
    slope = cot_all.reshape(n_w * tokens, width)
    gate = dot(h_second, gate_cols)
    upper = dot(h_second, upper_cols)
    sigma = jax.nn.sigmoid(gate)
    silu = gate * sigma
    hidden = (silu * upper).astype(BF)
    d_hidden = dot_nt(slope, down_weights)
    d_gate = (d_hidden * upper * sigma * (1.0 + gate * (1.0 - sigma))).astype(BF)
    d_upper = (d_hidden * silu).astype(BF)
    out_part = dot(hidden, down_weights).astype(BF)
    d_down = dot_tn(hidden, slope).astype(BF)
    d_gate_weights = dot_tn(h_second, d_gate).astype(BF)
    d_up_weights = dot_tn(h_second, d_upper).astype(BF)
    feed = (dot_nt(d_gate, gate_cols) + dot_nt(d_upper, upper_cols)).astype(BF)

    def grouped(v):
        return v.reshape(n_w, tokens, v.shape[-1])

    def flat(v):
        return v.reshape(n_w * tokens, v.shape[-1])

    rest = (
        output_weights, queries, kv, cosine, sine, up_cols, latent, gain_query, query_down, key_weights, value_weights,
        x_in, r_in, gain_one, x,
    )
    given = (d_down, d_gate_weights, d_up_weights)
    shapes = [v.shape for v in given]
    shapes += [output_weights.shape, up_cols.shape, (query_down.shape[0], rank + 2 * depth)]
    sums, gains, layer_output, input_gradient = late_part(
        n_w, n_c, shapes, (False, True, True, False, True, False), bounds, (grouped(feed), resid, gain_two, cot), rest,
        grouped(out_part), given, flat(attn), flat(q_all), flat(h_cols),
    )
    *sums, firsts = sums
    d_down, d_gate_weights, d_up_weights, d_output, d_query_up = (s.astype(F32) for s in sums)
    one, two = width // n_w, 2 * (width // n_w)
    return (
        layer_output.reshape(inputs.shape),
        input_gradient.reshape(inputs.shape),
        gains[0, :one],
        firsts[:, :rank].astype(F32),
        gains[0, two:],
        d_query_up,
        firsts[:, rank : rank + depth].astype(F32),
        firsts[:, rank + depth :].astype(F32),
        d_output,
        gains[0, one:two],
        d_gate_weights,
        d_up_weights,
        d_down,
    )


def solution(mesh):
    token = P("wt", None, "ctx", None)
    row, vec = P("wt", None), P("wt")
    in_specs = (token, row, vec, row, vec, row, row, row, row, vec, row, row, row, token)
    out_specs = (token, token, vec, row, vec, row, row, row, row, vec, row, row, row)
    return jax.shard_map(
        on_device, mesh=mesh, in_specs=in_specs, out_specs=out_specs, check_vma=False
    )
```

```python
import functools
import math

import jax
import jax.numpy as jnp
from jax import lax
from jax.experimental import pallas as pl
from jax.experimental.pallas import tpu as pltpu
from jax.sharding import PartitionSpec as P

EPS = 1e-06
NEG = -1e30
F32 = jnp.float32
BF = jnp.bfloat16
VMEM = pl.BlockSpec(memory_space=pltpu.VMEM)
SMEM = pl.BlockSpec(memory_space=pltpu.SMEM)
ANY = pl.BlockSpec(memory_space=pl.ANY)
MIB = 1 << 20
MESH = pl.DeviceIdType.MESH


def dot(a, b):
    return jnp.dot(a, b, preferred_element_type=F32)


def dot_nt(a, b):
    return lax.dot_general(a, b, (((1,), (1,)), ((), ())), preferred_element_type=F32)


def dot_tn(a, b):
    return lax.dot_general(a, b, (((0,), (0,)), ((), ())), preferred_element_type=F32)


def inv_rms(v):
    return lax.rsqrt(jnp.mean(v * v, axis=-1, keepdims=True) + EPS)


def rms_back(slope, normal, scale):
    return scale * (slope - normal * jnp.mean(slope * normal, axis=-1, keepdims=True))


def rotate(v, cosine, sine):
    middle = v.shape[-1] // 2
    a, b = v[..., :middle], v[..., middle:]
    return jnp.concatenate([a * cosine - b * sine, b * cosine + a * sine], axis=-1)


def shape_of(*shape, dtype=BF):
    return jax.ShapeDtypeStruct(shape, dtype)


def params(collective, mib):
    return pltpu.CompilerParams(collective_id=collective, has_side_effects=True, vmem_limit_bytes=mib * MIB)


class Group:
    def __init__(self, n_w, n_c):
        self.n_w, self.n_z, self.per = n_w, n_c // 2, n_w // 2
        c, w = lax.axis_index("ctx"), lax.axis_index("wt")
        self.core = lax.rem(c, 2)
        self.z, self.w, self.base = c // 2, w, c - self.core
        self.home = w // self.per
        self.at_home = self.core == self.home
        self.stream = w - self.home * self.per
        self.slot = self.stream * 2 + self.core

    def target(self, j):
        return {"ctx": self.base + self.home, "wt": j}

    def source(self, i):
        return {"ctx": self.base + lax.rem(i, 2), "wt": self.core * self.per + i // 2}

    def column(self, step):
        return {"ctx": 2 * lax.rem(self.z + step, self.n_z) + self.core, "wt": self.w}

    def greet(self, column):
        barrier = pltpu.get_barrier_semaphore()
        others = [
            {"ctx": self.base + lax.rem(self.core + q, 2), "wt": lax.rem(self.w + r, self.n_w)}
            for q in range(2)
            for r in range(self.n_w)
        ][1:]
        if column:
            others += [{"ctx": 2 * lax.rem(self.z + s, self.n_z) + q, "wt": self.w} for s in range(1, self.n_z) for q in range(2)]
        for there in others:
            pl.semaphore_signal(barrier, inc=1, device_id=there, device_id_type=MESH)
        pl.semaphore_wait(barrier, len(others))


class Moves:
    def __init__(self, group, send, recv, passed=None):
        self.group, self.send, self.recv, self.passed = group, send, recv, passed
        self.relay = group.n_w == 4 and passed is not None
        self.across_x = group.w + 1 - 2 * lax.rem(group.w, 2)
        self.across_y = lax.rem(group.w + 2, 4)

    def start(self, kind, src, dst, there, index, slot, here):
        remote = pltpu.make_async_remote_copy(
            src_ref=src, dst_ref=dst, send_sem=self.send.at[kind, index], recv_sem=self.recv.at[kind, slot],
            device_id=there, device_id_type=MESH,
        )
        local = pltpu.make_async_copy(src, dst, self.recv.at[kind, slot])
        pl.when(jnp.logical_not(here))(remote.start)
        pl.when(here)(local.start)

    def to_target(self, kind, j, src, dst):
        g = self.group
        self.start(kind, src, dst, g.target(j), j, g.slot, g.at_home & (g.w == j))

    def to_source(self, kind, i, src, dst):
        g = self.group
        self.start(kind, src, dst, g.source(i), i, g.w, g.at_home & (g.slot == i))

    def gather(self, kind, src, dst):
        g = self.group
        for j in range(g.n_w):
            start = functools.partial(self.to_target, kind, j, src, dst)
            if self.relay:
                pl.when(g.w != g.n_w - 1 - j)(start)
            else:
                start()

    def relayed(self, kind, part, i, dst):
        g = self.group
        there = self.across_y if part == 0 else self.across_x
        return pltpu.make_async_remote_copy(
            src_ref=dst, dst_ref=dst, send_sem=self.passed.at[kind, i], recv_sem=self.recv.at[kind, i],
            device_id={"ctx": g.base + g.core, "wt": there}, device_id_type=MESH,
        )

    def passes(self, part, i):
        origin = self.group.core * self.group.per + i // 2
        return origin == (self.across_x if part == 0 else self.across_y)

    def pass_on(self, kinds):
        g = self.group
        if not self.relay:
            for kind, _, dst in kinds:
                for i in range(g.n_w):
                    self.arrived(kind, i, dst(i))
            return
        for far in (False, True):
            for kind, part, dst in kinds:
                for i in range(g.n_w):
                    opposite = g.core * g.per + i // 2 == g.n_w - 1 - g.w
                    wait = functools.partial(self.arrived, kind, i, dst(i))
                    pl.when(opposite if far else jnp.logical_not(opposite))(wait)
                    if not far:
                        pl.when(self.passes(part, i))(self.relayed(kind, part, i, dst(i)).start)

    def gathered(self, kind, part, src, dst):
        g = self.group
        if not self.relay:
            self.sent(kind, lambda j: src, True)
            return
        for i in range(g.n_w):
            copy = pltpu.make_async_remote_copy(
                src_ref=src, dst_ref=src, send_sem=self.send.at[kind, i], recv_sem=self.recv.at[kind, i],
                device_id=g.target(i), device_id_type=MESH,
            )
            skip = (g.at_home & (g.w == i)) | (g.w == g.n_w - 1 - i)
            pl.when(jnp.logical_not(skip))(copy.wait_send)
            pl.when(self.passes(part, i))(self.relayed(kind, part, i, dst(i)).wait_send)

    def arrived(self, kind, index, dst):
        pltpu.make_async_copy(dst, dst, self.recv.at[kind, index]).wait()

    def sent(self, kind, src, by_target):
        g = self.group
        for i in range(g.n_w):
            at = src(i)
            copy = pltpu.make_async_remote_copy(
                src_ref=at, dst_ref=at, send_sem=self.send.at[kind, i], recv_sem=self.recv.at[kind, i],
                device_id=g.target(i) if by_target else g.source(i), device_id_type=MESH,
            )
            here = g.at_home & ((g.w if by_target else g.slot) == i)
            pl.when(jnp.logical_not(here))(copy.wait_send)


class Loads:
    def __init__(self, operands, buffers, sems):
        self.copies = [
            pltpu.make_async_copy(src, dst, sems.at[i]) for i, (src, dst) in enumerate(zip(operands, buffers, strict=True))
        ]
        for copy in self.copies:
            copy.start()

    def wait(self, *which):
        for i in which:
            self.copies[i].wait()


def vmem_like(arrays):
    return [pltpu.VMEM(v.shape, v.dtype) for v in arrays]


def column_copy(group, part, step, src, dst, send, recv):
    return pltpu.make_async_remote_copy(
        src_ref=src, dst_ref=dst, send_sem=send.at[part, step], recv_sem=recv.at[part, step],
        device_id=group.column(step), device_id_type=MESH,
    )


def exchange_kernel(n_w, split, *refs):
    count = len(split)
    ins, outs = refs[:count], refs[count : 2 * count]
    send, recv, local = refs[2 * count :]
    c, w = lax.axis_index("ctx"), lax.axis_index("wt")
    barrier = pltpu.get_barrier_semaphore()
    for step in range(1, n_w):
        pl.semaphore_signal(
            barrier, inc=1, device_id={"ctx": c, "wt": lax.rem(w + step, n_w)}, device_id_type=MESH
        )
    pl.semaphore_wait(barrier, n_w - 1)
    copies = []
    for a in range(count):
        for step in range(1, n_w):
            there = lax.rem(w + step, n_w)
            copies.append(
                pltpu.make_async_remote_copy(
                    src_ref=ins[a].at[there] if split[a] else ins[a], dst_ref=outs[a].at[w],
                    send_sem=send.at[a, step], recv_sem=recv.at[a, step],
                    device_id={"ctx": c, "wt": there}, device_id_type=MESH,
                )
            )
        copies.append(pltpu.make_async_copy(ins[a].at[w] if split[a] else ins[a], outs[a].at[w], local.at[a]))
    for copy in copies:
        copy.start()
    for copy in copies:
        copy.wait()


def exchange(arrays, split, n_w, collective):
    return pl.pallas_call(
        functools.partial(exchange_kernel, n_w, split),
        out_shape=[
            jax.ShapeDtypeStruct(v.shape if s else (n_w, *v.shape), v.dtype) for v, s in zip(arrays, split, strict=True)
        ],
        in_specs=[ANY] * len(arrays),
        out_specs=[ANY] * len(arrays),
        scratch_shapes=[
            pltpu.SemaphoreType.DMA((len(arrays), n_w)),
            pltpu.SemaphoreType.DMA((len(arrays), n_w)),
            pltpu.SemaphoreType.DMA((len(arrays),)),
        ],
        compiler_params=params(collective, 16),
    )(*arrays)


def first_kernel(
    n_w, n_c,
    x_ref, cot_ref, gain_ref, query_gain_ref, down_ref, key_ref, value_ref, cos_ref, sin_ref,
    h_out, x_out, r_out, latent_out, q_all, kv_all, cot_all,
    x_in, r_in, r_own, parts, low, q_own, kv_own, kv_column, down_own, key_own, value_own,
    send, recv, passed, z_send, z_recv, loaded,
):
    g = Group(n_w, n_c)
    m = Moves(g, send, recv, passed)
    loads = Loads([down_ref, key_ref, value_ref], [down_own, key_own, value_own], loaded)
    down_ref, key_ref, value_ref = down_own, key_own, value_own
    tokens, cols = x_in.shape[1:]
    rank, depth = down_ref.shape[1], key_ref.shape[1]
    r_own[...] = jnp.broadcast_to(inv_rms(x_ref[...].astype(F32)), r_own.shape)
    g.greet(True)
    for j in range(n_w):
        m.to_target(0, j, x_ref.at[:, pl.ds(j * cols, cols)], x_in.at[g.slot])
        m.to_target(1, j, r_own, r_in.at[g.slot])

    loads.wait(0, 1, 2)
    for i in range(n_w):
        m.arrived(0, i, x_in.at[i])
        m.arrived(1, i, r_in.at[i])
        x_out[i] = x_in[i]
        r_out[i] = r_in[i]
        h = (x_in[i].astype(F32) * r_in[i, :, :1] * gain_ref[...]).astype(BF)
        h_out[i] = h
        parts[i, :, :rank] = dot(h, down_ref[...]).astype(BF)
        parts[i, :, rank : rank + depth] = dot(h, key_ref[...]).astype(BF)
        parts[i, :, rank + depth :] = dot(h, value_ref[...]).astype(BF)
        m.to_source(2, i, parts.at[i], low.at[g.w])

    for j in range(n_w):
        m.arrived(2, j, low.at[j])
    total = low[0].astype(F32)
    for j in range(1, n_w):
        total += low[j].astype(F32)
    keys = rotate(total[:, rank : rank + depth], cos_ref[...], sin_ref[...]).astype(BF)
    kv = jnp.concatenate([keys, total[:, rank + depth :].astype(BF)], axis=1)
    half = tokens // 2
    mirror = g.n_z - 1 - g.z
    for part in range(2):
        kv_own[part] = kv[part * half : (part + 1) * half]

    def over_z(part, step):
        return column_copy(
            g, part, step, kv_own.at[part], kv_column.at[part, mirror if part else g.z], z_send, z_recv
        )

    for step in range(1, g.n_z):
        for part in range(2):
            over_z(part, step).start()
    kv_column[0, g.z] = kv_own[0]
    kv_column[1, mirror] = kv_own[1]
    latent = total[:, :rank]
    latent_out[...] = latent
    q_own[...] = (latent * inv_rms(latent) * query_gain_ref[...]).astype(BF)

    def rows(ref, part, *lead):
        return ref.at[(*lead, pl.ds(part * half, half))]

    def kv_place(part, stream, core):
        return kv_all.at[stream, part, :, 1 - core if part else core]

    for part in range(2):
        m.gather(3 + part, rows(q_own, part), rows(q_all, part, g.slot))
    for part in range(2):
        m.gather(5 + part, rows(cot_ref, part), rows(cot_all, part, g.slot))
    for step in range(1, g.n_z):
        for part in range(2):
            over_z(part, step).wait_recv()
    for part in range(2):
        m.gather(7 + part, kv_column.at[part], kv_place(part, g.stream, g.core))
    gathers = [(3 + part, part, functools.partial(rows, q_all, part)) for part in range(2)]
    gathers += [(5 + part, part, functools.partial(rows, cot_all, part)) for part in range(2)]
    gathers += [(7 + part, part, lambda i, part=part: kv_place(part, i // 2, i % 2)) for part in range(2)]
    m.pass_on(gathers)
    m.sent(0, lambda j: x_ref.at[:, pl.ds(j * cols, cols)], True)
    m.sent(1, lambda j: r_own, True)
    m.sent(2, lambda i: parts.at[i], False)
    for part in range(2):
        for kind, src in ((3, rows(q_own, part)), (5, rows(cot_ref, part)), (7, kv_column.at[part])):
            m.gathered(kind + part, part, src, gathers[kind + part - 3][2])
        for step in range(1, g.n_z):
            over_z(part, step).wait_send()


def first_part(n_w, n_c, x, cot, gain, query_gain, down, key, value, cosine, sine):
    tokens, width = x.shape
    cols, rank, depth = width // n_w, down.shape[1], key.shape[1]
    n_z, half, low = n_c // 2, tokens // 2, rank + 2 * depth
    return pl.pallas_call(
        functools.partial(first_kernel, n_w, n_c),
        out_shape=[
            shape_of(n_w, tokens, cols),
            shape_of(n_w, tokens, cols),
            shape_of(n_w, tokens, 128, dtype=F32),
            shape_of(tokens, rank, dtype=F32),
            shape_of(n_w, tokens, rank),
            shape_of(n_w // 2, 2, n_z, 2, half, 2 * depth),
            shape_of(n_w, tokens, width),
        ],
        in_specs=[VMEM, ANY, VMEM, VMEM, ANY, ANY, ANY, VMEM, VMEM],
        out_specs=[VMEM] * 4 + [ANY] * 3,
        scratch_shapes=[
            pltpu.VMEM((n_w, tokens, cols), BF),
            pltpu.VMEM((n_w, tokens, 128), F32),
            pltpu.VMEM((tokens, 128), F32),
            pltpu.VMEM((n_w, tokens, low), BF),
            pltpu.VMEM((n_w, tokens, low), BF),
            pltpu.VMEM((tokens, rank), BF),
            pltpu.VMEM((2, half, 2 * depth), BF),
            pltpu.VMEM((2, n_z, half, 2 * depth), BF),
            *vmem_like((down, key, value)),
            *[pltpu.SemaphoreType.DMA((9, n_w))] * 3,
            pltpu.SemaphoreType.DMA((2, n_z)),
            pltpu.SemaphoreType.DMA((2, n_z)),
            pltpu.SemaphoreType.DMA((3,)),
        ],
        compiler_params=params(1, 60),
    )(x, cot, gain, query_gain, down, key, value, cosine, sine)


def visible_keys(bounds_ref, stream, c, tokens, seqlen):
    half = tokens // 2
    row = lax.broadcasted_iota(jnp.int32, (tokens, 1), 0)
    pos = row + jnp.where(row < half, c * half, seqlen - (c + 1) * half - half)
    begin = jnp.zeros((tokens, 1), jnp.int32)
    for j in range(bounds_ref.shape[1]):
        start = bounds_ref[stream, j]
        begin = jnp.where(pos >= start, jnp.maximum(begin, start), begin)
    key = lax.broadcasted_iota(jnp.int32, (tokens, seqlen), 1)
    return (key >= begin) & (key <= pos)


def probabilities(q, keys, visible):
    scores = jnp.where(visible, dot_nt(q, keys), NEG)
    peak = jnp.max(scores, axis=-1, keepdims=True)
    weight = jnp.where(visible, jnp.exp(scores - peak), 0.0)
    return weight * (1.0 / jnp.sum(weight, axis=-1, keepdims=True))


def attend_kernel(
    n_w, n_c,
    bounds_ref, q_ref, up_ref, kv_ref, cos_ref, sin_ref, out_ref, x_ref, gain_ref,
    queries, attn, resid, h_all,
    parts, land, h_own, q_own, up_own, kv_own, out_own, send, recv, passed, loaded,
):
    g = Group(n_w, n_c)
    m = Moves(g, send, recv, passed)
    loads = Loads([q_ref, up_ref, kv_ref, out_ref], [q_own, up_own, kv_own, out_own], loaded)
    q_ref, up_ref, kv_ref, out_ref = q_own, up_own, kv_own, out_own
    tokens, seqlen, depth = q_ref.shape[1], kv_ref.shape[1], kv_ref.shape[2] // 2
    scale = 1.0 / math.sqrt(depth)
    g.greet(False)

    def one(i, carry):
        stream, core = i // 2, lax.rem(i, 2)
        visible = visible_keys(bounds_ref, g.core * g.per + stream, g.base + core, tokens, seqlen)
        raw = dot(q_ref[i], up_ref[...])
        for cut in range(0, up_ref.shape[1], depth):
            span = slice(cut, cut + depth)
            q = (rotate(raw[:, span], cos_ref[core], sin_ref[core]) * scale).astype(BF)
            queries[i, :, span] = q
            probs = probabilities(q, kv_ref[stream, :, :depth], visible).astype(BF)
            attn[i, :, span] = dot(probs, kv_ref[stream, :, depth:]).astype(BF)
        parts[i] = dot(attn[i], out_ref[...]).astype(BF)
        m.to_source(0, i, parts.at[i], land.at[g.w])
        return carry

    loads.wait(0, 1, 2, 3)
    lax.fori_loop(0, n_w, one, 0)
    total = x_ref[...].astype(F32)
    for j in range(n_w):
        m.arrived(0, j, land.at[j])
        total += land[j].astype(F32)
    resid[...] = total
    h_own[...] = (total * inv_rms(total) * gain_ref[...]).astype(BF)
    half = tokens // 2

    def rows(ref, part, *lead):
        return ref.at[(*lead, pl.ds(part * half, half))]

    gathers = [(1 + part, part, functools.partial(rows, h_all, part)) for part in range(2)]
    for part in range(2):
        m.gather(1 + part, rows(h_own, part), rows(h_all, part, g.slot))
    m.pass_on(gathers)
    m.sent(0, lambda i: parts.at[i], False)
    for part in range(2):
        m.gathered(1 + part, part, rows(h_own, part), gathers[part][2])


def attend_part(n_w, n_c, bounds, q_all, up_cols, kv, cosine, sine, output, x, gain):
    tokens, width = x.shape
    features = up_cols.shape[1]
    return pl.pallas_call(
        functools.partial(attend_kernel, n_w, n_c),
        out_shape=[
            shape_of(n_w, tokens, features),
            shape_of(n_w, tokens, features),
            shape_of(tokens, width, dtype=F32),
            shape_of(n_w, tokens, width),
        ],
        in_specs=[SMEM, ANY, ANY, ANY, VMEM, VMEM, ANY, VMEM, VMEM],
        out_specs=[VMEM] * 3 + [ANY],
        scratch_shapes=[
            pltpu.VMEM((n_w, tokens, width), BF),
            pltpu.VMEM((n_w, tokens, width), BF),
            pltpu.VMEM((tokens, width), BF),
            *vmem_like((q_all, up_cols, kv, output)),
            *[pltpu.SemaphoreType.DMA((3, n_w))] * 3,
            pltpu.SemaphoreType.DMA((4,)),
        ],
        compiler_params=params(2, 60),
    )(bounds, q_all, up_cols, kv, cosine, sine, output, x, gain)


class Plan:
    def __init__(self, shapes, turned, n_w, slots, limit):
        self.n_w, self.arrays, self.turned = n_w, shapes, turned
        self.wide = all(cols % 128 == 0 for (_, cols), turn in zip(shapes, turned, strict=True) if turn)
        self.shaped, self.pieces, self.members, self.ring_shapes = [], [], [[], []], [None, None]
        for (rows, cols), turn in zip(shapes, turned, strict=True):
            self.shaped.append((n_w, 2, 2, rows // n_w // 4, cols) if turn else (2, 2, rows // 4, cols))
        for kind in range(2):
            mine = [v for v, turn in zip(self.shaped, turned, strict=True) if turn == bool(kind)]
            if mine:
                lead, cols = (n_w, 2) if kind else (2,), max(v[-1] for v in mine)
                rows = 16
                common = math.gcd(*(v[-2] for v in mine))
                for more in range(16, common + 1, 16):
                    if common % more == 0 and math.prod(lead) * more * cols * 2 <= limit:
                        rows = more
                self.ring_shapes[kind] = (*lead, rows, cols)
        for a, (v, turn) in enumerate(zip(self.shaped, turned, strict=True)):
            rows = self.ring_shapes[int(turn)][-2]
            for row in range(0, v[-2], rows):
                self.members[int(turn)].append(len(self.pieces))
                self.pieces.append((a, int(turn), len(self.members[int(turn)]) - 1, row, rows, v[-1]))
        self.slots = [min(slots, len(members)) for members in self.members]

    def __len__(self):
        return len(self.pieces)

    def slot(self, q):
        return self.pieces[q][2] % self.slots[self.pieces[q][1]]

    def before(self, q):
        _, kind, index = self.pieces[q][:3]
        return self.members[kind][index - self.slots[kind]] if index >= self.slots[kind] else None

    def after(self, q):
        _, kind, index = self.pieces[q][:3]
        later = index + self.slots[kind]
        return self.members[kind][later] if later < len(self.members[kind]) else None

    def scratch(self):
        shapes = [v or (16, 128) for v in self.ring_shapes]
        slots = [max(v, 1) for v in self.slots]
        rings = [pltpu.VMEM((n, *v), BF) for n, v in zip(slots, shapes, strict=True)]
        rows, turned = shapes
        halves = [pltpu.VMEM((slots[0], *rows[-2:]), BF), pltpu.VMEM((slots[1], self.n_w, *turned[-2:]), BF)]
        moved = (turned[-2], self.n_w * turned[-1]) if self.wide else (self.n_w, *turned[-2:])
        kinds, count = 5 + self.n_w, len(self)
        return [
            *rings, *rings, *rings, *halves, pltpu.VMEM((slots[1], *moved), BF),
            pltpu.SemaphoreType.DMA((count,)),
            pltpu.SemaphoreType.DMA((count,)),
            pltpu.SemaphoreType.DMA((kinds, count)),
            pltpu.SemaphoreType.DMA((kinds, count)),
            pltpu.SemaphoreType.REGULAR((4, count)),
        ]

    def out_shapes(self):
        return [
            shape_of(2, 2, v[-2], self.n_w * v[-1]) if turn and self.wide else shape_of(*v)
            for v, turn in zip(self.shaped, self.turned, strict=True)
        ]

    def row_shards(self, sums):
        done = []
        for s, (rows, cols), turn in zip(sums, self.arrays, self.turned, strict=True):
            if self.wide or not turn:
                done.append(s.reshape(-1, s.shape[-1]))
            else:
                done.append(s.reshape(self.n_w, rows // self.n_w, cols).swapaxes(0, 1).reshape(rows // self.n_w, -1))
        return done


CHAIN_SCRATCH = 14


class Chain:
    AHEAD, LEAD, HALF, MOVE, DONE, LAG = 2, 3, 1, 2, 3, 9

    def __init__(self, plan, n_c, terms, outs, scratch):
        self.plan, self.n_w, self.terms, self.outs = plan, plan.n_w, terms, outs
        self.own, self.mates, self.ups, self.halves = (scratch[2 * i : 2 * i + 2] for i in range(4))
        self.moved, self.load, self.place, self.send, self.recv, self.credit = scratch[8:]
        c, w = lax.axis_index("ctx"), lax.axis_index("wt")
        chain, k = n_c // 2, c // 2
        self.w, self.core = w, lax.rem(c, 2)
        left = k < chain // 2
        self.side = jnp.where(left, 0, 1)
        far = jnp.where(left, k, chain - 1 - k)
        self.middle, self.outside = far == chain // 2 - 1, far > 0
        self.mate = {"ctx": c + 1 - 2 * self.core, "wt": w}
        self.inner = {"ctx": jnp.where(left, c + 2, c - 2), "wt": w}
        self.outer = {"ctx": jnp.where(left, c - 2, c + 2), "wt": w}
        self.peers = [{"ctx": c, "wt": lax.rem(w + r, self.n_w)} for r in range(1, self.n_w)]
        self.now, self.ready = 0, len(plan)

    def turned(self, q):
        return self.plan.turned[self.plan.pieces[q][0]]

    def every(self, q):
        return (slice(None),) if self.turned(q) else ()

    def term(self, q, core):
        a, _, _, row, rows, _ = self.plan.pieces[q]
        return self.terms[a].at[(*self.every(q), core, slice(None), pl.ds(row, rows))]

    def fitting(self, q, buffer):
        cols = self.plan.pieces[q][5]
        lead = (slice(None),) * (len(buffer.shape) - 2)
        return buffer.at[(self.plan.slot(q), *lead, pl.ds(0, cols))]

    def ring(self, q, buffers):
        return self.fitting(q, buffers[self.plan.pieces[q][1]])

    def half_buffer(self, q):
        return self.ring(q, self.halves)

    def remote(self, kind, q, src, dst, there):
        return pltpu.make_async_remote_copy(
            src_ref=src, dst_ref=dst, send_sem=self.send.at[kind, q], recv_sem=self.recv.at[kind, q], device_id=there,
            device_id_type=MESH,
        )

    def own_load(self, q):
        return pltpu.make_async_copy(self.term(q, self.core), self.ring(q, self.own), self.load.at[q])

    def to_mate(self, q):
        return self.remote(0, q, self.term(q, 1 - self.core), self.ring(q, self.mates), self.mate)

    def along(self, q, there):
        return self.remote(1, q, self.ring(q, self.own), self.ring(q, self.ups), there)

    def to_across(self, q):
        side = self.ring(q, self.own).at[(*self.every(q), 1 - self.side)]
        return self.remote(5, q, side, self.half_buffer(q), self.inner)

    def moved_part(self, q, source):
        cols = self.plan.pieces[q][5]
        if not self.plan.wide:
            return self.moved.at[self.plan.slot(q), source, :, pl.ds(0, cols)]
        return self.moved.at[self.plan.slot(q), :, pl.ds(pl.multiple_of(source * cols, 128), cols)]

    def to_peer(self, q, r, slot):
        there = self.peers[r]
        return self.remote(6 + r, q, self.half_buffer(q).at[there["wt"]], self.moved_part(q, slot), there)

    def finished(self, q):
        if not self.turned(q):
            return self.half_buffer(q)
        if self.plan.wide:
            return self.moved.at[self.plan.slot(q), :, pl.ds(0, self.n_w * self.plan.pieces[q][5])]
        return self.fitting(q, self.moved)

    def result(self, q, *lead):
        a, kind, _, row, rows, _ = self.plan.pieces[q]
        every = () if self.plan.wide else self.every(q)
        return self.outs[a].at[(*every, *lead, pl.ds(row, rows))]

    def half_place(self, q):
        return pltpu.make_async_copy(self.finished(q), self.result(q, self.core, self.side), self.place.at[q])

    def half_across(self, q, side):
        return self.remote(2, q, self.finished(q), self.result(q, self.core, side), self.inner)

    def down(self, kind, q, there):
        here = self.result(q, self.core, slice(None))
        return self.remote(kind, q, here, here, there)

    def add(self, q, ins, out):
        rows = out.shape[-2]
        step = 16 if rows % 16 == 0 else rows
        lead = (slice(None),) * (len(out.shape) - 2)

        def body(i, carry):
            at = (*lead, pl.ds(i * step, step))
            total = ins[0][at].astype(F32)
            for ref in ins[1:]:
                total += ref[at].astype(F32)
            out[at] = total.astype(BF)
            return carry

        lax.fori_loop(0, rows // step, body, 0)

    def grant(self, kind, q, there):
        pl.semaphore_signal(self.credit.at[kind, q], inc=1, device_id=there, device_id_type=MESH)

    def prefetch(self, q):
        before = self.plan.before(q)
        if before is not None:
            pl.when(self.middle)(self.to_across(before).wait_send)
            pl.when(jnp.logical_not(self.middle))(self.along(before, self.inner).wait_send)
            pl.semaphore_wait(self.credit.at[0, q], 1)
        self.own_load(q).start()
        self.to_mate(q).start()

    def up(self, q):
        self.own_load(q).wait()
        self.to_mate(q).wait_recv()
        after, before = self.plan.after(q), self.plan.before(q)
        own, mates, ups = (self.ring(q, b) for b in (self.own, self.mates, self.ups))

        @pl.when(self.outside)
        def _():
            self.along(q, self.outer).wait_recv()
            self.add(q, [own, mates, ups], own)
            if after is not None:
                self.grant(1, after, self.outer)

        @pl.when(jnp.logical_not(self.outside))
        def _():
            self.add(q, [own, mates], own)

        if after is not None:
            self.grant(0, after, self.mate)

        @pl.when(self.middle)
        def _():
            if before is not None:
                pl.semaphore_wait(self.credit.at[2, q], 1)
            self.to_across(q).start()

        @pl.when(jnp.logical_not(self.middle))
        def _():
            if before is not None:
                pl.semaphore_wait(self.credit.at[1, q], 1)
            self.along(q, self.inner).start()

    def finish_half(self, q):
        self.to_across(q).wait_recv()
        half = self.half_buffer(q)
        self.add(q, [self.ring(q, self.own).at[(*self.every(q), self.side)], half], half)
        if self.turned(q):
            if self.plan.before(q) is not None:
                pl.semaphore_wait(self.credit.at[3, q], self.n_w - 1)
            for r in range(self.n_w - 1):
                self.to_peer(q, r, self.w).start()
            self.moved_part(q, self.w)[...] = half[self.w]
        else:
            self.spread(q)

    def spread(self, q):
        self.half_place(q).start()
        self.half_across(q, self.side).start()

    def move(self, q):
        if self.turned(q):
            for r in range(self.n_w - 1):
                self.to_peer(q, r, lax.rem(self.w + self.n_w - r - 1, self.n_w)).wait_recv()
            self.spread(q)

    def pass_down(self, q):
        pl.when(self.outside)(self.down(3, q, self.outer).start)
        self.down(4, q, self.mate).start()

    def free(self, q):
        after = self.plan.after(q)
        if after is not None:
            self.half_across(q, self.side).wait_send()
            if self.turned(q):
                for r in range(self.n_w - 1):
                    self.to_peer(q, r, self.w).wait_send()
                for there in self.peers:
                    self.grant(3, after, there)
            self.grant(2, after, self.inner)

    def tick(self):
        t, count = self.now, len(self.plan)
        self.now += 1
        inside, outside = self.middle, jnp.logical_not(self.middle)

        @pl.when(outside)
        def _():
            if t == 0:
                for q in range(min(self.AHEAD, count)):
                    self.prefetch(q)
            for q in range(0 if t == 0 else t + self.LEAD, t + self.LEAD + 1):
                if q < count:
                    self.up(q)
                if q + self.AHEAD < count:
                    self.prefetch(q + self.AHEAD)
            if 0 <= t - self.LAG < count:
                self.down(3, t - self.LAG, self.inner).wait_recv()
                self.pass_down(t - self.LAG)

        @pl.when(inside)
        def _():
            if t == 0:
                for q in range(min(self.AHEAD, count)):
                    self.prefetch(q)
            if t < count:
                self.up(t)
            if 0 <= t - self.HALF < count:
                self.finish_half(t - self.HALF)
            if 0 <= t - self.MOVE < count:
                self.move(t - self.MOVE)
            done = t - self.DONE
            if 0 <= done < count:
                self.half_place(done).wait()
                self.half_across(done, 1 - self.side).wait_recv()
                self.pass_down(done)
                self.free(done)
            if t + self.AHEAD < count:
                self.prefetch(t + self.AHEAD)

    def ticks(self, number):
        for _ in range(number):
            if self.now + self.AHEAD + self.LEAD < self.ready or self.now < len(self.plan) + self.LAG and self.ready == len(self.plan):
                self.tick()

    def have(self, arrays):
        self.ready = sum(piece[0] < arrays for piece in self.plan.pieces)

    def finish(self):
        self.ticks(len(self.plan) + self.LAG)
        for q in range(len(self.plan)):
            last = self.plan.after(q) is None

            @pl.when(self.middle)
            def _():
                if last:
                    self.to_across(q).wait_send()
                    self.half_across(q, self.side).wait_send()
                    for r in range(self.n_w - 1 if self.turned(q) else 0):
                        self.to_peer(q, r, self.w).wait_send()

            if last:
                pl.when(jnp.logical_not(self.middle))(self.along(q, self.inner).wait_send)
            self.to_mate(q).wait_send()
            pl.when(self.outside)(self.down(3, q, self.outer).wait_send)
            other = self.result(q, 1 - self.core, slice(None))
            self.remote(4, q, other, other, self.mate).wait_recv()
            self.down(4, q, self.mate).wait_send()


class Small:
    def __init__(self, group, n_c, moves, terms, first_terms, layer_terms, resid, out, layer_out, layer_land, scratch):
        self.g, self.n_c, self.m = group, n_c, moves
        self.terms, self.first_terms, self.layer_terms, self.resid = terms, first_terms, layer_terms, resid
        self.out, self.layer_out, self.layer_land = out, layer_out, layer_land
        self.land, self.own, self.all, self.send, self.recv = scratch
        self.c = lax.axis_index("ctx")

    def block(self, step):
        n_w, j = self.g.n_w, lax.rem(self.g.w + step, self.g.n_w)
        return pltpu.make_async_remote_copy(
            src_ref=self.terms.at[j], dst_ref=self.land.at[step], send_sem=self.send.at[step],
            recv_sem=self.recv.at[step], device_id={"ctx": self.c, "wt": j}, device_id_type=MESH,
        )

    def total(self, step):
        at = self.g.n_w + step
        return pltpu.make_async_remote_copy(
            src_ref=self.own, dst_ref=self.all.at[step], send_sem=self.send.at[at], recv_sem=self.recv.at[at],
            device_id={"ctx": lax.rem(self.c + step, self.n_c), "wt": self.g.w}, device_id_type=MESH,
        )

    def begin(self):
        for step in range(1, self.g.n_w):
            self.block(step).start()
        for i in range(self.g.n_w):
            self.m.to_source(0, i, self.layer_terms.at[i], self.layer_land.at[self.g.w])

    def middle(self):
        first = self.first_terms.shape[1]
        total = self.terms[self.g.w]
        for step in range(1, self.g.n_w):
            self.block(step).wait_recv()
            total += self.land[step]
        self.own[:, :first] = self.first_terms[...]
        self.own[:, first:] = total
        for step in range(1, self.n_c):
            self.total(step).start()
        total = self.resid[...]
        for j in range(self.g.n_w):
            self.m.arrived(0, j, self.layer_land.at[j])
            total += self.layer_land[j].astype(F32)
        self.layer_out[...] = total.astype(BF)

    def end(self):
        total = self.own[...]
        for step in range(1, self.n_c):
            self.total(step).wait_recv()
            total += self.all[step]
        self.out[...] = total
        for step in range(1, self.g.n_w):
            self.block(step).wait_send()
        for step in range(1, self.n_c):
            self.total(step).wait_send()
        self.m.sent(0, lambda i: self.layer_terms.at[i], False)


SMALL_SCRATCH = 5


def small_scratch(n_w, n_c, width, first):
    return [
        pltpu.VMEM((n_w, 8, width), F32),
        pltpu.VMEM((8, width + first), F32),
        pltpu.VMEM((n_c, 8, width + first), F32),
        pltpu.SemaphoreType.DMA((n_w + n_c,)),
        pltpu.SemaphoreType.DMA((n_w + n_c,)),
    ]


def sum_kernel(plan, n_c, *refs):
    count = len(plan.arrays)
    terms, (gain_terms, first_terms, layer_terms, resid_ref), refs = refs[:count], refs[count : count + 4], refs[count + 4 :]
    outs, (gains_out, layer_out), refs = refs[:count], refs[count : count + 2], refs[count + 2 :]
    layer_land, group_send, group_recv = refs[CHAIN_SCRATCH + SMALL_SCRATCH :]
    g = Group(plan.n_w, n_c)
    chain = Chain(plan, n_c, terms, outs, refs[:CHAIN_SCRATCH])
    small = Small(
        g, n_c, Moves(g, group_send, group_recv), gain_terms, first_terms, layer_terms, resid_ref, gains_out, layer_out,
        layer_land, refs[CHAIN_SCRATCH : CHAIN_SCRATCH + SMALL_SCRATCH],
    )
    g.greet(True)
    chain.ticks(2)
    small.begin()
    chain.ticks(4)
    small.middle()
    chain.finish()
    small.end()


def sum_over_ctx(plan, terms, n_c, collective, gain_terms, first_terms, layer_terms, resid):
    n_w, count = plan.n_w, len(plan.arrays)
    width, first = gain_terms.shape[-1], first_terms.shape[-1]
    sums = pl.pallas_call(
        functools.partial(sum_kernel, plan, n_c),
        out_shape=[*plan.out_shapes(), shape_of(8, width + first, dtype=F32), shape_of(*resid.shape)],
        in_specs=[ANY] * count + [VMEM, VMEM, ANY, VMEM],
        out_specs=[ANY] * count + [VMEM, VMEM],
        scratch_shapes=[
            *plan.scratch(),
            *small_scratch(n_w, n_c, width, first),
            pltpu.VMEM(layer_terms.shape, BF),
            pltpu.SemaphoreType.DMA((1, n_w)),
            pltpu.SemaphoreType.DMA((1, n_w)),
        ],
        compiler_params=params(collective, 60),
    )(*(v.reshape(s) for v, s in zip(terms, plan.shaped, strict=True)), gain_terms, first_terms, layer_terms, resid)
    return plan.row_shards(sums[:count]), sums[-2], sums[-1]


def norm_back(g, m, feed_ref, resid_ref, gain_ref, cot_ref, land, proj_own, proj_in, d_resid, d_gain, ticks):
    for i in range(g.n_w):
        m.to_source(0, i, feed_ref.at[i], land.at[g.w])
    ticks(3)
    for j in range(g.n_w):
        m.arrived(0, j, land.at[j])
    d_h = land[0].astype(F32)
    for j in range(1, g.n_w):
        d_h += land[j].astype(F32)
    resid = resid_ref[...]
    scale = inv_rms(resid)
    normal = resid * scale
    d_gain[...] = jnp.broadcast_to(jnp.sum(d_h * normal, axis=0, keepdims=True), d_gain.shape)
    total = cot_ref[...].astype(F32) + rms_back(d_h * gain_ref[...], normal, scale)
    d_resid[...] = total
    proj_own[...] = total.astype(BF)
    for j in range(g.n_w):
        m.to_target(1, j, proj_own, proj_in.at[g.slot])
    ticks(3)
    for i in range(g.n_w):
        m.arrived(1, i, proj_in.at[i])


def norm_back_ends(m, feed_ref, proj_own):
    m.sent(0, lambda i: feed_ref.at[i], False)
    m.sent(1, lambda j: proj_own, True)


NORM_SEMAPHORES, BACK_SEMAPHORES = 2, 6
LOADED = (0, 1, 2, 5, 8, 9, 10, 11, 12, 15, 16, 17)


def norm_back_kernel(
    n_w, n_c, feed_ref, resid_ref, gain_ref, cot_ref, proj_all, d_resid, d_gain, land, proj_own, send, recv
):
    g = Group(n_w, n_c)
    m = Moves(g, send, recv)
    g.greet(False)
    norm_back(g, m, feed_ref, resid_ref, gain_ref, cot_ref, land, proj_own, proj_all, d_resid, d_gain, lambda n: None)
    norm_back_ends(m, feed_ref, proj_own)


def attend_back(
    g, m,
    bounds_ref, proj_ref, d_resid_ref, out_ref, queries_ref, kv_ref, cos_ref, sin_ref, up_ref, latent_ref,
    query_gain_ref, down_ref, key_ref, value_ref, x_in_ref, r_in_ref, gain_ref, x_ref,
    d_q_out, low_out, slope_out, d_query_gain, d_gain,
    d_kv, kv_parts, kv_land, kv_column, kv_z, q_parts, q_land,
    low_own, low_in, n_parts, n_land, z_send, z_recv, out_sem, work,
):
    tokens, seqlen, depth = x_ref.shape[0], kv_ref.shape[1], kv_ref.shape[2] // 2
    rank, half, cols = down_ref.shape[1], tokens // 2, x_in_ref.shape[2]
    n_w = g.n_w
    mirror = g.n_z - 1 - g.z
    scale = 1.0 / math.sqrt(depth)

    def kv_part(stream, core, part):
        return kv_parts.at[stream, part, :, 1 - core if part else core]

    work.before_attention()

    def one_stream(stream):
        d_kv[...] = jnp.zeros_like(d_kv)
        for core in range(2):
            i = 2 * stream + core
            visible = visible_keys(bounds_ref, g.core * g.per + stream, g.base + core, tokens, seqlen)
            slopes = dot_nt(proj_ref[i], out_ref[...]).astype(BF)
            d_keys = jnp.zeros((seqlen, depth), F32)
            d_values = jnp.zeros((seqlen, depth), F32)
            for cut in range(0, up_ref.shape[1], depth):
                span = slice(cut, cut + depth)
                q, slope = queries_ref[i, :, span], slopes[:, span]
                probs = probabilities(q, kv_ref[stream, :, :depth], visible)
                d_probs = dot_nt(slope, kv_ref[stream, :, depth:])
                delta = jnp.sum(probs * d_probs, axis=-1, keepdims=True)
                d_scores = (probs * (d_probs - delta)).astype(BF)
                d_q = dot(d_scores, kv_ref[stream, :, :depth])
                d_q_out[i, :, span] = (rotate(d_q, cos_ref[core], -sin_ref[core]) * scale).astype(BF)
                d_keys += dot_tn(d_scores, q)
                d_values += dot_tn(probs.astype(BF), slope)
            shaped = (2, g.n_z, 2, half, depth)
            d_kv[:, :, :, :, :depth] += d_keys.reshape(shaped)
            d_kv[:, :, :, :, depth:] += d_values.reshape(shaped)
            q_parts[i] = dot_nt(d_q_out[i], up_ref[...]).astype(BF)
            m.to_source(0, i, q_parts.at[i], q_land.at[g.w])
            work.ticks(3)
        kv_parts[stream] = d_kv[...].astype(BF)
        for core in range(2):
            for part in range(2):
                m.to_source(1 + part, 2 * stream + core, kv_part(stream, core, part), kv_land.at[g.w, part])

    if n_w <= 4:
        for stream in range(g.per):
            one_stream(stream)
    else:
        lax.fori_loop(0, g.per, lambda stream, carry: (one_stream(stream), carry)[1], 0)
    work.after_attention(d_q_out)
    for j in range(n_w):
        m.arrived(0, j, q_land.at[j])
    d_n = q_land[0].astype(F32)
    for j in range(1, n_w):
        d_n += q_land[j].astype(F32)
    latent = latent_ref[...]
    r_query = inv_rms(latent)
    n_query = latent * r_query
    d_query_gain[...] = jnp.broadcast_to(jnp.sum(d_n * n_query, axis=0, keepdims=True), d_query_gain.shape)
    low_own[:, :rank] = rms_back(d_n * query_gain_ref[...], n_query, r_query).astype(BF)
    lead = pl.ds(0, rank)
    for j in range(n_w):
        m.to_target(3, j, low_own.at[:, lead], low_in.at[g.slot, :, lead])
    work.ticks(2)

    for j in range(n_w):
        for part in range(2):
            m.arrived(1 + part, j, kv_land.at[j, part])
    total = kv_land[0].astype(F32)
    for j in range(1, n_w):
        total += kv_land[j].astype(F32)
    kv_column[...] = total.astype(BF)

    def over_z(part, step):
        z = lax.rem(g.z + step, g.n_z)
        return column_copy(
            g, part, step, kv_column.at[part, g.n_z - 1 - z if part else z], kv_z.at[step, part], z_send, z_recv
        )

    for step in range(1, g.n_z):
        for part in range(2):
            over_z(part, step).start()
    work.ticks(2)
    own = [kv_column[0, g.z].astype(F32), kv_column[1, mirror].astype(F32)]
    for step in range(1, g.n_z):
        for part in range(2):
            over_z(part, step).wait_recv()
            own[part] += kv_z[step, part].astype(F32)
    own = jnp.concatenate(own, axis=0)
    low_own[:, rank : rank + depth] = rotate(own[:, :depth], cos_ref[g.core], -sin_ref[g.core]).astype(BF)
    low_own[:, rank + depth :] = own[:, depth:].astype(BF)
    tail = pl.ds(rank, 2 * depth)
    for j in range(n_w):
        m.to_target(4, j, low_own.at[:, tail], low_in.at[g.slot, :, tail])

    d_first = jnp.zeros((1, cols), F32)
    for i in range(n_w):
        m.arrived(3, i, low_in.at[i, :, lead])
        d_h = dot_nt(low_in[i, :, :rank], down_ref[...])
        m.arrived(4, i, low_in.at[i, :, tail])
        d_h += dot_nt(low_in[i, :, rank : rank + depth], key_ref[...])
        d_h += dot_nt(low_in[i, :, rank + depth :], value_ref[...])
        normal = x_in_ref[i].astype(F32) * r_in_ref[i, :, :1]
        d_first += jnp.sum(d_h * normal, axis=0, keepdims=True)
        n_parts[i] = (d_h * gain_ref[...]).astype(BF)
        m.to_source(5, i, n_parts.at[i], n_land.at[g.w])
        work.ticks(1)
    d_gain[...] = jnp.broadcast_to(d_first, d_gain.shape)
    work.after_low(low_in, low_out, out_sem)
    for j in range(n_w):
        m.arrived(5, j, n_land.at[j])
    d_n = jnp.concatenate([n_land[j].astype(F32) for j in range(n_w)], axis=1)
    x = x_ref[...].astype(F32)
    r_first = inv_rms(x)
    slope_out[...] = (d_resid_ref[...] + rms_back(d_n, x * r_first, r_first)).astype(BF)

    work.at_end(low_in, low_out, out_sem)
    m.sent(0, lambda i: q_parts.at[i], False)
    m.sent(3, lambda j: low_own.at[:, lead], True)
    m.sent(4, lambda j: low_own.at[:, tail], True)
    m.sent(5, lambda i: n_parts.at[i], False)
    for part in range(2):
        m.sent(1 + part, lambda i: kv_part(i // 2, i % 2, part), False)
        for step in range(1, g.n_z):
            over_z(part, step).wait_send()


class Alone:
    def ticks(self, number):
        pass

    def before_attention(self):
        pass

    def after_attention(self, d_q):
        pass

    def after_low(self, low_in, low_out, sem):
        pltpu.make_async_copy(low_in, low_out, sem.at[0]).start()

    def at_end(self, low_in, low_out, sem):
        pltpu.make_async_copy(low_in, low_out, sem.at[0]).wait()


class Products:
    TILE = 512

    def __init__(self, chain, first, attn, proj, q_all, h_cols, stages, sems):
        self.chain, self.ticks, self.first = chain, chain.ticks, first
        self.attn, self.proj, self.q_all, self.h_cols = attn, proj, q_all, h_cols
        self.stages, self.sems = stages, sems

    def product(self, which, left, right, ticks):
        terms, stage = self.chain.terms[self.first + which], self.stages[which]
        cols, lead = terms.shape[-1], (slice(None),) * (len(terms.shape) - 1)
        tile = stage.shape[-1]
        rows = left.shape[0]

        def out(at):
            return pltpu.make_async_copy(stage, terms.at[(*lead, pl.ds(at, tile))], self.sems.at[which])

        for at in range(0, cols, tile):
            made = dot_tn(left[...], right[:, :, at : at + tile].reshape(rows, tile)).astype(BF)
            if at > 0:
                out(at - tile).wait()
            stage[...] = made.reshape(stage.shape)
            out(at).start()
            self.ticks(ticks)
        out(cols - tile).wait()
        self.chain.have(self.first + which + 1)

    def before_attention(self):
        self.product(0, self.attn, self.proj, 1)

    def after_attention(self, d_q):
        self.ticks(1)
        self.product(1, self.q_all, d_q, 1)

    def after_low(self, low_in, low_out, sem):
        self.product(2, self.h_cols, low_in, 1)

    def at_end(self, low_in, low_out, sem):
        pass


def attend_back_kernel(n_w, n_c, *refs):
    *refs, send, recv, z_send, z_recv, out_sem = refs
    g = Group(n_w, n_c)
    g.greet(True)
    attend_back(g, Moves(g, send, recv), *refs, z_send, z_recv, out_sem, Alone())


def late_kernel(n_w, n_c, plan, *refs):
    bounds_ref, feed_ref, resid_ref, gain_ref, cot_ref, *refs = refs
    rest, (layer_terms, attn, q_all, h_cols), given, refs = refs[:15], refs[15:19], refs[19:22], refs[22:]
    count = len(plan.arrays)
    sums, made, (d_q_out, slope_out, gains_out, layer_out), refs = (
        refs[:count], refs[count : count + 3], refs[count + 3 : count + 7], refs[count + 7 :]
    )
    chain_scratch, small_refs, refs = (
        refs[:CHAIN_SCRATCH], refs[CHAIN_SCRATCH : CHAIN_SCRATCH + SMALL_SCRATCH], refs[CHAIN_SCRATCH + SMALL_SCRATCH :]
    )
    land, proj_own, proj_in, d_resid, gain_terms, first_terms, norm_gain, query_gain, *refs = refs
    *stages, product_sems, small_send, small_recv, norm_send, norm_recv = refs[:8]
    back_scratch, (send, recv, z_send, z_recv, out_sem), buffers, loaded = refs[8:19], refs[19:24], refs[24:-1], refs[-1]
    wanted = [*rest, attn, q_all, h_cols]
    loads = Loads([wanted[i] for i in LOADED], buffers, loaded)
    for i, buffer in zip(LOADED, buffers, strict=True):
        wanted[i] = buffer
    *rest, attn, q_all, h_cols = wanted
    g = Group(n_w, n_c)
    norm_moves = Moves(g, norm_send, norm_recv)
    chain = Chain(plan, n_c, [*given, *made], sums, chain_scratch)
    chain.have(3)
    work = Products(chain, 3, attn, proj_in, q_all, h_cols, stages, product_sems)
    g.greet(True)
    norm_back(g, norm_moves, feed_ref, resid_ref, gain_ref, cot_ref, land, proj_own, proj_in, d_resid, norm_gain, chain.ticks)
    loads.wait(*range(len(LOADED)))
    attend_back(
        g, Moves(g, send, recv), bounds_ref, proj_in, d_resid, *rest, d_q_out, None, slope_out, query_gain, first_terms,
        *back_scratch, z_send, z_recv, out_sem, work,
    )
    width, rank = norm_gain.shape[1] // n_w, query_gain.shape[1] // n_w
    for j in range(n_w):
        gain_terms[j, :, :width] = norm_gain[:, j * width : (j + 1) * width]
        gain_terms[j, :, width:] = query_gain[:, j * rank : (j + 1) * rank]
    small = Small(
        g, n_c, Moves(g, small_send, small_recv), gain_terms, first_terms, layer_terms, resid_ref, gains_out, layer_out,
        land, small_refs,
    )
    small.begin()
    chain.ticks(4)
    small.middle()
    chain.finish()
    small.end()
    norm_back_ends(norm_moves, feed_ref, proj_own)


def bytes_of(shapes):
    return sum(math.prod(v.shape) * jnp.dtype(v.dtype).itemsize for v in shapes)


def late_part(n_w, n_c, shapes, turned, bounds, late, rest, out_part, given, attn, q_all, h_cols):
    feed, resid, gain, cot = late
    kv, up_cols, x = rest[2], rest[5], rest[14]
    (tokens, width), (rank, features) = x.shape, up_cols.shape
    per, seqlen, both = kv.shape
    n_z, half, cols, low = n_c // 2, tokens // 2, width // n_w, rank + both
    plan = Plan(shapes, turned, n_w, 8, 380_000)
    proj, d_q, slope = shape_of(n_w, tokens, width), shape_of(n_w, tokens, features), shape_of(tokens, width)
    d_resid, norm_gain = shape_of(tokens, width, dtype=F32), shape_of(8, width, dtype=F32)
    query_gain, first_gain = shape_of(8, rank, dtype=F32), shape_of(8, cols, dtype=F32)
    norm_scratch = [pltpu.VMEM((n_w, tokens, width), BF), pltpu.VMEM((tokens, width), BF)]
    norm_semaphores = [pltpu.SemaphoreType.DMA((NORM_SEMAPHORES, n_w))] * 2
    back_scratch = [
        pltpu.VMEM((2, n_z, 2, half, both), F32),
        pltpu.VMEM((per, 2, n_z, 2, half, both), BF),
        pltpu.VMEM((n_w, 2, n_z, half, both), BF),
        pltpu.VMEM((2, n_z, half, both), BF),
        pltpu.VMEM((n_z, 2, half, both), BF),
        pltpu.VMEM((n_w, tokens, rank), BF),
        pltpu.VMEM((n_w, tokens, rank), BF),
        pltpu.VMEM((tokens, low), BF),
        pltpu.VMEM((n_w, tokens, low), BF),
        pltpu.VMEM((n_w, tokens, cols), BF),
        pltpu.VMEM((n_w, tokens, cols), BF),
    ]
    back_semaphores = [
        pltpu.SemaphoreType.DMA((BACK_SEMAPHORES, n_w)),
        pltpu.SemaphoreType.DMA((BACK_SEMAPHORES, n_w)),
        pltpu.SemaphoreType.DMA((2, n_z)),
        pltpu.SemaphoreType.DMA((2, n_z)),
        pltpu.SemaphoreType.DMA((1,)),
    ]
    stages = [pltpu.VMEM((*v[:-1], math.gcd(v[-1], Products.TILE)), BF) for v in plan.shaped[3:]]
    gains = cols + rank // n_w
    merged_scratch = [
        *plan.scratch(),
        *small_scratch(n_w, n_c, gains, cols),
        *norm_scratch,
        *(pltpu.VMEM(v.shape, v.dtype) for v in (proj, d_resid)),
        pltpu.VMEM((n_w, 8, gains), F32),
        *(pltpu.VMEM(v.shape, v.dtype) for v in (first_gain, norm_gain, query_gain)),
        *stages,
        pltpu.SemaphoreType.DMA((3,)),
        *[pltpu.SemaphoreType.DMA((1, n_w))] * 2,
        *norm_semaphores,
        *back_scratch,
        *back_semaphores,
    ]
    wanted = [*rest, attn, q_all, h_cols]
    specs = [ANY if i in LOADED else VMEM for i in range(len(wanted))]
    buffers = [v for v in merged_scratch if v.dtype in (BF, F32)]
    if bytes_of([*buffers, *rest, *late[1:], attn, q_all, h_cols, d_q, slope, slope]) < 60 * MIB:
        count = len(plan.arrays)
        done = pl.pallas_call(
            functools.partial(late_kernel, n_w, n_c, plan),
            out_shape=[
                *plan.out_shapes(), *(shape_of(*v) for v in plan.shaped[3:]), d_q, slope,
                shape_of(8, gains + cols, dtype=F32), slope,
            ],
            in_specs=[SMEM, ANY, VMEM, VMEM, VMEM, *specs[:-3], ANY, *specs[-3:]] + [ANY] * 3,
            out_specs=[ANY] * (count + 3) + [VMEM] * 4,
            scratch_shapes=[
                *merged_scratch, *vmem_like(wanted[i] for i in LOADED), pltpu.SemaphoreType.DMA((len(LOADED),))
            ],
            compiler_params=params(3, 62),
        )(
            bounds, feed, resid, gain, cot, *rest, out_part, attn, q_all, h_cols,
            *(v.reshape(s) for v, s in zip(given, plan.shaped, strict=False)),
        )
        return plan.row_shards(done[:count]), done[-2], done[-1], done[-3]
    d_proj, d_resid, d_norm_gain = pl.pallas_call(
        functools.partial(norm_back_kernel, n_w, n_c),
        out_shape=[proj, d_resid, norm_gain],
        in_specs=[ANY, VMEM, VMEM, VMEM],
        out_specs=[ANY, VMEM, VMEM],
        scratch_shapes=[*norm_scratch, *norm_semaphores],
        compiler_params=params(5, 40),
    )(feed, resid, gain, cot)
    d_q_raw, d_low, d_x, d_query_gain, d_first_gain = pl.pallas_call(
        functools.partial(attend_back_kernel, n_w, n_c),
        out_shape=[d_q, shape_of(n_w, tokens, low), slope, query_gain, first_gain],
        in_specs=[SMEM] + [VMEM] * (2 + len(rest)),
        out_specs=[VMEM, ANY] + [VMEM] * 3,
        scratch_shapes=[*back_scratch, *back_semaphores],
        compiler_params=params(6, 60),
    )(bounds, d_proj, d_resid, *rest)
    pairs = ((attn, d_proj), (q_all, d_q_raw), (h_cols, d_low))
    terms = [*given, *(dot_tn(a, b.reshape(n_w * tokens, -1)).astype(BF) for a, b in pairs)]
    spread = [v.reshape(8, n_w, -1).swapaxes(0, 1) for v in (d_norm_gain, d_query_gain)]
    sums, gains, layer_output = sum_over_ctx(
        plan, terms, n_c, 4, jnp.concatenate(spread, axis=2), d_first_gain, out_part, resid
    )
    return sums, gains, layer_output, d_x


def tables(positions, width):
    exponent = jnp.arange(width // 2, dtype=F32) * (-2.0 / width)
    angles = positions.astype(F32)[..., None] * (10000.0**exponent)
    return jnp.cos(angles), jnp.sin(angles)


def whole_columns(part, rows):
    whole = lax.all_gather(part, "ctx", axis=1)
    return whole.reshape(rows, part.shape[-1])


def on_device(
    inputs,
    boundaries,
    first_gain,
    query_down,
    query_gain,
    query_up,
    key_weights,
    value_weights,
    output_weights,
    second_gain,
    gate_weights,
    up_weights,
    down_weights,
    cotangent,
):
    n_w, n_c, c = lax.axis_size("wt"), lax.axis_size("ctx"), lax.axis_index("ctx")
    width, half = inputs.shape[-1], inputs.shape[2]
    tokens, seqlen = 2 * half, 2 * half * n_c
    depth, rank = key_weights.shape[1], query_down.shape[1]
    hidden_cols = down_weights.shape[0]

    def for_columns(weight):
        rows = weight.shape[0] // n_c
        part = lax.dynamic_slice_in_dim(weight, c * rows, rows, 0)
        return part.reshape(rows, n_w, -1).swapaxes(0, 1)

    wide_bounds = jnp.zeros((8, 128), jnp.int32).at[0, : boundaries.shape[1]].set(boundaries[0])
    gains = jnp.concatenate([query_gain, second_gain]).astype(F32)
    gains = jnp.broadcast_to(gains[None], (8, gains.shape[0]))
    bounds, gains, up_part, gate_part, upper_part = exchange(
        [wide_bounds, gains, for_columns(query_up), for_columns(gate_weights), for_columns(up_weights)],
        (False, False, True, True, True), n_w, 0,
    )
    bounds = bounds[:, 0, : boundaries.shape[1]]
    gain_query = gains[:, 0, : rank // n_w].reshape(1, rank)
    gain_two = gains[:, 0, rank // n_w :].reshape(1, width)
    gain_one = first_gain.astype(F32)[None]
    up_cols = whole_columns(up_part, rank)
    gate_cols = whole_columns(gate_part, width)
    upper_cols = whole_columns(upper_part, width)

    ctx = jnp.stack([c - c % 2, c - c % 2 + 1])[:, None]
    offsets = jnp.arange(half, dtype=jnp.int32)[None]
    positions = jnp.concatenate([ctx * half + offsets, seqlen - (ctx + 1) * half + offsets], axis=1)
    cosine, sine = tables(positions, depth)
    x = inputs.reshape(tokens, width)
    cot = cotangent.reshape(tokens, width)
    h_cols, x_in, r_in, latent, q_all, kv, cot_all = first_part(
        n_w, n_c, x, cot, gain_one, gain_query, query_down, key_weights, value_weights,
        lax.dynamic_index_in_dim(cosine, c % 2, keepdims=False), lax.dynamic_index_in_dim(sine, c % 2, keepdims=False),
    )
    kv = kv.reshape(n_w // 2, seqlen, 2 * depth)
    queries, attn, resid, h_all = attend_part(
        n_w, n_c, bounds, q_all, up_cols, kv, cosine, sine, output_weights, x, gain_two
    )

    h_second = h_all.reshape(n_w * tokens, width)
    slope = cot_all.reshape(n_w * tokens, width)
    gate = dot(h_second, gate_cols)
    upper = dot(h_second, upper_cols)
    sigma = jax.nn.sigmoid(gate)
    silu = gate * sigma
    hidden = (silu * upper).astype(BF)
    d_hidden = dot_nt(slope, down_weights)
    d_gate = (d_hidden * upper * sigma * (1.0 + gate * (1.0 - sigma))).astype(BF)
    d_upper = (d_hidden * silu).astype(BF)
    out_part = dot(hidden, down_weights).astype(BF)
    d_down = dot_tn(hidden, slope).astype(BF)
    d_gate_weights = dot_tn(h_second, d_gate).astype(BF)
    d_up_weights = dot_tn(h_second, d_upper).astype(BF)
    feed = (dot_nt(d_gate, gate_cols) + dot_nt(d_upper, upper_cols)).astype(BF)

    def grouped(v):
        return v.reshape(n_w, tokens, v.shape[-1])

    def flat(v):
        return v.reshape(n_w * tokens, v.shape[-1])

    rest = (
        output_weights, queries, kv, cosine, sine, up_cols, latent, gain_query, query_down, key_weights, value_weights,
        x_in, r_in, gain_one, x,
    )
    given = (d_down, d_gate_weights, d_up_weights)
    shapes = [v.shape for v in given]
    shapes += [output_weights.shape, up_cols.shape, (query_down.shape[0], rank + 2 * depth)]
    sums, gains, layer_output, input_gradient = late_part(
        n_w, n_c, shapes, (False, True, True, False, True, False), bounds, (grouped(feed), resid, gain_two, cot), rest,
        grouped(out_part), given, flat(attn), flat(q_all), flat(h_cols),
    )
    *sums, firsts = sums
    d_down, d_gate_weights, d_up_weights, d_output, d_query_up = (s.astype(F32) for s in sums)
    one, two = width // n_w, 2 * (width // n_w)
    return (
        layer_output.reshape(inputs.shape),
        input_gradient.reshape(inputs.shape),
        gains[0, :one],
        firsts[:, :rank].astype(F32),
        gains[0, two:],
        d_query_up,
        firsts[:, rank : rank + depth].astype(F32),
        firsts[:, rank + depth :].astype(F32),
        d_output,
        gains[0, one:two],
        d_gate_weights,
        d_up_weights,
        d_down,
    )


def solution(mesh):
    token = P("wt", None, "ctx", None)
    row, vec = P("wt", None), P("wt")
    in_specs = (token, row, vec, row, vec, row, row, row, row, vec, row, row, row, token)
    out_specs = (token, token, vec, row, vec, row, row, row, row, vec, row, row, row)
    return jax.shard_map(
        on_device, mesh=mesh, in_specs=in_specs, out_specs=out_specs, check_vma=False
    )
```
